32 devices in a mesh: rep: 4 (over z), lat: 8 (over y, x, core).
Axes of the slice: x: 2, y: 2, z: 4, core: 2. Of those that a mesh axis runs over, the one named last changes fastest.
Arguments:
- residual: bfloat16 [4096, 768], P(('rep', 'lat')), may hold values from -6 to 6
- valid_mask: int32 [4096], P(('rep', 'lat')), may hold values from 0 to 1
- top_idx: int32 [4096, 32], P(('rep', 'lat')), may hold values from 0 to 32767, as said below
- aux_idx: int32 [4096, 512], P(('rep', 'lat')), may hold values from 0 to 32767, as said below
- dead_flags: int32 [32768], replicated, may hold values 0 or 1
- norm_params: float32 [6, 768], replicated
- biases: float32 [6912], replicated, may hold values from -1 to 1
- w_qkv: bfloat16 [768, 2304], P('lat'), may hold values from -0.21875 to 0.21875
- w_out: bfloat16 [768, 768], P('lat'), may hold values from -0.21875 to 0.21875
- w_fc: bfloat16 [768, 3072], P('lat'), may hold values from -0.21875 to 0.21875
- w_proj: bfloat16 [3072, 768], P('lat'), may hold values from -0.109375 to 0.109375
- head_table: bfloat16 [53248, 768], P('lat')
- w_enc: float32 [768, 32768], P(None, 'lat'), may hold values from -0.21875 to 0.21875
- encoder_bias_vec: float32 [32768], P('lat'), may hold values from -3 to 3
- w_dec: float32 [32768, 768], P('lat'), may hold values from -0.21875 to 0.21875
- decoder_bias_vec: float32 [768], replicated, may hold values from -3 to 3
- mom_enc: float32 [768, 32768], P(None, 'lat'), may hold values from -0.0005126953 to 0.0005126953
- mom_benc: float32 [32768], P('lat'), may hold values from -0.00029296876 to 0.00029296876
- mom_dec: float32 [32768, 768], P('lat'), may hold values from -0.0004394531 to 0.0004394531
- mom_bdec: float32 [768], replicated, may hold values from -0.001875 to 0.001875
- q_enc: float32 [32768, 8], P('lat'), may hold values from -5 to 5
- q_dec: float32 [32768, 8], P('lat'), may hold values from -5 to 5
- err_enc: float32 [4, 768, 32768], P('rep', None, 'lat'), may hold values from -0.0043945312 to 0.0043945312
- err_dec: float32 [4, 32768, 768], P('rep', 'lat'), may hold values from -0.0043945312 to 0.0043945312
Outputs:
- loss_sum: float32 [], replicated
- valid_total: float32 [], replicated
- w_enc_new: float32 [768, 32768], P(None, 'lat')
- b_enc_new: float32 [32768], P('lat')
- w_dec_new: float32 [32768, 768], P('lat')
- b_dec_new: float32 [768], replicated
- mom_enc_new: float32 [768, 32768], P(None, 'lat')
- mom_benc_new: float32 [32768], P('lat')
- mom_dec_new: float32 [32768, 768], P('lat')
- mom_bdec_new: float32 [768], replicated
- q_enc_new: float32 [32768, 8], P('lat')
- q_dec_new: float32 [32768, 8], P('lat')
- err_enc_new: float32 [4, 768, 32768], P('rep', None, 'lat')
- err_dec_new: float32 [4, 32768, 768], P('rep', 'lat')
The draws below stay inside these ranges and needn't reach their ends.
Inputs may be any that keep to these rules, and one draw needn't show every extreme that they name: `top_idx`: each row names 32 different latents. `aux_idx`: each row names 512 different latents.
All inputs are finite; a program needn't handle non-finite values.
Results may differ from the reference program's by a relative error of at most 0.01.
Values may be sent and summed in bfloat16 or wider, within the bound.
No kernel may reach another device: no remote copies, remote signals or barrier semaphores. Data moves between devices by JAX's collectives and lax.ppermute only.
A program may use at most 512 MiB of HBM per device.

```python
import math
import jax
import jax.numpy as jnp
from jax import lax

D = 768
FF = 3072
HEADS = 12
L = 32768
V = 53248
K = 32
KA = 512
RANK = 8
TOK_DEV = 128
GROUP = 1024
REPLICAS = 4
TOKENS = 4096


def draw_valid_mask(key, part):
    key = jax.random.fold_in(key, 1)
    row_ids = jnp.arange(TOKENS)
    lat_count = GROUP // TOK_DEV
    rep_count = TOKENS // GROUP
    lat_pos = row_ids % GROUP // TOK_DEV
    rep_pos = row_ids // GROUP
    numer = (lat_count - 1 + 2 * lat_pos) * (rep_count - 1 + 2 * rep_pos)
    denom = 9 * (lat_count - 1) * (rep_count - 1)
    drawn = jax.random.randint(key, (TOKENS,), 0, denom)
    return (drawn < numer).astype(jnp.int32)


def distinct_picks(key, count):
    drawn = jax.random.randint(key, (TOKENS, count), 0, L - count + 1)
    return (jnp.sort(drawn, axis=1) + jnp.arange(count)[None, :]).astype(jnp.int32)


def draw_top_idx(key, part):
    key = jax.random.fold_in(key, 2)
    return distinct_picks(key, K)


def draw_aux_idx(key, part):
    key = jax.random.fold_in(key, 3)
    return distinct_picks(key, KA)


def draw_head_table(key, part):
    key = jax.random.fold_in(key, 4)
    row_pos = jnp.arange(V).astype(jnp.float32) / (V - 1)
    values = jax.random.normal(key, (V, D), jnp.float32)
    scale_row = 1.0 + 2.0 * row_pos
    return (values * scale_row[:, None] / jnp.sqrt(jnp.float32(D))).astype(jnp.bfloat16)


def draw_norm_params(key, part):
    key = jax.random.fold_in(key, 5)
    gain_key, shift_key = jax.random.split(key)
    gains = jax.random.uniform(gain_key, (6, D), jnp.float32, 0.7, 1.3)
    shifts = 0.2 * jax.random.normal(shift_key, (6, D), jnp.float32)
    even_rows = (jnp.arange(6) % 2 == 0)[:, None]
    return jnp.where(even_rows, gains, shifts)


def touch_ends(values, own_key, least, high):
    shape = values.shape
    index_at = [jax.random.randint(jax.random.fold_in(own_key, axis), (), 0, shape[axis]) for axis in range(len(shape))]
    values = values.at[tuple(index_at)].set(least)
    longest = shape.index(max(shape))
    index_at[longest] = (index_at[longest] + 1) % shape[longest]
    return values.at[tuple(index_at)].set(high)


def block_levels(rng, dims, pieces, least, largest):
    def one(position, blocks):
        draws = jax.random.uniform(jax.random.fold_in(jax.random.fold_in(rng, 6), position), (blocks,), jnp.float32, least / len(pieces), largest / len(pieces))
        return jnp.repeat(jnp.exp(draws), dims[position] // blocks).reshape((-1,) + (1,) * (len(dims) - position - 1))

    loudness = one(*pieces[0])
    for cut in pieces[1:]:
        loudness = loudness * one(*cut)
    return loudness


def normal_values(stream_key, extent, deviation, most, shards=(), held_as=jnp.bfloat16):
    values = deviation * jax.random.normal(stream_key, extent, jnp.float32)
    if shards:
        values = values * block_levels(stream_key, extent, shards, -0.22, 0.18)
    return jnp.clip(values, -most, most).astype(held_as)


def setup_inputs(seed: int = 0) -> dict:
    keys = jax.random.split(jax.random.key(seed), 25)
    return {
        "residual": normal_values(keys[0], (TOKENS, D), 1.0, 6.0, ((0, 32),)),
        "valid_mask": draw_valid_mask(jax.random.fold_in(keys[24], 71), 0),
        "top_idx": draw_top_idx(jax.random.fold_in(keys[24], 71), 0),
        "aux_idx": draw_aux_idx(jax.random.fold_in(keys[24], 71), 0),
        "dead_flags": touch_ends((jax.random.randint(keys[4], (L,), 0, 3) < 1).astype(jnp.int32), jax.random.fold_in(keys[4], 1), 0, 1),
        "norm_params": draw_norm_params(jax.random.fold_in(keys[24], 71), 0),
        "biases": normal_values(keys[6], (5 * D + FF,), 0.2, 1.0, (), jnp.float32),
        "w_qkv": normal_values(keys[7], (D, 3 * D), D ** -0.5, 0.21875, ((0, 8),)),
        "w_out": normal_values(keys[8], (D, D), D ** -0.5, 0.21875, ((0, 8),)),
        "w_fc": normal_values(keys[9], (D, FF), D ** -0.5, 0.21875, ((0, 8),)),
        "w_proj": normal_values(keys[10], (FF, D), FF ** -0.5, 0.109375, ((0, 8),)),
        "head_table": draw_head_table(jax.random.fold_in(keys[24], 71), 0),
        "w_enc": normal_values(keys[12], (D, L), D ** -0.5, 0.21875, ((1, 8),), jnp.float32),
        "encoder_bias_vec": normal_values(keys[13], (L,), 0.5, 3.0, ((0, 8),), jnp.float32),
        "w_dec": normal_values(keys[14], (L, D), D ** -0.5, 0.21875, ((0, 8),), jnp.float32),
        "decoder_bias_vec": normal_values(keys[15], (D,), 0.5, 3.0, (), jnp.float32),
        "mom_enc": normal_values(keys[16], (D, L), (0.35 / TOKENS), 0.0005126953, ((1, 8),), jnp.float32),
        "mom_benc": normal_values(keys[17], (L,), (0.2 / TOKENS), 0.00029296876, ((0, 8),), jnp.float32),
        "mom_dec": normal_values(keys[18], (L, D), (0.3 / TOKENS), 0.0004394531, ((0, 8),), jnp.float32),
        "mom_bdec": normal_values(keys[19], (D,), (0.02 / TOKENS ** 0.5), 0.001875, (), jnp.float32),
        "q_enc": normal_values(keys[20], (L, RANK), 1.0, 5.0, ((0, 8),), jnp.float32),
        "q_dec": normal_values(keys[21], (L, RANK), 1.0, 5.0, ((0, 8),), jnp.float32),
        "err_enc": normal_values(keys[22], (REPLICAS, D, L), (3.0 / TOKENS), 0.0043945312, ((0, 4), (2, 8)), jnp.float32),
        "err_dec": normal_values(keys[23], (REPLICAS, L, D), (3.0 / TOKENS), 0.0043945312, ((0, 4), (1, 8)), jnp.float32),
    }


@jax.custom_vjp
def low(v):
    return lax.optimization_barrier(v.astype(jnp.bfloat16)).astype(jnp.float32)

@jax.custom_vjp
def low_back(v):
    return v

def low_keep(v):
    return (low(v), None)

def low_pass(kept, grad):
    return (grad,)

def back_keep(v):
    return (v, None)

def back_low(kept, grad):
    return (low(grad),)
low.defvjp(low_keep, low_pass)
low_back.defvjp(back_keep, back_low)
largest_values = lax.Precision.HIGHEST
aux_weight = 1.0 / 32.0
momentum_decay = 0.9
rate_enc = 3000.0
rate_dec = 3000.0
rate_benc = 10000.0
rate_bdec = 500.0

def layer_norm(values, gain_row, shift_row):
    center = values - lax.optimization_barrier(jnp.mean(values, axis=-1, keepdims=True))
    spread = lax.optimization_barrier(jnp.mean(center * center, axis=-1, keepdims=True))
    return center * lax.rsqrt(spread + 1e-05) * gain_row + shift_row

def frozen_block(residual, norm_params, biases, w_qkv, w_out, w_fc, w_proj):
    model_width = residual.shape[1]
    hidden_units = w_fc.shape[1]
    head_dim = model_width // HEADS
    stream = residual.astype(jnp.float32)
    normed = low(layer_norm(stream, norm_params[0], norm_params[1]))
    joined = jnp.dot(normed, w_qkv.astype(jnp.float32), precision=largest_values) + biases[:3 * model_width]
    joined = low(joined).reshape(-1, TOK_DEV, 3, HEADS, head_dim)
    scores = jnp.einsum('nqhd,nkhd->nhqk', joined[:, :, 0], joined[:, :, 1], precision=largest_values) / math.sqrt(head_dim)
    causal = jnp.arange(TOK_DEV)[:, None] >= jnp.arange(TOK_DEV)[None, :]
    scores = jnp.where(causal, scores, -1e+30)
    weights = low(jax.nn.softmax(scores, axis=-1))
    attended = jnp.einsum('nhqk,nkhd->nqhd', weights, joined[:, :, 2], precision=largest_values)
    attended = low(attended).reshape(-1, model_width)
    stream = stream + jnp.dot(attended, w_out.astype(jnp.float32), precision=largest_values) + biases[3 * model_width:4 * model_width]
    normed = low(layer_norm(stream, norm_params[2], norm_params[3]))
    inner_in = jnp.dot(normed, w_fc.astype(jnp.float32), precision=largest_values) + biases[4 * model_width:4 * model_width + hidden_units]
    activated = low(jax.nn.gelu(inner_in, approximate=True))
    return stream + jnp.dot(activated, w_proj.astype(jnp.float32), precision=largest_values) + biases[4 * model_width + hidden_units:]

def token_block(params, block_in, frozen):
    w_enc, encoder_bias_vec, w_dec, decoder_bias_vec = params
    stream, weight_row, topk_row_block, auxiliary_row_block = block_in
    norm_params, table_full, dead_full = frozen
    mean_removed = low(stream - decoder_bias_vec)
    encoder_columns = low(w_enc).T
    decoder_row_block = low(w_dec)
    topk_preact = low_back(jnp.einsum('hx,hpx->hp', mean_removed, encoder_columns[topk_row_block], precision=largest_values) + encoder_bias_vec[topk_row_block])
    auxiliary_preact = low_back(jnp.einsum('hx,hpx->hp', mean_removed, encoder_columns[auxiliary_row_block], precision=largest_values) + encoder_bias_vec[auxiliary_row_block])
    topk_code = low(topk_preact)
    auxiliary_code = low(auxiliary_preact * dead_full[auxiliary_row_block])
    rebuilt_input = low_back(jnp.einsum('fo,foh->fh', topk_code, decoder_row_block[topk_row_block], precision=largest_values) + decoder_bias_vec)
    auxiliary_rebuilt = low_back(jnp.einsum('fo,foh->fh', auxiliary_code, decoder_row_block[auxiliary_row_block], precision=largest_values))
    orig_normed = low(layer_norm(stream, norm_params[4], norm_params[5]))
    rec_normed = low(layer_norm(rebuilt_input, norm_params[4], norm_params[5]))
    logits_orig = jnp.dot(orig_normed, table_full.T, precision=largest_values)
    logits_rec = low_back(jnp.dot(rec_normed, table_full.T, precision=largest_values))
    lse_orig = jax.nn.logsumexp(logits_orig, axis=1)
    lse_rec = jax.nn.logsumexp(logits_rec, axis=1)
    probability = jnp.exp(logits_orig - lse_orig[:, None])
    kl_token = lax.optimization_barrier(jnp.sum(probability * (logits_orig - logits_rec), axis=1)) - lse_orig + lse_rec
    resid_err = stream - rebuilt_input - auxiliary_rebuilt
    per_token = kl_token + aux_weight * lax.optimization_barrier(jnp.sum(resid_err * resid_err, axis=1))
    return jnp.sum(weight_row * per_token)

def replica_grads(params, frozen, rep_in, valid_total, block_rows):
    stretched = jax.tree.map(lambda tensor: tensor.reshape((-1, block_rows) + tensor.shape[1:]), rep_in)

    def total_loss(params_in):

        def one_block(piece_rows):
            return token_block(params_in, piece_rows, frozen)
        return jnp.sum(lax.map(jax.checkpoint(one_block), stretched))
    loss_value, pull_back = jax.vjp(total_loss, params)
    grad_list, = pull_back(1.0 / valid_total)
    return (loss_value, grad_list)

def orthonormal(left_factor):
    gram_matrix = jnp.dot(left_factor.T, left_factor, precision=largest_values)
    cholesky_low = jnp.linalg.cholesky(gram_matrix)
    return lax.linalg.triangular_solve(cholesky_low, left_factor, left_side=False, lower=True, transpose_a=True)

def reference(residual, valid_mask, top_idx, aux_idx, dead_flags, norm_params, biases, w_qkv, w_out, w_fc, w_proj, head_table, w_enc, encoder_bias_vec, w_dec, decoder_bias_vec, mom_enc, mom_benc, mom_dec, mom_bdec, q_enc, q_dec, err_enc, err_dec):
    valid_float = valid_mask.astype(jnp.float32)
    valid_total = jnp.sum(valid_float)
    stream = frozen_block(residual, norm_params, biases, w_qkv, w_out, w_fc, w_proj)
    params = (w_enc, encoder_bias_vec, w_dec, decoder_bias_vec)
    frozen = (norm_params, head_table.astype(jnp.float32), dead_flags.astype(jnp.float32))
    block_rows = math.gcd(GROUP, 64)
    loss_parts, enc_parts, benc_parts, dec_parts, bdec_parts = ([], [], [], [], [])
    for replica in range(REPLICAS):
        row_span = slice(replica * GROUP, (replica + 1) * GROUP)
        rep_in = (stream[row_span], valid_float[row_span], top_idx[row_span], aux_idx[row_span])
        loss_value, grad_list = replica_grads(params, frozen, rep_in, valid_total, block_rows)
        loss_parts.append(loss_value)
        enc_parts.append(grad_list[0])
        benc_parts.append(grad_list[1])
        dec_parts.append(grad_list[2])
        bdec_parts.append(grad_list[3])
    loss_sum = jnp.sum(jnp.stack(loss_parts))
    grad_benc = lax.optimization_barrier(jnp.sum(jnp.stack(benc_parts), axis=0))
    grad_bdec = lax.optimization_barrier(jnp.sum(jnp.stack(bdec_parts), axis=0))
    full_enc = jnp.stack(enc_parts) + err_enc
    full_dec = jnp.stack(dec_parts) + err_dec
    ortho_enc = orthonormal(jnp.einsum('rdl,lk->dk', full_enc, q_enc, precision=largest_values))
    right_enc = jnp.einsum('rdl,dk->lk', full_enc, ortho_enc, precision=largest_values)
    approx_enc = jnp.dot(ortho_enc, right_enc.T, precision=largest_values)
    ortho_dec = orthonormal(jnp.einsum('rld,lk->dk', full_dec, q_dec, precision=largest_values))
    right_dec = jnp.einsum('rld,dk->lk', full_dec, ortho_dec, precision=largest_values)
    approx_dec = jnp.dot(right_dec, ortho_dec.T, precision=largest_values)
    err_enc_new = full_enc - approx_enc / REPLICAS
    err_dec_new = full_dec - approx_dec / REPLICAS
    mom_enc_new = momentum_decay * mom_enc + approx_enc
    mom_benc_new = momentum_decay * mom_benc + grad_benc
    mom_dec_new = momentum_decay * mom_dec + approx_dec
    mom_bdec_new = momentum_decay * mom_bdec + grad_bdec
    w_enc_new = w_enc - rate_enc * mom_enc_new
    b_enc_new = encoder_bias_vec - rate_benc * mom_benc_new
    b_dec_new = decoder_bias_vec - rate_bdec * mom_bdec_new
    dec_step = w_dec - rate_dec * mom_dec_new
    w_dec_new = dec_step * lax.rsqrt(lax.optimization_barrier(jnp.sum(dec_step * dec_step, axis=1, keepdims=True)) + 1e-06)
    return (loss_sum, valid_total, w_enc_new, b_enc_new, w_dec_new, b_dec_new, mom_enc_new, mom_benc_new, mom_dec_new, mom_bdec_new, right_enc, right_dec, err_enc_new, err_dec_new)
```

```python
import functools
import math

import jax
import jax.numpy as jnp
from jax import lax
from jax.experimental import pallas as pl
from jax.experimental.pallas import tpu as pltpu
from jax.sharding import PartitionSpec as P

HEADS = 12

pack_base = 32768
aux_weight = 1.0 / 32.0
momentum_decay = 0.9
rate_enc = 3000.0
rate_dec = 3000.0
rate_benc = 10000.0
rate_bdec = 500.0
lanes = 128
vmem_most = 60 * 2**20
largest_values = lax.Precision.HIGHEST
contract_cols = (((1,), (1,)), ((), ()))
contract_rows = (((0,), (0,)), ((), ()))
contract_plain = (((1,), (0,)), ((), ()))
f32 = jnp.float32
bf16 = jnp.bfloat16


def swap(values, axis, bit):
    count = lax.axis_size(axis)
    return lax.ppermute(values, axis, [(i, i ^ bit) for i in range(count)])


def bits_of(axis):
    count = lax.axis_size(axis)
    return [1 << k for k in range(count.bit_length() - 1)]


def gather_blocks(own):
    count = lax.axis_size("lat")
    if count == 8:
        half = own.shape[0] // 2
        blocks = {0: own, 2: swap(own, "lat", 2), 4: swap(own, "lat", 4)}
        blocks[1] = swap(own, "lat", 1)
        diag = [swap(blocks[4][:half], "lat", 2), swap(blocks[2][half:], "lat", 4)]
        blocks[3] = swap(blocks[2], "lat", 1)
        blocks[5] = swap(blocks[4], "lat", 1)
        blocks[6] = jnp.concatenate(diag, axis=0)
        blocks[7] = swap(blocks[6], "lat", 1)
    else:
        blocks = {0: own}
        for bit in bits_of("lat")[1:] + [1]:
            order = sorted(blocks)
            moved = swap(jnp.stack([blocks[j] for j in order]), "lat", bit)
            for at, j in enumerate(order):
                blocks[j ^ bit] = moved[at]
    return [blocks[j] for j in range(count)]


def gather_tokens(own):
    return jnp.concatenate(gather_blocks(own), axis=0)


def scatter_paths():
    others = bits_of("lat")[1:]
    if len(others) == 2:
        return [(0, 2, others), (1, 2, others[::-1])]
    return [(0, 1, others)]


def scatter_sum(partial):
    count = lax.axis_size("lat")
    rows, cols = partial.shape[0] // count, partial.shape[1]
    partial = partial.reshape(count, rows, cols)
    moved = swap(partial[1::2], "lat", 1)
    chip = partial[0::2] + moved
    done = []
    for part, parts, order in scatter_paths():
        width = cols // parts
        held = {2 * k: chip[k][:, part * width : (part + 1) * width] for k in range(count // 2)}
        for bit in order:
            sent = [j for j in sorted(held) if j & bit]
            got = swap(jnp.stack([held[j] for j in sent]).astype(bf16), "lat", bit)
            for at, j in enumerate(sent):
                held[j ^ bit] = held[j ^ bit] + got[at].astype(f32)
                del held[j]
        done.append(held[0])
    return jnp.concatenate(done, axis=1)


def merge(mean_a, lse_a, mean_b, lse_b):
    top = jnp.maximum(lse_a, lse_b)
    exp_a, exp_b = jnp.exp(lse_a - top), jnp.exp(lse_b - top)
    total = exp_a + exp_b
    mixed = mean_a.astype(f32) * (exp_a / total) + mean_b.astype(f32) * (exp_b / total)
    return mixed, top + jnp.log(total)


def scatter_mean(means, lses):
    count = lax.axis_size("lat")
    rows, cols = means.shape[0] // count, means.shape[1]
    means = means.reshape(count, rows, cols)
    lses = lses.reshape(count, rows, 1)
    chip, chip_lse = merge(
        means[0::2], lses[0::2], swap(means[1::2], "lat", 1), swap(lses[1::2], "lat", 1)
    )
    done = []
    for part, parts, order in scatter_paths():
        width = cols // parts
        held = {
            2 * k: (chip[k][:, part * width : (part + 1) * width], chip_lse[k])
            for k in range(count // 2)
        }
        for bit in order:
            sent = [j for j in sorted(held) if j & bit]
            got = swap(jnp.stack([held[j][0] for j in sent]).astype(bf16), "lat", bit)
            got_lse = swap(jnp.stack([held[j][1] for j in sent]), "lat", bit)
            for at, j in enumerate(sent):
                held[j ^ bit] = merge(*held[j ^ bit], got[at], got_lse[at])
                del held[j]
        done.append(held[0])
    return jnp.concatenate([mean for mean, _ in done], axis=1), done[0][1]


def sum_over(values, axes, sent_as=None):
    for axis in axes:
        for bit in bits_of(axis):
            if sent_as is not None:
                values = values.astype(sent_as)
            values = values.astype(f32) + swap(values, axis, bit).astype(f32)
    return values


def mask_kernel(tokens, hi_count, aux_count, ids_ref, dead_ref, out_ref, scratch):
    width = ids_ref.shape[1]
    hi_rows = lax.broadcasted_iota(jnp.int32, (hi_count, width), 0)
    lo_rows = lax.broadcasted_iota(jnp.int32, (lanes, width), 0)
    is_aux = lax.broadcasted_iota(jnp.int32, (hi_count, width), 1) < aux_count
    weight = jnp.where(is_aux, 2.0, 1.0)

    def one_token(t, carry):
        row = ids_ref[pl.ds(t, 1), :]
        hi_hot = jnp.where(hi_rows == (row >> 7), weight, 0.0).astype(bf16)
        lo_hot = jnp.where(lo_rows == (row & 127), 1.0, 0.0).astype(bf16)
        picked = lax.dot_general(hi_hot, lo_hot, contract_cols, preferred_element_type=f32)
        scratch[pl.ds(pl.multiple_of(t * hi_count, hi_count), hi_count), :] = picked
        return carry

    lax.fori_loop(0, tokens, one_token, 0, unroll=16)
    for hi in range(hi_count):
        code = scratch[pl.ds(hi, tokens, stride=hi_count), :]
        at = slice(hi * lanes, (hi + 1) * lanes)
        aux = jnp.where(code >= 2.0, 2.0, 0.0)
        out_ref[:, at] = (code - aux + aux * dead_ref[:, at]).astype(bf16)


def build_mask(local_ids, dead_local, aux_count):
    group, width = local_ids.shape
    lat_dev = dead_local.shape[1]
    hi_count, tokens = lat_dev // lanes, 64
    return pl.pallas_call(
        functools.partial(mask_kernel, tokens, hi_count, aux_count),
        out_shape=jax.ShapeDtypeStruct((group, lat_dev), bf16),
        grid=(group // tokens,),
        in_specs=[
            pl.BlockSpec((tokens, width), lambda i: (i, 0)),
            pl.BlockSpec((1, lat_dev), lambda i: (0, 0)),
        ],
        out_specs=pl.BlockSpec((tokens, lat_dev), lambda i: (i, 0)),
        scratch_shapes=[pltpu.VMEM((tokens * hi_count, lanes), f32)],
        compiler_params=pltpu.CompilerParams(vmem_limit_bytes=vmem_most),
        cost_estimate=pl.CostEstimate(
            flops=64 * group * lat_dev * width // 4, bytes_accessed=2 * group * lat_dev, transcendentals=0
        ),
        name="build_mask",
    )(local_ids, dead_local)


def head_kernel(chunk, chunks, normed_ref, table_ref, mean_ref, lse_ref):
    normed = normed_ref[...]

    def logits_of(c):
        return lax.dot_general(
            normed, table_ref[c * chunk : (c + 1) * chunk, :], contract_cols, preferred_element_type=f32
        )

    def fold(values, op):
        folded = values[:, :lanes]
        for k in range(1, chunk // lanes):
            folded = op(folded, values[:, k * lanes : (k + 1) * lanes])
        return folded

    top = total = mean = None
    logits = logits_of(0)
    for c in range(chunks):
        later = logits_of(c + 1) if c + 1 < chunks else None
        chunk_top = jnp.max(fold(logits, jnp.maximum), axis=1, keepdims=True)
        new_top = chunk_top if top is None else jnp.maximum(top, chunk_top)
        grown = jnp.exp(logits - new_top).astype(bf16)
        chunk_total = fold(grown.astype(f32), jnp.add)
        chunk_mean = lax.dot_general(
            grown, table_ref[c * chunk : (c + 1) * chunk, :], contract_plain, preferred_element_type=f32
        )
        if top is None:
            total, mean = chunk_total, chunk_mean
        else:
            shrink = jnp.exp(top - new_top)
            total, mean = total * shrink + chunk_total, mean * shrink + chunk_mean
        top, logits = new_top, later
    total = jnp.sum(total, axis=1, keepdims=True)
    mean_ref[...] = mean / total
    lse_ref[...] = top + jnp.log(total)


def head_part(normed, table):
    rows, width = normed.shape
    entries = table.shape[0]
    tiles = entries // lanes
    chunk = lanes * max(d for d in range(1, 14) if tiles % d == 0)
    block = 256
    return pl.pallas_call(
        functools.partial(head_kernel, chunk, entries // chunk),
        out_shape=(jax.ShapeDtypeStruct((rows, width), f32), jax.ShapeDtypeStruct((rows, 1), f32)),
        grid=(rows // block,),
        in_specs=[
            pl.BlockSpec((block, width), lambda i: (i, 0)),
            pl.BlockSpec((entries, width), lambda i: (0, 0), pipeline_mode=pl.Buffered(1)),
        ],
        out_specs=(
            pl.BlockSpec((block, width), lambda i: (i, 0)),
            pl.BlockSpec((block, 1), lambda i: (i, 0)),
        ),
        compiler_params=pltpu.CompilerParams(vmem_limit_bytes=vmem_most),
        cost_estimate=pl.CostEstimate(
            flops=6 * rows * entries * width,
            bytes_accessed=2 * entries * width + 6 * rows * width,
            transcendentals=rows * entries,
        ),
        name="head_part",
    )(normed, table)


def split_three(values):
    first = values.astype(bf16)
    rest = values - first.astype(f32)
    second = rest.astype(bf16)
    return first, second, (rest - second.astype(f32)).astype(bf16)


def enc_final_kernel(rep_count, left_ref, right_ref, full_ref, mom_ref, w_ref, w_out, mom_out, err_out):
    approx = lax.dot_general(
        left_ref[...], right_ref[...], contract_rows, preferred_element_type=f32
    )
    err_out[...] = full_ref[...] - approx * (1.0 / rep_count)
    mom = momentum_decay * mom_ref[...] + approx
    mom_out[...] = mom
    w_out[...] = w_ref[...] - rate_enc * mom


def dec_final_kernel(rep_count, left_ref, right_ref, full_ref, mom_ref, w_ref, w_out, mom_out, err_out):
    approx = lax.dot_general(
        right_ref[...], left_ref[...], contract_rows, preferred_element_type=f32
    )
    err_out[...] = full_ref[...] - approx * (1.0 / rep_count)
    mom = momentum_decay * mom_ref[...] + approx
    mom_out[...] = mom
    step = w_ref[...] - rate_dec * mom
    w_out[...] = step * lax.rsqrt(jnp.sum(step * step, axis=1, keepdims=True) + 1e-06)


def final_update(kernel, by_rows, rep_count, left, right, full, mom, weight):
    l1, l2, l3 = split_three(left)
    r1, r2, r3 = split_three(right)
    left = jnp.concatenate([l1, l1, l2, l2, l1, l3], axis=0)
    right = jnp.concatenate([r1, r2, r1, r2, r3, r1], axis=0)
    latents, width = right.shape[1], left.shape[1]
    block = 512
    if by_rows:
        big = pl.BlockSpec((block, width), lambda i: (i, 0))
    else:
        big = pl.BlockSpec((width, block), lambda i: (0, i))
    return pl.pallas_call(
        functools.partial(kernel, rep_count),
        out_shape=(jax.ShapeDtypeStruct(full.shape, f32),) * 3,
        grid=(latents // block,),
        in_specs=[
            pl.BlockSpec(left.shape, lambda i: (0, 0)),
            pl.BlockSpec((right.shape[0], block), lambda i: (0, i)),
            big,
            big,
            big,
        ],
        out_specs=(big, big, big),
        compiler_params=pltpu.CompilerParams(vmem_limit_bytes=vmem_most),
        cost_estimate=pl.CostEstimate(
            flops=2 * 48 * latents * width, bytes_accessed=24 * latents * width, transcendentals=0
        ),
        name="final_update",
    )(left, right, full, mom, weight)


def layer_norm(values, gain_row, shift_row):
    center = values - jnp.mean(values, axis=-1, keepdims=True)
    spread = jnp.mean(center * center, axis=-1, keepdims=True)
    return center * lax.rsqrt(spread + 1e-05) * gain_row + shift_row


def frozen_block(residual, norm_params, biases, qkv, w_out, fc, w_proj):
    seq_len = residual.shape[0]
    model_width = residual.shape[1]
    hidden_units = w_proj.shape[0]
    head_dim = model_width // HEADS
    stream = residual.astype(f32)
    normed = layer_norm(stream, norm_params[0], norm_params[1]).astype(bf16)

    def times(values, parts, bias):
        width = parts[0].shape[1]
        return [
            jnp.dot(values, part, preferred_element_type=f32) + bias[k * width : (k + 1) * width]
            for k, part in enumerate(parts)
        ]

    queries, keys, values = [
        part.astype(bf16).reshape(seq_len, HEADS, head_dim)
        for part in times(normed, qkv, biases[: 3 * model_width])
    ]
    scores = jnp.einsum("qhd,khd->hqk", queries, keys, preferred_element_type=f32) / math.sqrt(head_dim)
    causal = jnp.arange(seq_len)[:, None] >= jnp.arange(seq_len)[None, :]
    scores = jnp.where(causal, scores, -1e30)
    weights = jax.nn.softmax(scores, axis=-1).astype(bf16)
    attended = jnp.einsum("hqk,khd->qhd", weights, values, preferred_element_type=f32)
    attended = attended.astype(bf16).reshape(seq_len, model_width)
    stream = (
        stream
        + jnp.dot(attended, w_out, preferred_element_type=f32)
        + biases[3 * model_width : 4 * model_width]
    )
    normed = layer_norm(stream, norm_params[2], norm_params[3]).astype(bf16)
    inner_in = times(normed, fc, biases[4 * model_width : 4 * model_width + hidden_units])
    activated = jnp.concatenate(
        [jax.nn.gelu(part, approximate=True).astype(bf16) for part in inner_in], axis=1
    )
    return (
        stream
        + jnp.dot(activated, w_proj, preferred_element_type=f32)
        + biases[4 * model_width + hidden_units :]
    )


def orthonormal(left_factor):
    gram_matrix = jnp.dot(left_factor.T, left_factor, precision=largest_values)
    cholesky_low = jnp.linalg.cholesky(gram_matrix)
    return lax.linalg.triangular_solve(
        cholesky_low, left_factor, left_side=False, lower=True, transpose_a=True
    )


def times_factor(values, factor, numbers):
    rank = factor.shape[1]
    pieces = jnp.concatenate(split_three(factor), axis=1)
    product = lax.dot_general(values, pieces, numbers, preferred_element_type=f32)
    return product[:, :rank] + product[:, rank : 2 * rank] + product[:, 2 * rank :]


def per_device(
    residual,
    valid_mask,
    top_idx,
    aux_idx,
    dead_flags,
    norm_params,
    biases,
    w_qkv,
    w_out,
    w_fc,
    w_proj,
    head_table,
    w_enc,
    encoder_bias_vec,
    w_dec,
    decoder_bias_vec,
    mom_enc,
    mom_benc,
    mom_dec,
    mom_bdec,
    q_enc,
    q_dec,
    err_enc,
    err_dec,
):
    lat_count = lax.axis_size("lat")
    rep_count = lax.axis_size("rep")
    lat_index = lax.axis_index("lat")
    model_width = residual.shape[1]
    hidden_units = w_fc.shape[1]
    lat_dev = w_enc.shape[1]
    top_count, aux_count = top_idx.shape[1], aux_idx.shape[1]

    def side_by_side(weight):
        return [weight[:, k : k + model_width] for k in range(0, weight.shape[1], model_width)]

    share = w_qkv.shape[0]
    stacked = jnp.concatenate(side_by_side(w_qkv) + [w_out] + side_by_side(w_fc) + [w_proj], axis=0)
    gathered = lax.all_gather(stacked, "lat", axis=0)
    squares = [
        gathered[:, k * share : (k + 1) * share].reshape(model_width, model_width)
        for k in range(4 + hidden_units // model_width)
    ]
    proj_all = gathered[:, len(squares) * share :].reshape(hidden_units, model_width)

    half = aux_count // 2
    packed = jnp.concatenate([aux_idx[:, :half] * pack_base + aux_idx[:, half:], top_idx], axis=1)
    packed = gather_tokens(packed)
    group_rows = packed.shape[0]
    ids = jnp.concatenate([packed[:, :half] // pack_base, packed[:, :half] % pack_base, packed[:, half:]], axis=1)
    ids = ids - lat_index * lat_dev
    padding = -ids.shape[1] % lanes
    ids = jnp.concatenate([ids, jnp.full((group_rows, padding), -1, jnp.int32)], axis=1)
    dead_local = lax.dynamic_slice_in_dim(dead_flags, lat_index * lat_dev, lat_dev).astype(f32)
    mask = build_mask(ids, dead_local[None, :], aux_count)

    valid_float = valid_mask.astype(f32)
    valid_total = sum_over(jnp.full((1, lanes), jnp.sum(valid_float)), ("lat", "rep"))[0, 0]
    weight_own = (valid_float / valid_total)[:, None]

    enc_weight = w_enc.astype(bf16)
    dec_weight = w_dec.astype(bf16)
    err_left_enc = jnp.dot(err_enc[0], q_enc, precision=largest_values)
    err_left_dec = lax.dot_general(err_dec[0], q_dec, contract_rows, precision=largest_values)

    stream = frozen_block(
        residual, norm_params, biases, squares[:3], squares[3], squares[4:], proj_all
    )
    centered_group = gather_tokens((stream - decoder_bias_vec).astype(bf16))

    def final_norm(values):
        return layer_norm(values, norm_params[4], norm_params[5])

    orig_normed = final_norm(stream)
    orig_group = gather_tokens(orig_normed.astype(bf16))

    mask_top = (mask == 1.0) | (mask == 3.0)
    mask_aux = mask >= 2.0
    nothing = jnp.zeros((), bf16)
    code = (
        jnp.dot(centered_group, enc_weight, preferred_element_type=f32) + encoder_bias_vec
    ).astype(bf16)
    topk_code = jnp.where(mask_top, code, nothing)
    auxiliary_code = jnp.where(mask_aux, code, nothing)
    rebuilt_input = (
        scatter_sum(jnp.dot(topk_code, dec_weight, preferred_element_type=f32)) + decoder_bias_vec
    )
    rec_float, norm_back = jax.vjp(final_norm, rebuilt_input)
    rec_group = gather_tokens(rec_float.astype(bf16))

    orig_mean, orig_lse = head_part(orig_group, head_table)
    auxiliary_rebuilt = scatter_sum(jnp.dot(auxiliary_code, dec_weight, preferred_element_type=f32))
    orig_mean, orig_lse = scatter_mean(orig_mean, orig_lse)

    resid_err = stream - rebuilt_input - auxiliary_rebuilt
    aux_pull = -(2.0 * aux_weight) * weight_own * resid_err
    aux_group = gather_tokens(aux_pull.astype(bf16))

    rec_mean, rec_lse = head_part(rec_group, head_table)
    rec_mean, rec_lse = scatter_mean(rec_mean, rec_lse)

    gap = orig_normed.astype(bf16).astype(f32) - rec_float.astype(bf16).astype(f32)
    kl_own = jnp.sum(gap * orig_mean, axis=1) - orig_lse[:, 0] + rec_lse[:, 0]
    per_token = kl_own + aux_weight * jnp.sum(resid_err * resid_err, axis=1)
    loss_own = jnp.sum(valid_float * per_token)
    (grad_head,) = norm_back(weight_own * (rec_mean - orig_mean))
    grad_recon = (grad_head + aux_pull).astype(bf16)
    recon_group = gather_tokens(grad_recon)

    aux_back = lax.dot_general(aux_group, dec_weight, contract_cols, preferred_element_type=f32)
    grad_auxpre = jnp.where(mask_aux, aux_back.astype(bf16), nothing)
    top_back = lax.dot_general(recon_group, dec_weight, contract_cols, preferred_element_type=f32)
    grad_pre = jnp.where(mask_top, top_back.astype(bf16), nothing).astype(f32) + grad_auxpre.astype(f32)
    grad_benc = jnp.sum(grad_pre, axis=0)
    grad_pre = grad_pre.astype(bf16)

    left_enc = err_left_enc + times_factor(
        centered_group, times_factor(grad_pre, q_enc, contract_plain), contract_rows
    )
    left_dec = (
        err_left_dec
        + times_factor(recon_group, times_factor(topk_code, q_dec, contract_plain), contract_rows)
        + times_factor(aux_group, times_factor(auxiliary_code, q_dec, contract_plain), contract_rows)
    )
    grad_bdec = jnp.sum(grad_recon.astype(f32), axis=0) - jnp.dot(
        enc_weight.astype(f32), grad_benc, precision=largest_values
    )
    rank = q_enc.shape[1]
    small = jnp.concatenate(
        [left_enc.T, left_dec.T, grad_bdec[None], jnp.full((1, model_width), loss_own)], axis=0
    )
    small = sum_over(small, ("lat", "rep"))
    left_enc, left_dec = small[:rank].T, small[rank : 2 * rank].T
    grad_bdec, loss_sum = small[2 * rank], small[2 * rank + 1, 0]

    full_enc = (
        lax.dot_general(centered_group, grad_pre, contract_rows, preferred_element_type=f32) + err_enc[0]
    )
    full_dec = (
        lax.dot_general(topk_code, recon_group, contract_rows, preferred_element_type=f32)
        + lax.dot_general(auxiliary_code, aux_group, contract_rows, preferred_element_type=f32)
        + err_dec[0]
    )
    ortho_enc = orthonormal(left_enc)
    ortho_dec = orthonormal(left_dec)
    right_enc = lax.dot_general(ortho_enc, full_enc, contract_rows, precision=largest_values)
    right_dec = lax.dot_general(
        ortho_dec, full_dec, (((0,), (1,)), ((), ())), precision=largest_values
    )
    rights = sum_over(
        jnp.concatenate([right_enc, right_dec, grad_benc[None]], axis=0), ("rep",), sent_as=bf16
    )
    right_enc, right_dec, grad_benc = rights[:rank], rights[rank : 2 * rank], rights[2 * rank]

    w_enc_new, mom_enc_new, err_enc_new = final_update(
        enc_final_kernel, False, rep_count, ortho_enc.T, right_enc, full_enc, mom_enc, w_enc
    )
    w_dec_new, mom_dec_new, err_dec_new = final_update(
        dec_final_kernel, True, rep_count, ortho_dec.T, right_dec, full_dec, mom_dec, w_dec
    )
    mom_benc_new = momentum_decay * mom_benc + grad_benc
    mom_bdec_new = momentum_decay * mom_bdec + grad_bdec
    b_enc_new = encoder_bias_vec - rate_benc * mom_benc_new
    b_dec_new = decoder_bias_vec - rate_bdec * mom_bdec_new
    return (
        loss_sum,
        valid_total,
        w_enc_new,
        b_enc_new,
        w_dec_new,
        b_dec_new,
        mom_enc_new,
        mom_benc_new,
        mom_dec_new,
        mom_bdec_new,
        right_enc.T,
        right_dec.T,
        err_enc_new[None],
        err_dec_new[None],
    )


def solution(mesh):
    in_specs = (
        P(("rep", "lat"), None),
        P(("rep", "lat")),
        P(("rep", "lat"), None),
        P(("rep", "lat"), None),
        P(),
        P(),
        P(),
        P("lat", None),
        P("lat", None),
        P("lat", None),
        P("lat", None),
        P("lat", None),
        P(None, "lat"),
        P("lat"),
        P("lat", None),
        P(),
        P(None, "lat"),
        P("lat"),
        P("lat", None),
        P(),
        P("lat", None),
        P("lat", None),
        P("rep", None, "lat"),
        P("rep", "lat", None),
    )
    out_specs = (
        P(),
        P(),
        P(None, "lat"),
        P("lat"),
        P("lat", None),
        P(),
        P(None, "lat"),
        P("lat"),
        P("lat", None),
        P(),
        P("lat", None),
        P("lat", None),
        P("rep", None, "lat"),
        P("rep", "lat", None),
    )
    return jax.shard_map(
        per_device, mesh=mesh, in_specs=in_specs, out_specs=out_specs, check_vma=False
    )
```

```python
import functools
import math

import jax
import jax.numpy as jnp
from jax import lax
from jax.experimental import pallas as pl
from jax.experimental.pallas import tpu as pltpu
from jax.sharding import PartitionSpec as P

HEADS = 12

pack_base = 32768
aux_weight = 1.0 / 32.0
momentum_decay = 0.9
rate_enc = 3000.0
rate_dec = 3000.0
rate_benc = 10000.0
rate_bdec = 500.0
lanes = 128
vmem_most = 60 * 2**20
contract_cols = (((1,), (1,)), ((), ()))
contract_rows = (((0,), (0,)), ((), ()))
contract_plain = (((1,), (0,)), ((), ()))
f32 = jnp.float32
bf16 = jnp.bfloat16


def swap(values, axis, bit):
    count = lax.axis_size(axis)
    return lax.ppermute(values, axis, [(i, i ^ bit) for i in range(count)])


def bits_of(axis):
    count = lax.axis_size(axis)
    return [1 << k for k in range(count.bit_length() - 1)]


def even_order():
    count = lax.axis_size("lat")
    return [2, 6, 4, 0] if count == 8 else list(range(count - 2, -1, -2))


def gather_even(own):
    if lax.axis_size("lat") == 8:
        half = own.shape[0] // 2
        by_two, by_four = swap(own, "lat", 2), swap(own, "lat", 4)
        return jnp.concatenate(
            [by_two, swap(by_four[:half], "lat", 2), swap(by_two[half:], "lat", 4), by_four, own], axis=0
        )
    blocks = {0: own}
    for bit in bits_of("lat")[1:]:
        order = sorted(blocks)
        moved = swap(jnp.stack([blocks[j] for j in order]), "lat", bit)
        for at, j in enumerate(order):
            blocks[j ^ bit] = moved[at]
    return jnp.concatenate([blocks[j] for j in even_order()], axis=0)


def gather_tokens(own):
    even = gather_even(own)
    return even, swap(even, "lat", 1)


def scatter_paths():
    others = bits_of("lat")[1:]
    if len(others) == 2:
        return [(0, 2, others), (1, 2, others[::-1])]
    return [(0, 1, others)]


def take_blocks(values, part, parts):
    rows, width = values.shape[0] // len(even_order()), values.shape[1] // parts
    return {
        j: values[at * rows : (at + 1) * rows, part * width : (part + 1) * width]
        for at, j in enumerate(even_order())
    }


def scatter_sum(even, odd_moved):
    chip = even + odd_moved
    done = []
    for part, parts, order in scatter_paths():
        held = take_blocks(chip, part, parts)
        for bit in order:
            sent = [j for j in even_order() if j in held and j & bit]
            got = swap(jnp.concatenate([held[j] for j in sent], axis=0).astype(bf16), "lat", bit)
            rows = held[0].shape[0]
            for at, j in enumerate(sent):
                held[j ^ bit] = held[j ^ bit] + got[at * rows : (at + 1) * rows].astype(f32)
                del held[j]
        done.append(held[0])
    return jnp.concatenate(done, axis=1)


def merge(mean_a, lse_a, mean_b, lse_b):
    top = jnp.maximum(lse_a, lse_b)
    exp_a, exp_b = jnp.exp(lse_a - top), jnp.exp(lse_b - top)
    total = exp_a + exp_b
    mixed = mean_a.astype(f32) * (exp_a / total) + mean_b.astype(f32) * (exp_b / total)
    return mixed, top + jnp.log(total)


def scatter_mean(even, even_lse, odd_moved, odd_lse_moved):
    chip, chip_lse = merge(even, even_lse, odd_moved, odd_lse_moved)
    done = []
    for part, parts, order in scatter_paths():
        means, lses = take_blocks(chip, part, parts), take_blocks(chip_lse, 0, 1)
        held = {j: (means[j], lses[j]) for j in means}
        for bit in order:
            sent = [j for j in even_order() if j in held and j & bit]
            rows = held[0][0].shape[0]
            got = swap(jnp.concatenate([held[j][0] for j in sent], axis=0).astype(bf16), "lat", bit)
            got_lse = swap(jnp.concatenate([held[j][1] for j in sent], axis=0), "lat", bit)
            for at, j in enumerate(sent):
                span = slice(at * rows, (at + 1) * rows)
                held[j ^ bit] = merge(*held[j ^ bit], got[span], got_lse[span])
                del held[j]
        done.append(held[0])
    return jnp.concatenate([mean for mean, _ in done], axis=1), done[0][1]


def sum_round(values, axis, bits, sent_as=None):
    if sent_as is not None:
        values = values.astype(sent_as)
    if len(bits) == 2:
        one, two, both = (swap(values, axis, bit) for bit in (bits[0], bits[1], bits[0] | bits[1]))
        return (values.astype(f32) + one.astype(f32)) + (two.astype(f32) + both.astype(f32))
    for bit in bits:
        values = values.astype(f32) + swap(values, axis, bit).astype(f32)
    return values


untouched = pl.BlockSpec(memory_space=pl.ANY)
in_vmem = pl.BlockSpec(memory_space=pltpu.VMEM)


def dot(a, b, numbers):
    return lax.dot_general(a, b, numbers, preferred_element_type=f32)


def call(kernel, name, args, out_shape, grid=(), in_specs=None, out_specs=None, deps=(), cost=(0, 0), aliases=None, scratch=()):
    count, skipped = len(args), len(deps)

    def body(*refs):
        kernel(*refs[:count], *refs[count + skipped :])

    if in_specs is None:
        in_specs = [in_vmem] * count
        out_specs = jax.tree.map(lambda _: in_vmem, out_shape)
    flops, moved = cost
    return pl.pallas_call(
        body,
        out_shape=out_shape,
        grid=grid,
        in_specs=list(in_specs) + [untouched] * skipped,
        out_specs=out_specs,
        scratch_shapes=list(scratch),
        input_output_aliases=aliases or {},
        compiler_params=pltpu.CompilerParams(vmem_limit_bytes=vmem_most),
        cost_estimate=pl.CostEstimate(flops=flops, bytes_accessed=moved, transcendentals=0),
        name=name,
    )(*args, *deps)


def like(shape, dtype=f32):
    return jax.ShapeDtypeStruct(shape, dtype)


def clear_at_start(*refs):
    @pl.when(pl.program_id(0) == 0)
    def _():
        for ref in refs:
            ref[...] = jnp.zeros_like(ref)


def mask_kernel(tokens, hi_count, aux_count, ids_ref, dead_ref, own_ref, partner_ref, scratch):
    width = ids_ref.shape[1]
    hi_rows = lax.broadcasted_iota(jnp.int32, (2 * hi_count, width), 0)
    lo_rows = lax.broadcasted_iota(jnp.int32, (lanes, width), 0)
    is_aux = lax.broadcasted_iota(jnp.int32, (2 * hi_count, width), 1) < aux_count
    weight = jnp.where(is_aux, 2.0, 1.0)

    def one_token(t, carry):
        row = ids_ref[pl.ds(t, 1), :]
        hi_hot = jnp.where(hi_rows == (row >> 7), weight, 0.0).astype(bf16)
        lo_hot = jnp.where(lo_rows == (row & 127), 1.0, 0.0).astype(bf16)
        picked = lax.dot_general(hi_hot, lo_hot, contract_cols, preferred_element_type=f32)
        at = pl.multiple_of(t * 2 * hi_count, 2 * hi_count)
        scratch[pl.ds(at, 2 * hi_count), :] = picked
        return carry

    lax.fori_loop(0, tokens, one_token, 0, unroll=16)
    for hi in range(2 * hi_count):
        code = scratch[pl.ds(hi, tokens, stride=2 * hi_count), :]
        aux = jnp.where(code >= 2.0, 2.0, 0.0)
        code = (code - aux + aux * dead_ref[:, hi * lanes : (hi + 1) * lanes]).astype(bf16)
        if hi < hi_count:
            own_ref[:, hi * lanes : (hi + 1) * lanes] = code
        else:
            partner_ref[:, (hi - hi_count) * lanes : (hi - hi_count + 1) * lanes] = code


def build_mask(pair_ids, dead_pair, aux_count):
    rows, width = pair_ids.shape
    lat_dev = dead_pair.shape[1] // 2
    hi_count, tokens = lat_dev // lanes, 64
    out_block = pl.BlockSpec((tokens, lat_dev), lambda i: (i, 0))
    return pl.pallas_call(
        functools.partial(mask_kernel, tokens, hi_count, aux_count),
        out_shape=(jax.ShapeDtypeStruct((rows, lat_dev), bf16),) * 2,
        grid=(rows // tokens,),
        in_specs=[
            pl.BlockSpec((tokens, width), lambda i: (i, 0)),
            pl.BlockSpec((1, 2 * lat_dev), lambda i: (0, 0)),
        ],
        out_specs=(out_block, out_block),
        scratch_shapes=[pltpu.VMEM((tokens * 2 * hi_count, lanes), f32)],
        compiler_params=pltpu.CompilerParams(vmem_limit_bytes=vmem_most),
        cost_estimate=pl.CostEstimate(
            flops=16 * rows * 2 * lat_dev * width, bytes_accessed=4 * rows * lat_dev, transcendentals=0
        ),
        name="build_mask",
    )(pair_ids, dead_pair)


def split_three(values):
    first = values.astype(bf16)
    rest = values - first.astype(f32)
    second = rest.astype(bf16)
    return first, second, (rest - second.astype(f32)).astype(bf16)


def split_floats(values):
    return [piece.astype(f32) for piece in split_three(values)]


def high_low(values):
    high = values.astype(bf16)
    return high, (values - high.astype(f32)).astype(bf16)


def halves_kernel(by_two_ref, by_four_ref, first_ref, second_ref):
    half = by_two_ref.shape[0] // 2
    first_ref[...] = by_four_ref[:half, :]
    second_ref[...] = by_two_ref[half:, :]


def assemble_kernel(by_two_ref, first_ref, second_ref, by_four_ref, own_ref, even_ref):
    rows = own_ref.shape[0]
    even_ref[:rows, :] = by_two_ref[...]
    even_ref[rows : rows + rows // 2, :] = first_ref[...]
    even_ref[rows + rows // 2 : 2 * rows, :] = second_ref[...]
    even_ref[2 * rows : 3 * rows, :] = by_four_ref[...]
    even_ref[3 * rows :, :] = own_ref[...]


class Gather:
    def __init__(self, own):
        self.own, self.plain = own, lax.axis_size("lat") != 8
        if not self.plain:
            self.by_two, self.by_four = swap(own, "lat", 2), swap(own, "lat", 4)

    def middle(self, *deps):
        if not self.plain:
            rows, width = self.own.shape
            piece = like((rows // 2, width), self.own.dtype)
            first, second = call(halves_kernel, "halves", (self.by_two, self.by_four), (piece, piece), deps=deps)
            self.diag = swap(first, "lat", 2), swap(second, "lat", 4)

    def end(self, *deps):
        if self.plain:
            return gather_tokens(self.own)
        rows, width = self.own.shape
        even = call(
            assemble_kernel,
            "assemble",
            (self.by_two, *self.diag, self.by_four, self.own),
            like((4 * rows, width), self.own.dtype),
            deps=deps,
        )
        return even, swap(even, "lat", 1)


def reorder_kernel(blocks_ref, even_ref, odd_ref):
    me, rows = lax.axis_index("lat"), blocks_ref.shape[1]
    for at, j in enumerate(even_order()):
        even_ref[at * rows : (at + 1) * rows, :] = blocks_ref[me ^ j]
        odd_ref[at * rows : (at + 1) * rows, :] = blocks_ref[me ^ (j ^ 1)]


def gather_behind(own, *deps):
    blocks = lax.all_gather(own, "lat", axis=0)
    count, rows, width = blocks.shape
    half = like((count // 2 * rows, width), own.dtype)
    return call(reorder_kernel, "reorder", (blocks,), (half, half), deps=deps)


def weigh(lse_a, lse_b):
    top = jnp.maximum(lse_a, lse_b)
    exp_a, exp_b = jnp.exp(lse_a - top), jnp.exp(lse_b - top)
    total = exp_a + exp_b
    return exp_a / total, exp_b / total, top + jnp.log(total)


def joint(a, b, tail):
    if not tail:
        return a + b
    share_a, share_b, lse = weigh(a[:, -tail:], b[:, -tail:])
    return jnp.concatenate([a[:, :-tail] * share_a[:, :1] + b[:, :-tail] * share_b[:, :1], lse], axis=1)


def to_send(values, tail):
    if not tail:
        return values.astype(bf16)
    lane = lax.broadcasted_iota(jnp.int32, (values.shape[0], tail), 1)
    one, two, three = split_floats(values[:, -tail:])
    logs = jnp.where(lane < 32, one, jnp.where(lane < 64, two, three))
    return jnp.concatenate([values[:, :-tail], logs], axis=1).astype(bf16)


def received(ref, span, tail):
    values = ref[span, :].astype(f32)
    if not tail:
        return values
    logs = values[:, -tail:]
    lse = logs[:, :1] + logs[:, 32:33] + logs[:, 64:65]
    return jnp.concatenate([values[:, :-tail], jnp.broadcast_to(lse, logs.shape)], axis=1)


def chip_kernel(tail, even_ref, odd_ref, keep_a, send_a, keep_b, send_b):
    rows = even_ref.shape[0] // 4
    total = joint(even_ref[...], odd_ref[...], tail)
    half = (total.shape[1] - tail) // 2

    def columns(values, part):
        means = values[:, part * half : (part + 1) * half]
        return jnp.concatenate([means, values[:, -tail:]], axis=1) if tail else means

    send_a[...] = to_send(columns(total[: 2 * rows], 0), tail)
    keep_a[...] = columns(total[2 * rows :], 0)
    send_b[...] = to_send(columns(total[rows : 3 * rows], 1), tail)
    keep_b[:rows, :] = columns(total[:rows], 1)
    keep_b[rows:, :] = columns(total[3 * rows :], 1)


def hop_kernel(tail, keep_a, got_a, keep_b, got_b, next_a, send_a, next_b, send_b):
    rows = keep_a.shape[0] // 2
    early, late = slice(0, rows), slice(rows, 2 * rows)
    send_a[...] = to_send(joint(keep_a[early, :], received(got_a, late, tail), tail), tail)
    next_a[...] = joint(keep_a[late, :], received(got_a, early, tail), tail)
    send_b[...] = to_send(joint(keep_b[early, :], received(got_b, early, tail), tail), tail)
    next_b[...] = joint(keep_b[late, :], received(got_b, late, tail), tail)


def last_kernel(tail, keep_a, got_a, keep_b, got_b, total_ref):
    rows = keep_a.shape[0]
    for part, (keep, got) in enumerate(((keep_a, got_a), (keep_b, got_b))):
        total = joint(keep[...], received(got, slice(0, rows), tail), tail)
        half = total.shape[1] - tail
        total_ref[:, part * half : (part + 1) * half] = total[:, :half]
        if tail and part == 0:
            total_ref[:, 2 * half :] = total[:, half:]


class Scatter:
    def __init__(self, odd, tail=0):
        self.moved, self.tail, self.plain = swap(odd, "lat", 1), tail, lax.axis_size("lat") != 8

    def step(self, kernel, name, args, rows, width, deps):
        outs = (like((rows, width)), like((rows, width), bf16))
        self.state = call(functools.partial(kernel, self.tail), name, args, outs * 2, deps=deps)

    def chip(self, even, *deps):
        self.even = even
        if not self.plain:
            rows, width = even.shape
            self.width = (width - self.tail) // 2 + self.tail
            self.rows = rows // 4
            self.step(chip_kernel, "chip_sum", (even, self.moved), 2 * self.rows, self.width, deps)
            keep_a, send_a, keep_b, send_b = self.state
            self.pending = keep_a, swap(send_a, "lat", 2), keep_b, swap(send_b, "lat", 4)
            return send_a
        return even

    def hop(self, *deps):
        if self.plain:
            return self.even
        self.step(hop_kernel, "hop_sum", self.pending, self.rows, self.width, deps)
        keep_a, send_a, keep_b, send_b = self.state
        self.pending = keep_a, swap(send_a, "lat", 4), keep_b, swap(send_b, "lat", 2)
        return send_a

    def last(self, *deps):
        if self.plain:
            if not self.tail:
                return scatter_sum(self.even, self.moved)
            width = self.even.shape[1] - self.tail
            mean, lse = scatter_mean(
                self.even[:, :width], self.even[:, width : width + 1], self.moved[:, :width], self.moved[:, width : width + 1]
            )
            return jnp.concatenate([mean, jnp.broadcast_to(lse, (lse.shape[0], self.tail))], axis=1)
        width = 2 * (self.width - self.tail) + self.tail
        return call(
            functools.partial(last_kernel, self.tail), "last_sum", self.pending, like((self.rows, width)), deps=deps
        )


def head_kernel(chunk, chunks, normed_ref, table_ref, out_ref):
    normed = normed_ref[...]

    def logits_of(c):
        return dot(normed, table_ref[c * chunk : (c + 1) * chunk, :], contract_cols)

    def fold(values, op):
        folded = values[:, :lanes]
        for k in range(1, chunk // lanes):
            folded = op(folded, values[:, k * lanes : (k + 1) * lanes])
        return folded

    top = total = mean = None
    logits = logits_of(0)
    for c in range(chunks):
        later = logits_of(c + 1) if c + 1 < chunks else None
        chunk_top = jnp.max(fold(logits, jnp.maximum), axis=1, keepdims=True)
        new_top = chunk_top if top is None else jnp.maximum(top, chunk_top)
        grown = jnp.exp(logits - new_top).astype(bf16)
        chunk_total = fold(grown.astype(f32), jnp.add)
        chunk_mean = dot(grown, table_ref[c * chunk : (c + 1) * chunk, :], contract_plain)
        if top is None:
            total, mean = chunk_total, chunk_mean
        else:
            shrink = jnp.exp(top - new_top)
            total, mean = total * shrink + chunk_total, mean * shrink + chunk_mean
        top, logits = new_top, later
    total = jnp.sum(total, axis=1, keepdims=True)
    width = mean.shape[1]
    out_ref[:, :width] = mean / total
    out_ref[:, width:] = jnp.broadcast_to(top + jnp.log(total), (mean.shape[0], lanes))


def head_part(normed, table, *deps):
    rows, width = normed.shape
    entries = table.shape[0]
    tiles = entries // lanes
    chunk = lanes * max(d for d in range(1, 14) if tiles % d == 0)
    block = min(512, rows)
    return call(
        functools.partial(head_kernel, chunk, entries // chunk),
        "head_part",
        (normed, table),
        like((rows, width + lanes)),
        (rows // block,),
        [
            pl.BlockSpec((block, width), lambda i: (i, 0)),
            pl.BlockSpec(table.shape, lambda i: (0, 0), pipeline_mode=pl.Buffered(1)),
        ],
        pl.BlockSpec((block, width + lanes), lambda i: (i, 0)),
        deps,
        (6 * rows * entries * width, 2 * entries * width),
    )


def round_kernel(values_ref, out_ref):
    out_ref[...] = values_ref[...].astype(bf16)


def rounded(values, by_rows, *deps):
    latents = values.shape[0 if by_rows else 1]
    block = min(1024, latents)
    spec = row_block(block, values.shape[1]) if by_rows else column_block(values.shape[0], block)
    return call(
        round_kernel,
        "rounded",
        (values,),
        like(values.shape, bf16),
        (latents // block,),
        [spec],
        spec,
        deps,
        (0, 6 * values.size),
    )


def pieces_kernel(factor_ref, rows_ref, columns_ref):
    one, two, three = split_floats(factor_ref[...])
    rank, latents = one.shape
    rows_ref[...] = jnp.concatenate([one, two, three, jnp.zeros_like(one)], axis=0).astype(bf16)
    tall = jnp.concatenate([one, two, three, jnp.zeros((lanes - 3 * rank, latents), f32)], axis=0)
    columns_ref[...] = tall.T.astype(bf16)


def factor_pieces(factor, *deps):
    rank, latents = factor.shape
    block = min(1024, latents)
    return call(
        pieces_kernel,
        "factor_pieces",
        (factor,),
        (like((4 * rank, latents), bf16), like((latents, lanes), bf16)),
        (latents // block,),
        [column_block(rank, block)],
        (column_block(4 * rank, block), row_block(block, lanes)),
        deps,
        (0, 1024 * latents),
    )


def column_block(rows, block):
    return pl.BlockSpec((rows, block), lambda i: (0, i))


def row_block(block, width):
    return pl.BlockSpec((block, width), lambda i: (i, 0))


def whole_of(shape):
    return pl.BlockSpec(shape, lambda i: (0,) * len(shape))


def forward_kernel(inputs_ref, enc_ref, bias_ref, mask_ref, dec_ref, tops_ref, auxes_ref, part_ref):
    clear_at_start(part_ref)
    code = (dot(inputs_ref[...], enc_ref[...], contract_plain) + bias_ref[...]).astype(bf16)
    mask = mask_ref[...]
    nothing = jnp.zeros((), bf16)
    tops = jnp.where((mask == 1.0) | (mask == 3.0), code, nothing)
    tops_ref[...] = tops
    auxes_ref[...] = jnp.where(mask >= 2.0, code, nothing)
    part_ref[...] += dot(tops, dec_ref[...], contract_plain)


def forward(inputs, enc, bias, mask, dec, *deps):
    rows, width = inputs.shape
    latents = enc.shape[1]
    block = min(1024, latents)
    column = column_block(rows, block)
    return call(
        forward_kernel,
        "forward",
        (inputs, enc, bias, mask, dec),
        (like((rows, latents), bf16), like((rows, latents), bf16), like((rows, width))),
        (latents // block,),
        [whole_of((rows, width)), column_block(width, block), column_block(1, block), column, row_block(block, width)],
        (column, column, whole_of((rows, width))),
        deps,
        (4 * rows * latents * width, 2 * latents * (2 * width + 3 * rows)),
    )


def aux_forward_kernel(odd_ref, even_ref, dec_ref, out_ref, odd_sum, even_sum):
    clear_at_start(odd_sum, even_sum)
    odd_sum[...] += dot(odd_ref[...], dec_ref[...], contract_plain)
    even_sum[...] += dot(even_ref[...], dec_ref[...], contract_plain)

    @pl.when(pl.program_id(0) == pl.num_programs(0) - 1)
    def _():
        me, rows = lax.axis_index("lat"), out_ref.shape[1]
        for at, j in enumerate(even_order()):
            out_ref[me ^ j] = even_sum[at * rows : (at + 1) * rows, :]
            out_ref[me ^ (j ^ 1)] = odd_sum[at * rows : (at + 1) * rows, :]


def aux_forward(odd, even, dec, *deps):
    latents, width = dec.shape
    rows, count = odd.shape[0], lax.axis_size("lat")
    block = min(1024, latents)
    column, shape = column_block(rows, block), (count, 2 * rows // count, width)
    return call(
        aux_forward_kernel,
        "aux_forward",
        (odd, even, dec),
        like(shape),
        (latents // block,),
        [column, column, row_block(block, width)],
        whole_of(shape),
        deps,
        (4 * rows * latents * width, 2 * latents * (width + 2 * rows)),
        scratch=[pltpu.VMEM((rows, width), f32)] * 2,
    )


def aux_back_kernel(odd_ref, even_ref, dec_ref, odd_mask, even_mask, odd_out, even_out):
    dec = dec_ref[...]
    for grads, mask, out in ((odd_ref, odd_mask, odd_out), (even_ref, even_mask, even_out)):
        pulled = dot(grads[...], dec, contract_cols).astype(bf16)
        out[...] = jnp.where(mask[...] >= 2.0, pulled, jnp.zeros((), bf16))


def aux_back(odd, even, dec, odd_mask, even_mask, *deps):
    latents, width = dec.shape
    rows = odd.shape[0]
    block = min(1024, latents)
    column, whole = column_block(rows, block), whole_of((rows, width))
    return call(
        aux_back_kernel,
        "aux_back",
        (odd, even, dec, odd_mask, even_mask),
        (like((rows, latents), bf16),) * 2,
        (latents // block,),
        [whole, whole, row_block(block, width), column, column],
        (column, column),
        deps,
        (4 * rows * latents * width, 2 * latents * (width + 4 * rows)),
    )


def product_kernel(odd_ref, even_ref, factor_ref, odd_out, even_out):
    clear_at_start(odd_out, even_out)
    odd_out[...] += dot(odd_ref[...], factor_ref[...], contract_plain)
    even_out[...] += dot(even_ref[...], factor_ref[...], contract_plain)


def factor_products(odd, even, factor, *deps):
    rows, latents = odd.shape
    block = min(1024, latents)
    column, out = column_block(rows, block), whole_of((rows, lanes))
    return call(
        product_kernel,
        "factor_products",
        (odd, even, factor),
        (like((rows, lanes)),) * 2,
        (latents // block,),
        [column, column, row_block(block, lanes)],
        (out, out),
        deps,
        (4 * rows * latents * lanes, 4 * latents * rows),
    )


def add_left(ref, pieces, values, numbers):
    high, low = high_low(values)
    by_high, by_low = dot(pieces, high, numbers), dot(pieces, low, numbers)
    ref[...] += (by_high[:8] + by_high[8:16] + by_high[16:24]) + (by_low[:8] + by_low[8:16])


def err_left_kernel(pieces_ref, err_ref, out_ref):
    clear_at_start(out_ref)
    add_left(out_ref, pieces_ref[...], err_ref[...], contract_cols)


def err_left(pieces, err, *deps):
    width, latents = err.shape
    block = min(1024, latents)
    return call(
        err_left_kernel,
        "err_left",
        (pieces, err),
        like((8, width)),
        (latents // block,),
        [column_block(32, block), column_block(width, block)],
        whole_of((8, width)),
        deps,
        (128 * latents * width, 4 * latents * width),
    )


def part_dec_kernel(odd_codes, even_codes, odd_grads, even_grads, err_ref, pieces_ref, part_ref, left_ref):
    total = err_ref[...] + dot(odd_codes[...], odd_grads[...], contract_rows)
    total = total + dot(even_codes[...], even_grads[...], contract_rows)
    part_ref[...] = total
    clear_at_start(left_ref)
    add_left(left_ref, pieces_ref[...], total, contract_plain)


def part_dec(codes, grads, err, pieces, *deps):
    latents, width = err.shape
    rows = codes[0].shape[0]
    block = min(1024, latents)
    column, whole, big = column_block(rows, block), whole_of((rows, width)), row_block(block, width)
    return call(
        part_dec_kernel,
        "part_dec",
        (*codes, *grads, err, pieces),
        (like((latents, width)), like((8, width))),
        (latents // block,),
        [column, column, whole, whole, big, column_block(32, block)],
        (big, whole_of((8, width))),
        deps,
        (4 * rows * latents * width, latents * (8 * width + 4 * rows)),
    )


def add_dec_kernel(odd_codes, even_codes, odd_grads, even_grads, base_ref, out_ref):
    total = base_ref[...] + dot(odd_codes[...], odd_grads[...], contract_rows)
    out_ref[...] = total + dot(even_codes[...], even_grads[...], contract_rows)


def add_dec(codes, grads, base, part, parts, *deps):
    latents, width = base.shape
    rows = codes[0].shape[0]
    block = min(1024, latents // parts)
    steps = latents // parts // block
    column = pl.BlockSpec((rows, block), lambda i: (0, i + part * steps))
    big = pl.BlockSpec((block, width), lambda i: (i + part * steps, 0))
    whole = whole_of((rows, width))
    return call(
        add_dec_kernel,
        "add_dec",
        (*codes, *grads, base),
        like((latents, width)),
        (steps,),
        [column, column, whole, whole, big],
        big,
        deps,
        (4 * rows * latents * width // parts, latents * (8 * width + 4 * rows) // parts),
        aliases={4: 0},
    )


def form_enc_kernel(odd_inputs, even_inputs, odd_grads, even_grads, err_ref, out_ref):
    total = err_ref[...] + dot(odd_inputs[...], odd_grads[...], contract_rows)
    out_ref[...] = total + dot(even_inputs[...], even_grads[...], contract_rows)


def form_enc(inputs, grads, err, *deps):
    width, latents = err.shape
    rows = grads[0].shape[0]
    block = min(1024, latents)
    column, whole, big = column_block(rows, block), whole_of((rows, width)), column_block(width, block)
    return call(
        form_enc_kernel,
        "form_enc",
        (*inputs, *grads, err),
        like((width, latents)),
        (latents // block,),
        [whole, whole, column, column, big],
        big,
        deps,
        (4 * rows * latents * width, latents * (8 * width + 4 * rows)),
    )


def back_kernel(odd_ref, even_ref, dec_ref, enc_ref, odd_mask, even_mask, odd_aux, even_aux, factor_ref, *outs):
    odd_out, even_out, bias_ref, pull_ref, odd_sums, even_sums = outs
    dec, factor = dec_ref[...], factor_ref[...]
    clear_at_start(pull_ref, odd_sums, even_sums)
    nothing = jnp.zeros((), bf16)
    bias = None
    for grads, mask, aux, out, sums in (
        (odd_ref, odd_mask, odd_aux, odd_out, odd_sums),
        (even_ref, even_mask, even_aux, even_out, even_sums),
    ):
        pulled = dot(grads[...], dec, contract_cols).astype(bf16)
        mask = mask[...]
        total = jnp.where((mask == 1.0) | (mask == 3.0), pulled, nothing).astype(f32) + aux[...].astype(f32)
        column = jnp.sum(total, axis=0, keepdims=True)
        bias = column if bias is None else bias + column
        rounded = total.astype(bf16)
        out[...] = rounded
        sums[...] += dot(rounded, factor, contract_plain)
    bias_ref[...] = bias
    one, two, three = split_floats(bias)
    pieces = jnp.concatenate([one, two, three, jnp.zeros((13, bias.shape[1]), f32)], axis=0).astype(bf16)
    pull_ref[...] += dot(pieces, enc_ref[...], contract_cols)


def back_pass(odd, even, dec, enc, odd_mask, even_mask, odd_aux, even_aux, factor, *deps):
    latents, width = dec.shape
    rows = odd.shape[0]
    block = min(1024, latents)
    column, whole = column_block(rows, block), whole_of((rows, width))
    return call(
        back_kernel,
        "back_pass",
        (odd, even, dec, enc, odd_mask, even_mask, odd_aux, even_aux, factor),
        (
            like((rows, latents), bf16),
            like((rows, latents), bf16),
            like((1, latents)),
            like((16, width)),
            like((rows, lanes)),
            like((rows, lanes)),
        ),
        (latents // block,),
        [whole, whole, row_block(block, width), column_block(width, block)]
        + [column] * 4
        + [row_block(block, lanes)],
        (
            column,
            column,
            column_block(1, block),
            whole_of((16, width)),
            whole_of((rows, lanes)),
            whole_of((rows, lanes)),
        ),
        deps,
        (4 * rows * latents * (width + lanes), 2 * latents * (2 * width + 6 * rows)),
    )


def left_sums_kernel(
    rank,
    enc_odd,
    enc_even,
    odd_inputs,
    even_inputs,
    dec_odd,
    dec_even,
    odd_grads,
    even_grads,
    enc_base,
    dec_base,
    own_grads,
    pull_ref,
    loss_ref,
    out_ref,
):
    def against(products, inputs):
        total = None
        for piece in split_three(products[...]):
            wide = dot(piece, inputs[...], contract_rows)
            total = wide if total is None else total + wide
        return total[:rank] + total[rank : 2 * rank] + total[2 * rank : 3 * rank]

    out_ref[:rank, :] = enc_base[...] + against(enc_odd, odd_inputs) + against(enc_even, even_inputs)
    out_ref[rank : 2 * rank, :] = dec_base[...] + against(dec_odd, odd_grads) + against(dec_even, even_grads)
    bias = jnp.sum(own_grads[...].astype(f32), axis=0, keepdims=True)
    bias = bias - jnp.sum(pull_ref[...], axis=0, keepdims=True)
    index = lax.broadcasted_iota(jnp.int32, (8, bias.shape[1]), 0)
    out_ref[2 * rank :, :] = jnp.where(index == 0, bias, jnp.where(index == 1, loss_ref[...], 0.0))


def ortho_kernel(rank, left_ref, enc_ref, dec_ref):
    def spread(rows):
        index = lax.broadcasted_iota(jnp.int32, rows.shape, 0)
        for i in range(rank):
            unit = rows[i : i + 1, :]
            unit = unit * lax.rsqrt(jnp.sum(unit * unit, axis=1, keepdims=True))
            along = jnp.sum(rows * unit, axis=1, keepdims=True)
            rows = jnp.where(index == i, unit, jnp.where(index > i, rows - along * unit, rows))
        one, two, three = split_floats(rows)
        return jnp.concatenate([one, one, two, two, one, three], axis=0).astype(bf16)

    enc_ref[...] = spread(left_ref[:rank, :])
    dec_ref[...] = spread(left_ref[rank : 2 * rank, :])


def orthonormal(left, rank):
    shape = jax.ShapeDtypeStruct((6 * rank, left.shape[1]), bf16)
    return pl.pallas_call(
        functools.partial(ortho_kernel, rank), out_shape=(shape, shape), name="orthonormal"
    )(left)


def right_kernel(numbers, rank, left_ref, full_ref, out_ref):
    high, low = high_low(full_ref[...])
    left = left_ref[...]
    by_high, by_low = dot(left, high, numbers), dot(left, low, numbers)
    one, two, three = slice(0, rank), slice(2 * rank, 3 * rank), slice(5 * rank, 6 * rank)
    total = by_high[one] + by_high[two] + by_high[three] + by_low[one] + by_low[two]
    out_ref[...] = total.astype(out_ref.dtype)


def right_part(left, full, by_rows, dtype, *deps):
    latents, width = full.shape if by_rows else full.shape[::-1]
    rank = left.shape[0] // 6
    block = min(1024, latents)
    return call(
        functools.partial(right_kernel, contract_cols if by_rows else contract_plain, rank),
        "right_part",
        (left, full),
        like((rank, latents), dtype),
        (latents // block,),
        [whole_of(left.shape), row_block(block, width) if by_rows else column_block(width, block)],
        column_block(rank, block),
        deps,
        (24 * rank * latents * width, 4 * latents * width),
    )


def stack_kernel(right_ref, bias_ref, out_ref):
    index = lax.broadcasted_iota(jnp.int32, right_ref.shape, 0)
    bias = jnp.where(index == 0, bias_ref[...], 0.0)
    out_ref[...] = jnp.concatenate([right_ref[...], bias], axis=0).astype(bf16)


def pieces_of_right(right):
    one, two, three = split_floats(right)
    return jnp.concatenate([one, two, one, two, three, one], axis=0).astype(bf16)


def enc_final_kernel(rep_count, left_ref, right_ref, full_ref, mom_ref, w_ref, w_out, mom_out, err_out):
    approx = dot(left_ref[...], pieces_of_right(right_ref[:8, :]), contract_rows)
    err_out[...] = full_ref[...] - approx * (1.0 / rep_count)
    mom = momentum_decay * mom_ref[...] + approx
    mom_out[...] = mom
    w_out[...] = w_ref[...] - rate_enc * mom


def dec_final_kernel(rep_count, left_ref, right_ref, full_ref, mom_ref, w_ref, w_out, mom_out, err_out):
    approx = dot(pieces_of_right(right_ref[:8, :]), left_ref[...], contract_rows)
    err_out[...] = full_ref[...] - approx * (1.0 / rep_count)
    mom = momentum_decay * mom_ref[...] + approx
    mom_out[...] = mom
    step = w_ref[...] - rate_dec * mom
    w_out[...] = step * lax.rsqrt(jnp.sum(step * step, axis=1, keepdims=True) + 1e-06)


def final_update(kernel, by_rows, rep_count, left, right, full, mom, weight, *deps):
    latents, width = right.shape[1], left.shape[1]
    block = min(1024, latents)
    big = row_block(block, width) if by_rows else column_block(width, block)
    return call(
        functools.partial(kernel, rep_count),
        "final_update",
        (left, right, full, mom, weight),
        (like(full.shape),) * 3,
        (latents // block,),
        [whole_of(left.shape), column_block(right.shape[0], block), big, big, big],
        (big, big, big),
        deps,
        (2 * 48 * latents * width, 24 * latents * width),
    )


def layer_norm(values, gain_row, shift_row):
    center = values - jnp.mean(values, axis=-1, keepdims=True)
    spread = jnp.mean(center * center, axis=-1, keepdims=True)
    return center * lax.rsqrt(spread + 1e-05) * gain_row + shift_row


def frozen_block(residual, norm_params, biases, qkv, w_out, fc, w_proj):
    seq_len = residual.shape[0]
    model_width = residual.shape[1]
    hidden_units = w_proj.shape[0]
    head_dim = model_width // HEADS
    stream = residual.astype(f32)
    normed = layer_norm(stream, norm_params[0], norm_params[1]).astype(bf16)

    def times(values, parts, bias):
        width = parts[0].shape[1]
        return [
            jnp.dot(values, part, preferred_element_type=f32) + bias[k * width : (k + 1) * width]
            for k, part in enumerate(parts)
        ]

    queries, keys, values = [
        part.astype(bf16).reshape(seq_len, HEADS, head_dim)
        for part in times(normed, qkv, biases[: 3 * model_width])
    ]
    scores = jnp.einsum("qhd,khd->hqk", queries, keys, preferred_element_type=f32) / math.sqrt(head_dim)
    causal = jnp.arange(seq_len)[:, None] >= jnp.arange(seq_len)[None, :]
    scores = jnp.where(causal, scores, -1e30)
    weights = jax.nn.softmax(scores, axis=-1).astype(bf16)
    attended = jnp.einsum("hqk,khd->qhd", weights, values, preferred_element_type=f32)
    attended = attended.astype(bf16).reshape(seq_len, model_width)
    stream = (
        stream
        + jnp.dot(attended, w_out, preferred_element_type=f32)
        + biases[3 * model_width : 4 * model_width]
    )
    normed = layer_norm(stream, norm_params[2], norm_params[3]).astype(bf16)
    inner_in = times(normed, fc, biases[4 * model_width : 4 * model_width + hidden_units])
    activated = jnp.concatenate(
        [jax.nn.gelu(part, approximate=True).astype(bf16) for part in inner_in], axis=1
    )
    return (
        stream
        + jnp.dot(activated, w_proj, preferred_element_type=f32)
        + biases[4 * model_width + hidden_units :]
    )


def per_device(
    residual,
    valid_mask,
    top_idx,
    aux_idx,
    dead_flags,
    norm_params,
    biases,
    w_qkv,
    w_out,
    w_fc,
    w_proj,
    head_table,
    w_enc,
    encoder_bias_vec,
    w_dec,
    decoder_bias_vec,
    mom_enc,
    mom_benc,
    mom_dec,
    mom_bdec,
    q_enc,
    q_dec,
    err_enc,
    err_dec,
):
    rep_count = lax.axis_size("rep")
    lat_index = lax.axis_index("lat")
    model_width = residual.shape[1]
    hidden_units = w_fc.shape[1]
    lat_dev = w_enc.shape[1]
    top_count, aux_count = top_idx.shape[1], aux_idx.shape[1]
    rank = q_enc.shape[1]
    err_enc, err_dec = err_enc[0], err_dec[0]

    joined = lax.all_gather(jnp.concatenate([w_qkv, w_out, w_fc], axis=1), "lat", axis=0, tiled=True)
    proj_all = lax.all_gather(w_proj, "lat", axis=0, tiled=True)
    squares = [joined[:, k : k + model_width] for k in range(0, joined.shape[1], model_width)]

    half = aux_count // 2
    valid_float = valid_mask.astype(f32)
    packed = jnp.concatenate(
        [aux_idx[:, :half] * pack_base + aux_idx[:, half:], top_idx, valid_mask[:, None]], axis=1
    )
    gather = Gather(packed)
    enc_weight = rounded(w_enc, False, packed)
    gather.middle(enc_weight)
    dec_weight = rounded(w_dec, True, enc_weight)
    packed, _ = gather.end(dec_weight)
    picks = packed[:, half : half + top_count]
    ids = jnp.concatenate([packed[:, :half] // pack_base, packed[:, :half] % pack_base, picks], axis=1)
    own_base, partner_base = lat_index * lat_dev, (lat_index ^ 1) * lat_dev
    from_own, from_partner = ids - own_base, ids - partner_base
    ids = jnp.where(
        (from_own >= 0) & (from_own < lat_dev),
        from_own,
        jnp.where((from_partner >= 0) & (from_partner < lat_dev), from_partner + lat_dev, -1),
    )
    padding = -ids.shape[1] % lanes
    ids = jnp.concatenate([ids, jnp.full((ids.shape[0], padding), -1, jnp.int32)], axis=1)
    dead_pair = jnp.concatenate(
        [lax.dynamic_slice_in_dim(dead_flags, base, lat_dev) for base in (own_base, partner_base)]
    ).astype(f32)
    mask_even, mask_partner = build_mask(ids, dead_pair[None, :], aux_count)
    mask_odd = swap(mask_partner, "lat", 1)

    valid_total = jnp.full((1, lanes), jnp.sum(packed[:, half + top_count].astype(f32)))
    valid_total = sum_round(valid_total, "lat", [1])
    for bit in bits_of("rep"):
        valid_total = sum_round(valid_total, "rep", [bit])
    weight_own = (valid_float / valid_total[0, 0])[:, None]

    stream = frozen_block(
        residual, norm_params, biases, squares[:3], squares[3], squares[4:], proj_all
    )

    def final_norm(values):
        return layer_norm(values, norm_params[4], norm_params[5])

    gather = Gather((stream - decoder_bias_vec).astype(bf16))
    orig_normed = final_norm(stream)
    q_enc_rows, q_enc_columns = factor_pieces(q_enc.T, gather.own, valid_total)
    gather.middle(q_enc_rows)
    q_dec_rows, q_dec_columns = factor_pieces(q_dec.T, q_enc_rows)
    centered = gather.end(q_dec_rows)
    orig_blocks = orig_normed.astype(bf16)

    bias_row = encoder_bias_vec[None, :]
    tops_odd, auxes_odd, top_odd = forward(
        centered[1], enc_weight, bias_row, mask_odd, dec_weight
    )
    rebuilt = Scatter(top_odd)
    tops_even, auxes_even, top_even = forward(centered[0], enc_weight, bias_row, mask_even, dec_weight, top_odd)
    sent = rebuilt.chip(top_even)
    aux_part = aux_forward(auxes_odd, auxes_even, dec_weight, sent)
    auxiliary_rebuilt = lax.psum_scatter(aux_part, "lat", scatter_dimension=0, tiled=False)
    sent = rebuilt.hop(aux_part)
    orig_group = gather_behind(orig_blocks, aux_part)
    orig_odd = head_part(orig_group[1], head_table, sent)
    rebuilt_input = rebuilt.last(orig_odd) + decoder_bias_vec
    rec_float, norm_back = jax.vjp(final_norm, rebuilt_input)
    gather = Gather(rec_float.astype(bf16))
    orig_mean = Scatter(orig_odd, lanes)
    orig_even = head_part(orig_group[0], head_table, gather.own)
    gather.middle(orig_even)
    products_dec = factor_products(tops_odd, tops_even, q_dec_columns, orig_even)
    rec_group = gather.end(products_dec[0])
    sent = orig_mean.chip(orig_even, products_dec[0])

    resid_err = stream - rebuilt_input - auxiliary_rebuilt
    aux_pull = -(2.0 * aux_weight) * weight_own * resid_err
    aux_blocks = aux_pull.astype(bf16)

    rec_odd = head_part(rec_group[1], head_table, sent)
    rec_mean = Scatter(rec_odd, lanes)
    sent = orig_mean.hop(rec_odd)
    rec_even = head_part(rec_group[0], head_table, sent, rec_odd)
    sent = rec_mean.chip(rec_even)
    orig_mean = orig_mean.last(rec_even)
    aux_group = gather_behind(aux_blocks, rec_even)

    pre_odd, pre_even = aux_back(aux_group[1], aux_group[0], dec_weight, mask_odd, mask_even, sent)
    sent = rec_mean.hop(pre_odd)
    dec_part, left_dec = part_dec(
        (auxes_odd, auxes_even), (aux_group[1], aux_group[0]), err_dec, q_dec_rows, sent, pre_odd
    )
    rec_mean = rec_mean.last(dec_part)

    orig_lse, rec_lse = orig_mean[:, model_width], rec_mean[:, model_width]
    orig_mean, rec_mean = orig_mean[:, :model_width], rec_mean[:, :model_width]
    (grad_head,) = norm_back(weight_own * (rec_mean - orig_mean))
    grad_recon = (grad_head + aux_pull).astype(bf16)
    gather = Gather(grad_recon)
    gap = orig_normed.astype(bf16).astype(f32) - rec_float.astype(bf16).astype(f32)
    kl_own = jnp.sum(gap * orig_mean, axis=1) - orig_lse + rec_lse
    per_token = kl_own + aux_weight * jnp.sum(resid_err * resid_err, axis=1)
    loss_row = jnp.full((1, model_width), jnp.sum(valid_float * per_token))
    left_enc = err_left(q_enc_rows, err_enc, grad_recon)
    gather.middle(left_enc)
    recon_group = gather.end()

    pre_odd, pre_even, grad_benc, bias_pull, enc_odd, enc_even = back_pass(
        recon_group[1], recon_group[0], dec_weight, enc_weight, mask_odd, mask_even, pre_odd, pre_even, q_enc_columns
    )
    small = call(
        functools.partial(left_sums_kernel, rank),
        "left_sums",
        (
            enc_odd,
            enc_even,
            centered[1],
            centered[0],
            *products_dec,
            recon_group[1],
            recon_group[0],
            left_enc,
            left_dec,
            grad_recon,
            bias_pull,
            loss_row,
        ),
        like((2 * rank + 8, model_width)),
    )
    codes, grads = (tops_odd, tops_even), (recon_group[1], recon_group[0])
    full_dec = add_dec(codes, grads, dec_part, 0, 2, small)
    small = sum_round(small, "lat", [1])
    full_dec = add_dec(codes, grads, full_dec, 1, 2, small)
    small = sum_round(small, "lat", bits_of("lat")[1:])
    full_enc = form_enc((centered[1], centered[0]), (pre_odd, pre_even), err_enc, small, full_dec)
    small = sum_round(small, "rep", bits_of("rep"))
    grad_bdec, loss_sum = small[2 * rank], small[2 * rank + 1, 0]

    ortho_enc, ortho_dec = orthonormal(small[: 2 * rank], rank)
    right_enc = right_part(ortho_enc, full_enc, False, bf16)
    right_dec = right_part(ortho_dec, full_dec, True, f32, right_enc)
    right_enc = sum_round(right_enc, "rep", bits_of("rep"), sent_as=bf16)
    right_dec = call(
        stack_kernel, "stack", (right_dec, grad_benc), like((2 * rank, lat_dev), bf16), deps=(right_enc,)
    )
    right_dec = sum_round(right_dec, "rep", bits_of("rep"), sent_as=bf16)
    grad_benc = right_dec[rank]

    w_enc_new, mom_enc_new, err_enc_new = final_update(
        enc_final_kernel, False, rep_count, ortho_enc, right_enc, full_enc, mom_enc, w_enc
    )
    w_dec_new, mom_dec_new, err_dec_new = final_update(
        dec_final_kernel, True, rep_count, ortho_dec, right_dec, full_dec, mom_dec, w_dec, w_enc_new
    )
    mom_benc_new = momentum_decay * mom_benc + grad_benc
    mom_bdec_new = momentum_decay * mom_bdec + grad_bdec
    b_enc_new = encoder_bias_vec - rate_benc * mom_benc_new
    b_dec_new = decoder_bias_vec - rate_bdec * mom_bdec_new
    return (
        loss_sum,
        valid_total[0, 0],
        w_enc_new,
        b_enc_new,
        w_dec_new,
        b_dec_new,
        mom_enc_new,
        mom_benc_new,
        mom_dec_new,
        mom_bdec_new,
        right_enc.T,
        right_dec[:rank].T,
        err_enc_new[None],
        err_dec_new[None],
    )


def solution(mesh):
    in_specs = (
        P(("rep", "lat"), None),
        P(("rep", "lat")),
        P(("rep", "lat"), None),
        P(("rep", "lat"), None),
        P(),
        P(),
        P(),
        P("lat", None),
        P("lat", None),
        P("lat", None),
        P("lat", None),
        P("lat", None),
        P(None, "lat"),
        P("lat"),
        P("lat", None),
        P(),
        P(None, "lat"),
        P("lat"),
        P("lat", None),
        P(),
        P("lat", None),
        P("lat", None),
        P("rep", None, "lat"),
        P("rep", "lat", None),
    )
    out_specs = (
        P(),
        P(),
        P(None, "lat"),
        P("lat"),
        P("lat", None),
        P(),
        P(None, "lat"),
        P("lat"),
        P("lat", None),
        P(),
        P("lat", None),
        P("lat", None),
        P("rep", None, "lat"),
        P("rep", "lat", None),
    )
    return jax.shard_map(
        per_device, mesh=mesh, in_specs=in_specs, out_specs=out_specs, check_vma=False
    )
```

```python
import functools
import math

import jax
import jax.numpy as jnp
from jax import lax
from jax.experimental import pallas as pl
from jax.experimental.pallas import tpu as pltpu
from jax.sharding import PartitionSpec as P

HEADS = 12
HEAD_PARTS = (3, 13)

pack_base = 32768
aux_weight = 1.0 / 32.0
momentum_decay = 0.9
rate_enc = 3000.0
rate_dec = 3000.0
rate_benc = 10000.0
rate_bdec = 500.0
lanes = 128
vmem_most = 60 * 2**20
contract_cols = (((1,), (1,)), ((), ()))
contract_rows = (((0,), (0,)), ((), ()))
contract_plain = (((1,), (0,)), ((), ()))
f32 = jnp.float32
bf16 = jnp.bfloat16


def swap(values, axis, bit):
    count = lax.axis_size(axis)
    return lax.ppermute(values, axis, [(i, i ^ bit) for i in range(count)])


def bits_of(axis):
    count = lax.axis_size(axis)
    return [1 << k for k in range(count.bit_length() - 1)]


def even_order():
    count = lax.axis_size("lat")
    return [2, 6, 4, 0] if count == 8 else list(range(count - 2, -1, -2))


def gather_even(own):
    if lax.axis_size("lat") == 8:
        half = own.shape[0] // 2
        by_two, by_four = swap(own, "lat", 2), swap(own, "lat", 4)
        return jnp.concatenate(
            [by_two, swap(by_four[:half], "lat", 2), swap(by_two[half:], "lat", 4), by_four, own], axis=0
        )
    blocks = {0: own}
    for bit in bits_of("lat")[1:]:
        order = sorted(blocks)
        moved = swap(jnp.stack([blocks[j] for j in order]), "lat", bit)
        for at, j in enumerate(order):
            blocks[j ^ bit] = moved[at]
    return jnp.concatenate([blocks[j] for j in even_order()], axis=0)


def gather_tokens(own):
    even = gather_even(own)
    return even, swap(even, "lat", 1)


def scatter_paths():
    others = bits_of("lat")[1:]
    if len(others) == 2:
        return [(0, 2, others), (1, 2, others[::-1])]
    return [(0, 1, others)]


def take_blocks(values, part, parts):
    rows, width = values.shape[0] // len(even_order()), values.shape[1] // parts
    return {
        j: values[at * rows : (at + 1) * rows, part * width : (part + 1) * width]
        for at, j in enumerate(even_order())
    }


def scatter_sum(even, odd_moved):
    chip = even + odd_moved
    done = []
    for part, parts, order in scatter_paths():
        held = take_blocks(chip, part, parts)
        for bit in order:
            sent = [j for j in even_order() if j in held and j & bit]
            got = swap(jnp.concatenate([held[j] for j in sent], axis=0).astype(bf16), "lat", bit)
            rows = held[0].shape[0]
            for at, j in enumerate(sent):
                held[j ^ bit] = held[j ^ bit] + got[at * rows : (at + 1) * rows].astype(f32)
                del held[j]
        done.append(held[0])
    return jnp.concatenate(done, axis=1)


def merge(mean_a, lse_a, mean_b, lse_b):
    top = jnp.maximum(lse_a, lse_b)
    exp_a, exp_b = jnp.exp(lse_a - top), jnp.exp(lse_b - top)
    total = exp_a + exp_b
    mixed = mean_a.astype(f32) * (exp_a / total) + mean_b.astype(f32) * (exp_b / total)
    return mixed, top + jnp.log(total)


def scatter_mean(even, even_lse, odd_moved, odd_lse_moved):
    chip, chip_lse = merge(even, even_lse, odd_moved, odd_lse_moved)
    done = []
    for part, parts, order in scatter_paths():
        means, lses = take_blocks(chip, part, parts), take_blocks(chip_lse, 0, 1)
        held = {j: (means[j], lses[j]) for j in means}
        for bit in order:
            sent = [j for j in even_order() if j in held and j & bit]
            rows = held[0][0].shape[0]
            got = swap(jnp.concatenate([held[j][0] for j in sent], axis=0).astype(bf16), "lat", bit)
            got_lse = swap(jnp.concatenate([held[j][1] for j in sent], axis=0), "lat", bit)
            for at, j in enumerate(sent):
                span = slice(at * rows, (at + 1) * rows)
                held[j ^ bit] = merge(*held[j ^ bit], got[span], got_lse[span])
                del held[j]
        done.append(held[0])
    return jnp.concatenate([mean for mean, _ in done], axis=1), done[0][1]


def sum_round(values, axis, bits, sent_as=None):
    if sent_as is not None:
        values = values.astype(sent_as)
    if len(bits) == 2:
        one, two, both = (swap(values, axis, bit) for bit in (bits[0], bits[1], bits[0] | bits[1]))
        return (values.astype(f32) + one.astype(f32)) + (two.astype(f32) + both.astype(f32))
    for bit in bits:
        values = values.astype(f32) + swap(values, axis, bit).astype(f32)
    return values


untouched = pl.BlockSpec(memory_space=pl.ANY)
in_vmem = pl.BlockSpec(memory_space=pltpu.VMEM)


def dot(a, b, numbers):
    return lax.dot_general(a, b, numbers, preferred_element_type=f32)


def call(kernel, name, args, out_shape, grid=(), in_specs=None, out_specs=None, deps=(), cost=(0, 0), aliases=None, scratch=()):
    count, skipped = len(args), len(deps)

    def body(*refs):
        kernel(*refs[:count], *refs[count + skipped :])

    if in_specs is None:
        in_specs = [in_vmem] * count
        out_specs = jax.tree.map(lambda _: in_vmem, out_shape)
    flops, moved = cost
    return pl.pallas_call(
        body,
        out_shape=out_shape,
        grid=grid,
        in_specs=list(in_specs) + [untouched] * skipped,
        out_specs=out_specs,
        scratch_shapes=list(scratch),
        input_output_aliases=aliases or {},
        compiler_params=pltpu.CompilerParams(vmem_limit_bytes=vmem_most),
        cost_estimate=pl.CostEstimate(flops=flops, bytes_accessed=moved, transcendentals=0),
        name=name,
    )(*args, *deps)


def like(shape, dtype=f32):
    return jax.ShapeDtypeStruct(shape, dtype)


def clear_at_start(*refs):
    @pl.when(pl.program_id(0) == 0)
    def _():
        for ref in refs:
            ref[...] = jnp.zeros_like(ref)


def mask_kernel(tokens, hi_count, aux_count, top_count, *refs):
    packed = refs[0][...]
    dead_ref, own_ref, partner_ref, valid_ref, ids_ref, top_ref, scratch = refs[1], *refs[-6:]
    me, lat_dev = lax.axis_index("lat"), hi_count * lanes
    half, rows = aux_count // 2, 2 * hi_count

    def placed(ids):
        from_own, from_partner = ids - me * lat_dev, ids - (me ^ 1) * lat_dev
        return jnp.where(
            (from_own >= 0) & (from_own < lat_dev),
            from_own,
            jnp.where((from_partner >= 0) & (from_partner < lat_dev), from_partner + lat_dev, -(2**20)),
        )

    ids_ref[:, :half] = placed(packed[:, :half] >> 15)
    ids_ref[:, half:] = placed(packed[:, :half] & (pack_base - 1))
    joint_count = lanes // top_count
    tops = packed[:, half:]
    lane = lax.broadcasted_iota(jnp.int32, tops.shape, 1)
    repeated = tops
    for k in range(1, joint_count):
        repeated = jnp.where(lane // top_count == k, pltpu.roll(tops, k * top_count, 1), repeated)
    top_ref[...] = placed(repeated) + (lane // top_count) * (rows * lanes)
    counted = jnp.where(lane == top_count, -1 - tops, 0).astype(f32)
    valid = jnp.sum(jnp.sum(counted, axis=0, keepdims=True), axis=1, keepdims=True)
    clear_at_start(valid_ref)
    valid_ref[...] += jnp.broadcast_to(valid, valid_ref.shape)

    def hot(count, width, index):
        return jnp.where(lax.broadcasted_iota(jnp.int32, (count, width), 0) == index, 1.0, 0.0).astype(bf16)

    def some_tokens(group, carry):
        base = group * joint_count
        for k in range(joint_count):
            row = ids_ref[pl.ds(base + k, 1), :]
            picked = dot(hot(rows, aux_count, row >> 7), hot(lanes, aux_count, row & 127), contract_cols)
            scratch[pl.ds(pl.multiple_of((base + k) * rows, rows), rows), :] = 2.0 * picked
        joint_row = top_ref[pl.ds(base, 1), :]
        for k in range(1, joint_count):
            joint_row = jnp.where(lane[:1] // top_count == k, top_ref[pl.ds(base + k, 1), :], joint_row)
        picked = dot(hot(joint_count * rows, lanes, joint_row >> 7), hot(lanes, lanes, joint_row & 127), contract_cols)
        scratch[pl.ds(pl.multiple_of(base * rows, rows), joint_count * rows), :] += picked
        return carry

    lax.fori_loop(0, tokens // joint_count, some_tokens, 0, unroll=4)
    for hi in range(2 * hi_count):
        code = scratch[pl.ds(hi, tokens, stride=2 * hi_count), :]
        aux = jnp.where(code >= 2.0, 2.0, 0.0)
        code = (code - aux + aux * dead_ref[:, hi * lanes : (hi + 1) * lanes]).astype(bf16)
        if hi < hi_count:
            own_ref[:, hi * lanes : (hi + 1) * lanes] = code
        else:
            partner_ref[:, (hi - hi_count) * lanes : (hi - hi_count + 1) * lanes] = code


def build_mask(packed, dead_pair, aux_count, top_count, rows, first, so_far=(), deps=()):
    width = packed.shape[1]
    lat_dev = dead_pair.shape[1] // 2
    hi_count, tokens = lat_dev // lanes, 64
    steps = packed.shape[0] // tokens
    out_block = pl.BlockSpec((tokens, lat_dev), lambda i: (i + first // tokens, 0))
    *masks, valid = call(
        functools.partial(mask_kernel, tokens, hi_count, aux_count, top_count),
        "build_mask",
        (packed, dead_pair, *so_far),
        (like((rows, lat_dev), bf16), like((rows, lat_dev), bf16), like((1, lanes))),
        (steps,),
        [row_block(tokens, width), whole_of((1, 2 * lat_dev))] + [untouched] * len(so_far),
        (out_block, out_block, whole_of((1, lanes))),
        deps,
        (16 * steps * tokens * 2 * lat_dev * aux_count, 4 * steps * tokens * lat_dev),
        aliases={2 + k: k for k in range(len(so_far))},
        scratch=[
            pltpu.VMEM((tokens, aux_count), jnp.int32),
            pltpu.VMEM((tokens, lanes), jnp.int32),
            pltpu.VMEM((tokens * 2 * hi_count, lanes), f32),
        ],
    )
    return masks, valid


def pass_kernel(in_ref, out_ref):
    pass


def pass_after(value, *deps):
    return call(
        pass_kernel, "pass_after", (value,), like(value.shape, value.dtype), (), [untouched], untouched, deps, aliases={0: 0}
    )


def split_three(values):
    first = values.astype(bf16)
    rest = values - first.astype(f32)
    second = rest.astype(bf16)
    return first, second, (rest - second.astype(f32)).astype(bf16)


def split_floats(values):
    return [piece.astype(f32) for piece in split_three(values)]


def residual_kernel(weight, stream_ref, rebuilt_ref, aux_ref, weight_ref, pull_ref, rounded_ref, square_ref):
    err = stream_ref[...] - rebuilt_ref[...] - aux_ref[...]
    pull = -(2.0 * weight) * weight_ref[...] * err
    pull_ref[...] = pull
    rounded_ref[...] = pull.astype(bf16)
    square_ref[...] = jnp.sum(err * err, axis=1, keepdims=True)


def residual_pull(stream, rebuilt, aux, weight_own, *deps):
    shape = stream.shape
    return call(
        functools.partial(residual_kernel, aux_weight),
        "residual_pull",
        (stream, rebuilt, aux, weight_own),
        (like(shape), like(shape, bf16), like((shape[0], 1))),
        deps=deps,
    )


def high_low(values):
    high = values.astype(bf16)
    return high, (values - high.astype(f32)).astype(bf16)


def assemble_kernel(*refs):
    *blocks, even_ref = refs
    rows = blocks[0].shape[0]
    for at, block in enumerate(blocks):
        even_ref[at * rows : (at + 1) * rows, :] = block[...]


class Gather:
    def __init__(self, own):
        self.own, self.plain = own, lax.axis_size("lat") != 8
        if not self.plain:
            self.blocks = [swap(own, "lat", j) if j else own for j in even_order()]

    def end(self, *deps):
        if self.plain:
            return gather_tokens(self.own)
        rows, width = self.own.shape
        even = call(assemble_kernel, "assemble", self.blocks, like((4 * rows, width), self.own.dtype), deps=deps)
        return even, swap(even, "lat", 1)


def reorder_kernel(blocks_ref, even_ref, odd_ref):
    me, rows = lax.axis_index("lat"), blocks_ref.shape[1]
    for at, j in enumerate(even_order()):
        even_ref[at * rows : (at + 1) * rows, :] = blocks_ref[me ^ j]
        odd_ref[at * rows : (at + 1) * rows, :] = blocks_ref[me ^ (j ^ 1)]


def gather_behind(own, *deps):
    blocks = lax.all_gather(own, "lat", axis=0)
    count, rows, width = blocks.shape
    half = like((count // 2 * rows, width), own.dtype)
    return call(reorder_kernel, "reorder", (blocks,), (half, half), deps=deps)


def joint(parts, tail):
    if not tail:
        return sum(parts[1:], parts[0])
    lses = [part[:, -tail:] for part in parts]
    top = functools.reduce(jnp.maximum, lses)
    weights = [jnp.exp(lse - top) for lse in lses]
    total = sum(weights[1:], weights[0])
    means = [part[:, :-tail] * (weight / total)[:, :1] for part, weight in zip(parts, weights)]
    return jnp.concatenate([sum(means[1:], means[0]), top + jnp.log(total)], axis=1)


def to_send(values, tail):
    if not tail:
        return values.astype(bf16)
    lane = lax.broadcasted_iota(jnp.int32, (values.shape[0], tail), 1)
    one, two, three = split_floats(values[:, -tail:])
    logs = jnp.where(lane < 32, one, jnp.where(lane < 64, two, three))
    return jnp.concatenate([values[:, :-tail], logs], axis=1).astype(bf16)


def received(ref, tail):
    values = ref[...].astype(f32)
    if not tail:
        return values
    logs = values[:, -tail:]
    lse = logs[:, :1] + logs[:, 32:33] + logs[:, 64:65]
    return jnp.concatenate([values[:, :-tail], jnp.broadcast_to(lse, logs.shape)], axis=1)


def chip_kernel(tail, even_ref, odd_ref, *outs):
    rows = outs[0].shape[0]
    for at, out in enumerate(outs):
        span = slice(at * rows, (at + 1) * rows)
        total = joint([even_ref[span, :], odd_ref[span, :]], tail)
        out[...] = total if at == len(outs) - 1 else to_send(total, tail)


def last_kernel(tail, *refs):
    *got, keep, total_ref = refs
    total_ref[...] = joint([keep[...]] + [received(ref, tail) for ref in got], tail)


class Scatter:
    def __init__(self, odd, tail=0):
        self.moved, self.tail, self.plain = swap(odd, "lat", 1), tail, lax.axis_size("lat") != 8

    def chip(self, even, *deps):
        self.even = even
        if self.plain:
            return even
        rows, width = even.shape[0] // 4, even.shape[1]
        shapes = [like((rows, width), bf16)] * 3 + [like((rows, width))]
        *sends, keep = call(
            functools.partial(chip_kernel, self.tail), "chip_sum", (even, self.moved), shapes, deps=deps
        )
        self.pending = [swap(send, "lat", j) for send, j in zip(sends, even_order())] + [keep]
        return keep

    def last(self, *deps):
        if self.plain:
            if not self.tail:
                return scatter_sum(self.even, self.moved)
            width = self.even.shape[1] - self.tail
            mean, lse = scatter_mean(
                self.even[:, :width], self.even[:, width : width + 1], self.moved[:, :width], self.moved[:, width : width + 1]
            )
            return jnp.concatenate([mean, jnp.broadcast_to(lse, (lse.shape[0], self.tail))], axis=1)
        return call(
            functools.partial(last_kernel, self.tail), "last_sum", self.pending, like(self.pending[-1].shape), deps=deps
        )


def head_kernel(cuts, steps, normed_ref, table_hbm, out_ref, table_ref, sems):
    def piece(c):
        span = pl.ds(cuts[c], cuts[c + 1] - cuts[c])
        return pltpu.make_async_copy(table_hbm.at[span, :], table_ref.at[span, :], sems.at[c])

    def at_start(action):
        if steps == 1:
            action()
        else:
            pl.when(pl.program_id(0) == 0)(action)

    chunks = len(cuts) - 1
    at_start(lambda: [piece(c).start() for c in range(chunks)] and None)
    normed = normed_ref[...]

    def logits_of(c):
        at_start(lambda: piece(c).wait())
        return dot(normed, table_ref[cuts[c] : cuts[c + 1], :], contract_cols)

    def fold(values, op):
        folded = values[:, :lanes]
        for k in range(lanes, values.shape[1], lanes):
            folded = op(folded, values[:, k : k + lanes])
        return folded

    top = total = mean = None
    logits = logits_of(0)
    for c in range(chunks):
        later = logits_of(c + 1) if c + 1 < chunks else None
        chunk_top = jnp.max(fold(logits, jnp.maximum), axis=1, keepdims=True)
        new_top = chunk_top if top is None else jnp.maximum(top, chunk_top)
        grown = jnp.exp(logits - new_top).astype(bf16)
        chunk_total = fold(grown.astype(f32), jnp.add)
        chunk_mean = dot(grown, table_ref[cuts[c] : cuts[c + 1], :], contract_plain)
        if top is None:
            total, mean = chunk_total, chunk_mean
        else:
            shrink = jnp.exp(top - new_top)
            total, mean = total * shrink + chunk_total, mean * shrink + chunk_mean
        top, logits = new_top, later
    total = jnp.sum(total, axis=1, keepdims=True)
    width = mean.shape[1]
    out_ref[:, :width] = mean / total
    out_ref[:, width:] = jnp.broadcast_to(top + jnp.log(total), (mean.shape[0], lanes))


def head_cuts(entries):
    unit = 256 if entries % 256 == 0 else lanes
    tiles = entries // unit
    ends = sorted({max(1, tiles * part // 26) for part in HEAD_PARTS} | {tiles})
    return [0] + [unit * end for end in ends]


def head_part(normed, table, *deps):
    rows, width = normed.shape
    entries = table.shape[0]
    block = min(512, rows)
    cuts = head_cuts(entries)
    return call(
        functools.partial(head_kernel, cuts, rows // block),
        "head_part",
        (normed, table),
        like((rows, width + lanes)),
        (rows // block,),
        [pl.BlockSpec((block, width), lambda i: (i, 0)), untouched],
        pl.BlockSpec((block, width + lanes), lambda i: (i, 0)),
        deps,
        (6 * rows * entries * width, 2 * entries * width),
        scratch=[pltpu.VMEM(table.shape, bf16), pltpu.SemaphoreType.DMA((len(cuts) - 1,))],
    )


def round_kernel(values_ref, out_ref):
    out_ref[...] = values_ref[...].astype(bf16)


def rounded(values, by_rows, *deps):
    latents = values.shape[0 if by_rows else 1]
    block = min(1024, latents)
    spec = row_block(block, values.shape[1]) if by_rows else column_block(values.shape[0], block)
    return call(
        round_kernel,
        "rounded",
        (values,),
        like(values.shape, bf16),
        (latents // block,),
        [spec],
        spec,
        deps,
        (0, 6 * values.size),
    )


def pieces_kernel(factor_ref, rows_ref, columns_ref):
    one, two, three = split_floats(factor_ref[...])
    rank, latents = one.shape
    rows_ref[...] = jnp.concatenate([one, two, three, jnp.zeros_like(one)], axis=0).astype(bf16)
    tall = jnp.concatenate([one, two, three, jnp.zeros((lanes - 3 * rank, latents), f32)], axis=0)
    columns_ref[...] = tall.T.astype(bf16)


def factor_pieces(factor, *deps):
    rank, latents = factor.shape
    block = min(1024, latents)
    return call(
        pieces_kernel,
        "factor_pieces",
        (factor,),
        (like((4 * rank, latents), bf16), like((latents, lanes), bf16)),
        (latents // block,),
        [column_block(rank, block)],
        (column_block(4 * rank, block), row_block(block, lanes)),
        deps,
        (0, 1024 * latents),
    )


def column_block(rows, block):
    return pl.BlockSpec((rows, block), lambda i: (0, i))


def row_block(block, width):
    return pl.BlockSpec((block, width), lambda i: (i, 0))


def whole_of(shape):
    return pl.BlockSpec(shape, lambda i: (0,) * len(shape))


def forward_kernel(inputs_ref, enc_ref, bias_ref, mask_ref, dec_ref, tops_ref, auxes_ref, part_ref):
    clear_at_start(part_ref)
    code = (dot(inputs_ref[...], enc_ref[...], contract_plain) + bias_ref[...]).astype(bf16)
    mask = mask_ref[...]
    nothing = jnp.zeros((), bf16)
    tops = jnp.where((mask == 1.0) | (mask == 3.0), code, nothing)
    tops_ref[...] = tops
    auxes_ref[...] = jnp.where(mask >= 2.0, code, nothing)
    part_ref[...] += dot(tops, dec_ref[...], contract_plain)


def forward(inputs, enc, bias, mask, dec, *deps):
    rows, width = inputs.shape
    latents = enc.shape[1]
    block = min(1024, latents)
    column = column_block(rows, block)
    return call(
        forward_kernel,
        "forward",
        (inputs, enc, bias, mask, dec),
        (like((rows, latents), bf16), like((rows, latents), bf16), like((rows, width))),
        (latents // block,),
        [whole_of((rows, width)), column_block(width, block), column_block(1, block), column, row_block(block, width)],
        (column, column, whole_of((rows, width))),
        deps,
        (4 * rows * latents * width, 2 * latents * (2 * width + 3 * rows)),
    )


def aux_forward_kernel(odd_ref, even_ref, dec_ref, out_ref, odd_sum, even_sum):
    clear_at_start(odd_sum, even_sum)
    odd_sum[...] += dot(odd_ref[...], dec_ref[...], contract_plain)
    even_sum[...] += dot(even_ref[...], dec_ref[...], contract_plain)

    @pl.when(pl.program_id(0) == pl.num_programs(0) - 1)
    def _():
        me, rows = lax.axis_index("lat"), out_ref.shape[1]
        for at, j in enumerate(even_order()):
            out_ref[me ^ j] = even_sum[at * rows : (at + 1) * rows, :]
            out_ref[me ^ (j ^ 1)] = odd_sum[at * rows : (at + 1) * rows, :]


def aux_forward(odd, even, dec, *deps):
    latents, width = dec.shape
    rows, count = odd.shape[0], lax.axis_size("lat")
    block = min(1024, latents)
    column, shape = column_block(rows, block), (count, 2 * rows // count, width)
    return call(
        aux_forward_kernel,
        "aux_forward",
        (odd, even, dec),
        like(shape),
        (latents // block,),
        [column, column, row_block(block, width)],
        whole_of(shape),
        deps,
        (4 * rows * latents * width, 2 * latents * (width + 2 * rows)),
        scratch=[pltpu.VMEM((rows, width), f32)] * 2,
    )


def aux_back_kernel(odd_ref, even_ref, dec_ref, odd_mask, even_mask, odd_out, even_out):
    dec = dec_ref[...]
    for grads, mask, out in ((odd_ref, odd_mask, odd_out), (even_ref, even_mask, even_out)):
        pulled = dot(grads[...], dec, contract_cols).astype(bf16)
        out[...] = jnp.where(mask[...] >= 2.0, pulled, jnp.zeros((), bf16))


def aux_back(odd, even, dec, odd_mask, even_mask, *deps):
    latents, width = dec.shape
    rows = odd.shape[0]
    block = min(1024, latents)
    column, whole = column_block(rows, block), whole_of((rows, width))
    return call(
        aux_back_kernel,
        "aux_back",
        (odd, even, dec, odd_mask, even_mask),
        (like((rows, latents), bf16),) * 2,
        (latents // block,),
        [whole, whole, row_block(block, width), column, column],
        (column, column),
        deps,
        (4 * rows * latents * width, 2 * latents * (width + 4 * rows)),
    )


def product_kernel(odd_ref, even_ref, factor_ref, odd_out, even_out):
    clear_at_start(odd_out, even_out)
    odd_out[...] += dot(odd_ref[...], factor_ref[...], contract_plain)
    even_out[...] += dot(even_ref[...], factor_ref[...], contract_plain)


def factor_products(odd, even, factor, *deps):
    rows, latents = odd.shape
    block = min(1024, latents)
    column, out = column_block(rows, block), whole_of((rows, lanes))
    return call(
        product_kernel,
        "factor_products",
        (odd, even, factor),
        (like((rows, lanes)),) * 2,
        (latents // block,),
        [column, column, row_block(block, lanes)],
        (out, out),
        deps,
        (4 * rows * latents * lanes, 4 * latents * rows),
    )


def add_left(ref, pieces, values, numbers):
    high, low = high_low(values)
    by_high, by_low = dot(pieces, high, numbers), dot(pieces, low, numbers)
    ref[...] += (by_high[:8] + by_high[8:16] + by_high[16:24]) + (by_low[:8] + by_low[8:16])


def err_left_kernel(pieces_ref, err_ref, out_ref):
    clear_at_start(out_ref)
    add_left(out_ref, pieces_ref[...], err_ref[...], contract_cols)


def err_left(pieces, err, *deps):
    width, latents = err.shape
    block = min(1024, latents)
    return call(
        err_left_kernel,
        "err_left",
        (pieces, err),
        like((8, width)),
        (latents // block,),
        [column_block(32, block), column_block(width, block)],
        whole_of((8, width)),
        deps,
        (128 * latents * width, 4 * latents * width),
    )


def part_dec_kernel(odd_codes, even_codes, odd_grads, even_grads, err_ref, pieces_ref, part_ref, left_ref):
    total = err_ref[...] + dot(odd_codes[...], odd_grads[...], contract_rows)
    total = total + dot(even_codes[...], even_grads[...], contract_rows)
    part_ref[...] = total
    clear_at_start(left_ref)
    add_left(left_ref, pieces_ref[...], total, contract_plain)


def part_dec(codes, grads, err, pieces, *deps):
    latents, width = err.shape
    rows = codes[0].shape[0]
    block = min(1024, latents)
    column, whole, big = column_block(rows, block), whole_of((rows, width)), row_block(block, width)
    return call(
        part_dec_kernel,
        "part_dec",
        (*codes, *grads, err, pieces),
        (like((latents, width)), like((8, width))),
        (latents // block,),
        [column, column, whole, whole, big, column_block(32, block)],
        (big, whole_of((8, width))),
        deps,
        (4 * rows * latents * width, latents * (8 * width + 4 * rows)),
    )


def add_dec_kernel(odd_codes, even_codes, odd_grads, even_grads, base_ref, out_ref):
    total = base_ref[...] + dot(odd_codes[...], odd_grads[...], contract_rows)
    out_ref[...] = total + dot(even_codes[...], even_grads[...], contract_rows)


def add_dec(codes, grads, base, part, parts, *deps):
    latents, width = base.shape
    rows = codes[0].shape[0]
    block = min(1024, latents // parts)
    steps = latents // parts // block
    column = pl.BlockSpec((rows, block), lambda i: (0, i + part * steps))
    big = pl.BlockSpec((block, width), lambda i: (i + part * steps, 0))
    whole = whole_of((rows, width))
    return call(
        add_dec_kernel,
        "add_dec",
        (*codes, *grads, base),
        like((latents, width)),
        (steps,),
        [column, column, whole, whole, big],
        big,
        deps,
        (4 * rows * latents * width // parts, latents * (8 * width + 4 * rows) // parts),
        aliases={4: 0},
    )


def form_enc_kernel(odd_inputs, even_inputs, odd_grads, even_grads, err_ref, out_ref):
    total = err_ref[...] + dot(odd_inputs[...], odd_grads[...], contract_rows)
    out_ref[...] = total + dot(even_inputs[...], even_grads[...], contract_rows)


def form_enc(inputs, grads, err, *deps):
    width, latents = err.shape
    rows = grads[0].shape[0]
    block = min(1024, latents)
    column, whole, big = column_block(rows, block), whole_of((rows, width)), column_block(width, block)
    return call(
        form_enc_kernel,
        "form_enc",
        (*inputs, *grads, err),
        like((width, latents)),
        (latents // block,),
        [whole, whole, column, column, big],
        big,
        deps,
        (4 * rows * latents * width, latents * (8 * width + 4 * rows)),
    )


def back_kernel(odd_ref, even_ref, dec_ref, enc_ref, odd_mask, even_mask, odd_aux, even_aux, factor_ref, *outs):
    odd_out, even_out, bias_ref, pull_ref, odd_sums, even_sums = outs
    dec, factor = dec_ref[...], factor_ref[...]
    clear_at_start(pull_ref, odd_sums, even_sums)
    nothing = jnp.zeros((), bf16)
    bias = None
    for grads, mask, aux, out, sums in (
        (odd_ref, odd_mask, odd_aux, odd_out, odd_sums),
        (even_ref, even_mask, even_aux, even_out, even_sums),
    ):
        pulled = dot(grads[...], dec, contract_cols).astype(bf16)
        mask = mask[...]
        total = jnp.where((mask == 1.0) | (mask == 3.0), pulled, nothing).astype(f32) + aux[...].astype(f32)
        column = jnp.sum(total, axis=0, keepdims=True)
        bias = column if bias is None else bias + column
        rounded = total.astype(bf16)
        out[...] = rounded
        sums[...] += dot(rounded, factor, contract_plain)
    bias_ref[...] = bias
    one, two, three = split_floats(bias)
    pieces = jnp.concatenate([one, two, three, jnp.zeros((13, bias.shape[1]), f32)], axis=0).astype(bf16)
    pull_ref[...] += dot(pieces, enc_ref[...], contract_cols)


def back_pass(odd, even, dec, enc, odd_mask, even_mask, odd_aux, even_aux, factor, *deps):
    latents, width = dec.shape
    rows = odd.shape[0]
    block = min(1024, latents)
    column, whole = column_block(rows, block), whole_of((rows, width))
    return call(
        back_kernel,
        "back_pass",
        (odd, even, dec, enc, odd_mask, even_mask, odd_aux, even_aux, factor),
        (
            like((rows, latents), bf16),
            like((rows, latents), bf16),
            like((1, latents)),
            like((16, width)),
            like((rows, lanes)),
            like((rows, lanes)),
        ),
        (latents // block,),
        [whole, whole, row_block(block, width), column_block(width, block)]
        + [column] * 4
        + [row_block(block, lanes)],
        (
            column,
            column,
            column_block(1, block),
            whole_of((16, width)),
            whole_of((rows, lanes)),
            whole_of((rows, lanes)),
        ),
        deps,
        (4 * rows * latents * (width + lanes), 2 * latents * (2 * width + 6 * rows)),
    )


def left_sums_kernel(
    rank,
    enc_odd,
    enc_even,
    odd_inputs,
    even_inputs,
    dec_odd,
    dec_even,
    odd_grads,
    even_grads,
    enc_base,
    dec_base,
    own_grads,
    pull_ref,
    loss_ref,
    out_ref,
):
    def against(products, inputs):
        total = None
        for piece in split_three(products[...]):
            wide = dot(piece, inputs[...], contract_rows)
            total = wide if total is None else total + wide
        return total[:rank] + total[rank : 2 * rank] + total[2 * rank : 3 * rank]

    out_ref[:rank, :] = enc_base[...] + against(enc_odd, odd_inputs) + against(enc_even, even_inputs)
    out_ref[rank : 2 * rank, :] = dec_base[...] + against(dec_odd, odd_grads) + against(dec_even, even_grads)
    bias = jnp.sum(own_grads[...].astype(f32), axis=0, keepdims=True)
    bias = bias - jnp.sum(pull_ref[...], axis=0, keepdims=True)
    index = lax.broadcasted_iota(jnp.int32, (8, bias.shape[1]), 0)
    out_ref[2 * rank :, :] = jnp.where(index == 0, bias, jnp.where(index == 1, jnp.sum(loss_ref[...], axis=1, keepdims=True), 0.0))


def ortho_kernel(rank, left_ref, enc_ref, dec_ref):
    def spread(rows):
        index = lax.broadcasted_iota(jnp.int32, rows.shape, 0)
        for i in range(rank):
            unit = rows[i : i + 1, :]
            unit = unit * lax.rsqrt(jnp.sum(unit * unit, axis=1, keepdims=True))
            along = jnp.sum(rows * unit, axis=1, keepdims=True)
            rows = jnp.where(index == i, unit, jnp.where(index > i, rows - along * unit, rows))
        one, two, three = split_floats(rows)
        return jnp.concatenate([one, one, two, two, one, three], axis=0).astype(bf16)

    enc_ref[...] = spread(left_ref[:rank, :])
    dec_ref[...] = spread(left_ref[rank : 2 * rank, :])


def orthonormal(left, rank):
    shape = jax.ShapeDtypeStruct((6 * rank, left.shape[1]), bf16)
    return pl.pallas_call(
        functools.partial(ortho_kernel, rank), out_shape=(shape, shape), name="orthonormal"
    )(left)


def right_kernel(numbers, rank, left_ref, full_ref, out_ref):
    high, low = high_low(full_ref[...])
    left = left_ref[...]
    by_high, by_low = dot(left, high, numbers), dot(left, low, numbers)
    one, two, three = slice(0, rank), slice(2 * rank, 3 * rank), slice(5 * rank, 6 * rank)
    total = by_high[one] + by_high[two] + by_high[three] + by_low[one] + by_low[two]
    out_ref[...] = total.astype(out_ref.dtype)


def right_part(left, full, by_rows, dtype, *deps):
    latents, width = full.shape if by_rows else full.shape[::-1]
    rank = left.shape[0] // 6
    block = min(1024, latents)
    return call(
        functools.partial(right_kernel, contract_cols if by_rows else contract_plain, rank),
        "right_part",
        (left, full),
        like((rank, latents), dtype),
        (latents // block,),
        [whole_of(left.shape), row_block(block, width) if by_rows else column_block(width, block)],
        column_block(rank, block),
        deps,
        (24 * rank * latents * width, 4 * latents * width),
    )


def stack_kernel(right_ref, bias_ref, out_ref):
    index = lax.broadcasted_iota(jnp.int32, right_ref.shape, 0)
    bias = jnp.where(index == 0, bias_ref[...], 0.0)
    out_ref[...] = jnp.concatenate([right_ref[...], bias], axis=0).astype(bf16)


def pieces_of_right(right):
    one, two, three = split_floats(right)
    return jnp.concatenate([one, two, one, two, three, one], axis=0).astype(bf16)


def enc_final_kernel(rep_count, left_ref, right_ref, full_ref, mom_ref, w_ref, w_out, mom_out, err_out):
    approx = dot(left_ref[...], pieces_of_right(right_ref[:8, :]), contract_rows)
    err_out[...] = full_ref[...] - approx * (1.0 / rep_count)
    mom = momentum_decay * mom_ref[...] + approx
    mom_out[...] = mom
    w_out[...] = w_ref[...] - rate_enc * mom


def dec_final_kernel(rep_count, left_ref, right_ref, full_ref, mom_ref, w_ref, w_out, mom_out, err_out):
    approx = dot(pieces_of_right(right_ref[:8, :]), left_ref[...], contract_rows)
    err_out[...] = full_ref[...] - approx * (1.0 / rep_count)
    mom = momentum_decay * mom_ref[...] + approx
    mom_out[...] = mom
    step = w_ref[...] - rate_dec * mom
    w_out[...] = step * lax.rsqrt(jnp.sum(step * step, axis=1, keepdims=True) + 1e-06)


def final_update(kernel, by_rows, rep_count, left, right, full, mom, weight, *deps):
    latents, width = right.shape[1], left.shape[1]
    block = min(1024, latents)
    big = row_block(block, width) if by_rows else column_block(width, block)
    return call(
        functools.partial(kernel, rep_count),
        "final_update",
        (left, right, full, mom, weight),
        (like(full.shape),) * 3,
        (latents // block,),
        [whole_of(left.shape), column_block(right.shape[0], block), big, big, big],
        (big, big, big),
        deps,
        (2 * 48 * latents * width, 24 * latents * width),
    )


def stack_weights_kernel(qkv_ref, out_ref, fc_ref, proj_ref, top_ref, bottom_ref):
    share, width = out_ref.shape
    squares = [qkv_ref[:, k * width : (k + 1) * width] for k in range(3)] + [out_ref[...]]
    squares += [fc_ref[:, k * width : (k + 1) * width] for k in range(fc_ref.shape[1] // width)]
    half = top_ref.shape[0] // share
    for k, square in enumerate(squares):
        if k < half:
            top_ref[k * share : (k + 1) * share, :] = square
        else:
            bottom_ref[(k - half) * share : (k - half + 1) * share, :] = square
    bottom_ref[(len(squares) - half) * share :, :] = proj_ref[...]


def stack_weights(w_qkv, w_out, w_fc, w_proj):
    share, width = w_out.shape
    rows = share * (4 + w_fc.shape[1] // width) + w_proj.shape[0]
    half = like((rows // 2, width), bf16)
    return call(stack_weights_kernel, "stack_weights", (w_qkv, w_out, w_fc, w_proj), (half, half))


def frozen_kernel(share, *refs):
    residual_ref, norm_ref, bias_ref, dec_bias_ref = refs[:4]
    count = refs[-2].shape[0]
    pieces = refs[4 : 4 + 2 * count]
    stream_out, centered_out, orig_out, weights, sems = refs[4 + 2 * count :]
    me = lax.axis_index("lat")
    total_rows, width = weights.shape[1:]
    hidden = (total_rows // share - 8) * share * count
    cuts = [0, 3 * share, total_rows // 2, total_rows]
    copies = [[] for _ in cuts[1:]]
    for j in range(count):
        for k in range(len(cuts) - 1):
            rows = cuts[k + 1] - cuts[k]
            piece, inner = (pieces[2 * j], cuts[k]) if k < len(cuts) - 2 else (pieces[2 * j + 1], 0)
            copies[k].append(
                pltpu.make_async_copy(
                    piece.at[pl.ds(inner, rows), :],
                    weights.at[me ^ j, pl.ds(cuts[k], rows), :],
                    sems.at[k, j],
                )
            )
    for group in copies:
        for copy in group:
            copy.start()

    def square(k):
        return weights[:, k * share : (k + 1) * share, :].reshape(width, width)

    def norm(values, row):
        return layer_norm(values, norm_ref[row : row + 1, :], norm_ref[row + 1 : row + 2, :])

    def bias(k, count=1):
        return bias_ref[:, k * width : (k + count) * width]

    stream = residual_ref[...].astype(f32)
    normed = norm(stream, 0).astype(bf16)
    for copy in copies[0]:
        copy.wait()
    queries, keys, values = [
        (dot(normed, square(k), contract_plain) + bias(k)).astype(bf16) for k in range(3)
    ]
    seq_len = stream.shape[0]
    early = lax.broadcasted_iota(jnp.int32, (seq_len, lanes), 1) < width // HEADS
    causal = lax.broadcasted_iota(jnp.int32, (seq_len, seq_len), 0) >= lax.broadcasted_iota(
        jnp.int32, (seq_len, seq_len), 1
    )
    nothing = jnp.zeros((), bf16)
    attended = []
    for k in range(0, width, lanes):
        pair_q, pair_k, pair_v = (part[:, k : k + lanes] for part in (queries, keys, values))
        outs = []
        for is_early in (True, False):
            head_q = jnp.where(early == is_early, pair_q, nothing)
            scores = dot(head_q, pair_k, contract_cols) / math.sqrt(width // HEADS)
            scores = jnp.where(causal, scores, -1e30)
            grown = jnp.exp(scores - jnp.max(scores, axis=1, keepdims=True))
            share_of = (grown / jnp.sum(grown, axis=1, keepdims=True)).astype(bf16)
            outs.append(dot(share_of, pair_v, contract_plain))
        attended.append(jnp.where(early, outs[0], outs[1]).astype(bf16))
    attended = jnp.concatenate(attended, axis=1)
    for copy in copies[1]:
        copy.wait()
    stream = stream + dot(attended, square(3), contract_plain) + bias(3)
    normed = norm(stream, 2).astype(bf16)
    for copy in copies[2]:
        copy.wait()
    out = None
    for k in range(hidden // width):
        inner = dot(normed, square(4 + k), contract_plain) + bias(4 + k)
        activated = jax.nn.gelu(inner, approximate=True).astype(bf16)
        per = width // (hidden // weights.shape[0])
        block = weights[k * per : (k + 1) * per, 8 * share :, :].reshape(width, width)
        part = dot(activated, block, contract_plain)
        out = part if out is None else out + part
    stream = stream + out + bias(4 + hidden // width)
    stream_out[...] = stream
    centered_out[...] = (stream - dec_bias_ref[...]).astype(bf16)
    orig_out[...] = norm(stream, 4).astype(bf16)


def frozen_whole(residual, norm_params, biases, dec_bias, pieces, share, *deps):
    rows, width = residual.shape
    total = 2 * pieces[0].shape[0]
    count = len(pieces) // 2
    return call(
        functools.partial(frozen_kernel, share),
        "frozen_block",
        (residual, norm_params, biases[None, :], dec_bias[None, :], *pieces),
        (like((rows, width)), like((rows, width), bf16), like((rows, width), bf16)),
        (),
        [in_vmem] * 4 + [untouched] * len(pieces),
        (in_vmem,) * 3,
        deps,
        (2 * rows * count * total * width, 2 * count * total * width),
        scratch=[pltpu.VMEM((count, total, width), bf16), pltpu.SemaphoreType.DMA((3, count))],
    )


def layer_norm(values, gain_row, shift_row):
    center = values - jnp.mean(values, axis=-1, keepdims=True)
    spread = jnp.mean(center * center, axis=-1, keepdims=True)
    return center * lax.rsqrt(spread + 1e-05) * gain_row + shift_row


def frozen_block(residual, norm_params, biases, qkv, w_out, fc, w_proj):
    seq_len = residual.shape[0]
    model_width = residual.shape[1]
    hidden_units = w_proj.shape[0]
    head_dim = model_width // HEADS
    stream = residual.astype(f32)
    normed = layer_norm(stream, norm_params[0], norm_params[1]).astype(bf16)

    def times(values, parts, bias):
        width = parts[0].shape[1]
        return [
            jnp.dot(values, part, preferred_element_type=f32) + bias[k * width : (k + 1) * width]
            for k, part in enumerate(parts)
        ]

    queries, keys, values = [
        part.astype(bf16).reshape(seq_len, HEADS, head_dim)
        for part in times(normed, qkv, biases[: 3 * model_width])
    ]
    scores = jnp.einsum("qhd,khd->hqk", queries, keys, preferred_element_type=f32) / math.sqrt(head_dim)
    causal = jnp.arange(seq_len)[:, None] >= jnp.arange(seq_len)[None, :]
    scores = jnp.where(causal, scores, -1e30)
    weights = jax.nn.softmax(scores, axis=-1).astype(bf16)
    attended = jnp.einsum("hqk,khd->qhd", weights, values, preferred_element_type=f32)
    attended = attended.astype(bf16).reshape(seq_len, model_width)
    stream = (
        stream
        + jnp.dot(attended, w_out, preferred_element_type=f32)
        + biases[3 * model_width : 4 * model_width]
    )
    normed = layer_norm(stream, norm_params[2], norm_params[3]).astype(bf16)
    inner_in = times(normed, fc, biases[4 * model_width : 4 * model_width + hidden_units])
    activated = jnp.concatenate(
        [jax.nn.gelu(part, approximate=True).astype(bf16) for part in inner_in], axis=1
    )
    return (
        stream
        + jnp.dot(activated, w_proj, preferred_element_type=f32)
        + biases[4 * model_width + hidden_units :]
    )


def per_device(
    residual,
    valid_mask,
    top_idx,
    aux_idx,
    dead_flags,
    norm_params,
    biases,
    w_qkv,
    w_out,
    w_fc,
    w_proj,
    head_table,
    w_enc,
    encoder_bias_vec,
    w_dec,
    decoder_bias_vec,
    mom_enc,
    mom_benc,
    mom_dec,
    mom_bdec,
    q_enc,
    q_dec,
    err_enc,
    err_dec,
):
    rep_count = lax.axis_size("rep")
    lat_index = lax.axis_index("lat")
    model_width = residual.shape[1]
    hidden_units = w_fc.shape[1]
    lat_dev = w_enc.shape[1]
    top_count, aux_count = top_idx.shape[1], aux_idx.shape[1]
    rank = q_enc.shape[1]
    err_enc, err_dec = err_enc[0], err_dec[0]

    half = aux_count // 2
    valid_float = valid_mask.astype(f32)
    packed = jnp.concatenate(
        [
            aux_idx[:, :half] * pack_base + aux_idx[:, half:],
            top_idx,
            jnp.broadcast_to(-1 - valid_mask[:, None], (valid_mask.shape[0], lanes - top_count)),
        ],
        axis=1,
    )
    dead_pair = jnp.concatenate(
        [
            lax.dynamic_slice_in_dim(dead_flags, base * lat_dev, lat_dev)
            for base in (lat_index, lat_index ^ 1)
        ]
    ).astype(f32)[None, :]
    share = w_qkv.shape[0]
    by_piece = lax.axis_size("lat") == 8 and share % 16 == 0
    if by_piece:
        top, bottom = stack_weights(w_qkv, w_out, w_fc, w_proj)
        picks = Gather(packed)
        four_top, two_bottom = swap(top, "lat", 4), swap(bottom, "lat", 2)
        two_top, four_bottom = swap(top, "lat", 2), swap(bottom, "lat", 4)
        rows = packed.shape[0]
        masks, valid_0 = build_mask(packed, dead_pair, aux_count, top_count, 4 * rows, 3 * rows, deps=(top,))
        by_two, by_six, by_four, _ = picks.blocks
        masks, valid_1 = build_mask(
            by_two, dead_pair, aux_count, top_count, 4 * rows, 0, masks, deps=(by_six, by_four)
        )
        four_top, two_bottom = pass_after(four_top, masks[0]), pass_after(two_bottom, masks[0])
        six_top, six_bottom = swap(four_top, "lat", 2), swap(two_bottom, "lat", 4)
        masks, valid_2 = build_mask(by_four, dead_pair, aux_count, top_count, 4 * rows, 2 * rows, masks)
        masks, valid_3 = build_mask(by_six, dead_pair, aux_count, top_count, 4 * rows, rows, masks)
        valid_total = valid_0 + valid_1 + valid_2 + valid_3
        even_pieces = [(top, bottom), (two_top, two_bottom), (four_top, four_bottom)]
        even_pieces.append((pass_after(six_top, masks[0]), pass_after(six_bottom, masks[0])))
        pieces = [
            piece
            for pair in even_pieces
            for piece in (*pair, *(swap(half_piece, "lat", 1) for half_piece in pair))
        ]
    else:
        joined = lax.all_gather(jnp.concatenate([w_qkv, w_out, w_fc], axis=1), "lat", axis=0, tiled=True)
        proj_all = lax.all_gather(w_proj, "lat", axis=0, tiled=True)
        squares = [joined[:, k : k + model_width] for k in range(0, joined.shape[1], model_width)]
        packed = gather_even(packed)
        masks, valid_total = build_mask(packed, dead_pair, aux_count, top_count, packed.shape[0], 0)
    mask_even, mask_partner = masks
    valid_total = sum_round(valid_total, "lat", [1])
    def final_norm(values):
        return layer_norm(values, norm_params[4], norm_params[5])

    if by_piece:
        stream, centered_own, orig_blocks = frozen_whole(
            residual,
            norm_params,
            biases,
            decoder_bias_vec,
            pieces,
            share,
            masks[0],
            valid_total,
        )
        mask_partner = pass_after(mask_partner, centered_own)
    else:
        stream = frozen_block(residual, norm_params, biases, squares[:3], squares[3], squares[4:], proj_all)
        centered_own = (stream - decoder_bias_vec).astype(bf16)
        orig_blocks = final_norm(stream).astype(bf16)
    gather = Gather(centered_own)
    enc_weight = rounded(w_enc, False, centered_own)
    mask_odd = swap(mask_partner, "lat", 1)
    valid_total = sum_round(pass_after(valid_total, centered_own), "rep", bits_of("rep"))
    weight_own = (valid_float / valid_total[0, 0])[:, None]
    dec_weight = rounded(w_dec, True, enc_weight, valid_total)
    centered = gather.end(dec_weight)
    q_enc_rows, q_enc_columns = factor_pieces(q_enc.T, dec_weight)
    q_dec_rows, q_dec_columns = factor_pieces(q_dec.T, q_enc_rows)

    bias_row = encoder_bias_vec[None, :]
    tops_odd, auxes_odd, top_odd = forward(
        centered[1], enc_weight, bias_row, mask_odd, dec_weight, q_dec_rows
    )
    rebuilt = Scatter(top_odd)
    tops_even, auxes_even, top_even = forward(centered[0], enc_weight, bias_row, mask_even, dec_weight, top_odd)
    sent = rebuilt.chip(top_even)
    aux_part = aux_forward(auxes_odd, auxes_even, dec_weight, sent)
    auxiliary_rebuilt = lax.psum_scatter(aux_part, "lat", scatter_dimension=0, tiled=False)
    orig_group = gather_behind(orig_blocks, aux_part)
    rebuilt_input = rebuilt.last(orig_group[0]) + decoder_bias_vec
    rec_float, norm_back = jax.vjp(final_norm, rebuilt_input)
    gather = Gather(rec_float.astype(bf16))
    orig_odd = head_part(orig_group[1], head_table, gather.own)
    rec_group = gather.end(orig_odd)
    orig_mean = Scatter(pass_after(orig_odd, rec_group[0]), lanes)
    orig_even = head_part(orig_group[0], head_table, rec_group[0])
    sent = orig_mean.chip(orig_even)
    rec_odd = head_part(rec_group[1], head_table, sent)
    orig_mean = orig_mean.last(rec_odd)
    rec_odd = pass_after(rec_odd, orig_mean)
    rec_mean = Scatter(rec_odd, lanes)
    aux_pull, aux_blocks, err_square = residual_pull(
        stream, rebuilt_input, auxiliary_rebuilt, weight_own, orig_mean
    )
    rec_even = head_part(rec_group[0], head_table, aux_blocks)
    sent = rec_mean.chip(rec_even)

    products_dec = factor_products(tops_odd, tops_even, q_dec_columns, sent)
    left_enc = err_left(q_enc_rows, err_enc, products_dec[0])
    rec_mean = rec_mean.last(left_enc)

    orig_lse, rec_lse = orig_mean[:, model_width], rec_mean[:, model_width]
    orig_mean, rec_mean = orig_mean[:, :model_width], rec_mean[:, :model_width]
    (grad_head,) = norm_back(weight_own * (rec_mean - orig_mean))
    grad_recon = (grad_head + aux_pull).astype(bf16)
    gather = Gather(grad_recon)
    aux_group = gather_behind(aux_blocks, grad_recon)
    pre_odd, pre_even = aux_back(aux_group[1], aux_group[0], dec_weight, mask_odd, mask_even)
    recon_group = gather.end(pre_odd)
    dec_part, left_dec = part_dec((auxes_odd, auxes_even), (aux_group[1], aux_group[0]), err_dec, q_dec_rows, recon_group[0])
    gap = orig_blocks.astype(f32) - rec_float.astype(bf16).astype(f32)
    kl_own = jnp.sum(gap * orig_mean, axis=1) - orig_lse + rec_lse
    loss_tokens = (valid_float * (kl_own + aux_weight * err_square[:, 0]))[None, :]

    pre_odd, pre_even, grad_benc, bias_pull, enc_odd, enc_even = back_pass(
        recon_group[1],
        recon_group[0],
        dec_weight,
        enc_weight,
        mask_odd,
        mask_even,
        pre_odd,
        pre_even,
        q_enc_columns,
        dec_part,
    )
    small = call(
        functools.partial(left_sums_kernel, rank),
        "left_sums",
        (
            enc_odd,
            enc_even,
            centered[1],
            centered[0],
            *products_dec,
            recon_group[1],
            recon_group[0],
            left_enc,
            left_dec,
            grad_recon,
            bias_pull,
            loss_tokens,
        ),
        like((2 * rank + 8, model_width)),
    )
    codes, grads = (tops_odd, tops_even), (recon_group[1], recon_group[0])
    full_dec = add_dec(codes, grads, dec_part, 0, 2, small)
    small = sum_round(small, "lat", [1])
    full_dec = add_dec(codes, grads, full_dec, 1, 2, small)
    small = sum_round(small, "lat", bits_of("lat")[1:])
    full_enc = form_enc((centered[1], centered[0]), (pre_odd, pre_even), err_enc, small, full_dec)
    small = sum_round(small, "rep", bits_of("rep"))
    grad_bdec, loss_sum = small[2 * rank], small[2 * rank + 1, 0]

    ortho_enc, ortho_dec = orthonormal(small[: 2 * rank], rank)
    right_enc = right_part(ortho_enc, full_enc, False, bf16)
    right_dec = right_part(ortho_dec, full_dec, True, f32, right_enc)
    right_enc = sum_round(right_enc, "rep", bits_of("rep"), sent_as=bf16)
    right_dec = call(
        stack_kernel, "stack", (right_dec, grad_benc), like((2 * rank, lat_dev), bf16), deps=(right_enc,)
    )
    right_dec = sum_round(right_dec, "rep", bits_of("rep"), sent_as=bf16)
    grad_benc = right_dec[rank]

    w_enc_new, mom_enc_new, err_enc_new = final_update(
        enc_final_kernel, False, rep_count, ortho_enc, right_enc, full_enc, mom_enc, w_enc
    )
    w_dec_new, mom_dec_new, err_dec_new = final_update(
        dec_final_kernel, True, rep_count, ortho_dec, right_dec, full_dec, mom_dec, w_dec, w_enc_new
    )
    mom_benc_new = momentum_decay * mom_benc + grad_benc
    mom_bdec_new = momentum_decay * mom_bdec + grad_bdec
    b_enc_new = encoder_bias_vec - rate_benc * mom_benc_new
    b_dec_new = decoder_bias_vec - rate_bdec * mom_bdec_new
    return (
        loss_sum,
        valid_total[0, 0],
        w_enc_new,
        b_enc_new,
        w_dec_new,
        b_dec_new,
        mom_enc_new,
        mom_benc_new,
        mom_dec_new,
        mom_bdec_new,
        right_enc.T,
        right_dec[:rank].T,
        err_enc_new[None],
        err_dec_new[None],
    )


def solution(mesh):
    in_specs = (
        P(("rep", "lat"), None),
        P(("rep", "lat")),
        P(("rep", "lat"), None),
        P(("rep", "lat"), None),
        P(),
        P(),
        P(),
        P("lat", None),
        P("lat", None),
        P("lat", None),
        P("lat", None),
        P("lat", None),
        P(None, "lat"),
        P("lat"),
        P("lat", None),
        P(),
        P(None, "lat"),
        P("lat"),
        P("lat", None),
        P(),
        P("lat", None),
        P("lat", None),
        P("rep", None, "lat"),
        P("rep", "lat", None),
    )
    out_specs = (
        P(),
        P(),
        P(None, "lat"),
        P("lat"),
        P("lat", None),
        P(),
        P(None, "lat"),
        P("lat"),
        P("lat", None),
        P(),
        P("lat", None),
        P("lat", None),
        P("rep", None, "lat"),
        P("rep", "lat", None),
    )
    return jax.shard_map(
        per_device, mesh=mesh, in_specs=in_specs, out_specs=out_specs, check_vma=False
    )
```

```python
import functools
import math

import jax
import jax.numpy as jnp
from jax import lax
from jax.experimental import pallas as pl
from jax.experimental.pallas import tpu as pltpu
from jax.sharding import PartitionSpec as P

HEADS = 12
HEAD_PARTS = (3, 13)

pack_base = 32768
aux_weight = 1.0 / 32.0
momentum_decay = 0.9
rate_enc = 3000.0
rate_dec = 3000.0
rate_benc = 10000.0
rate_bdec = 500.0
lanes = 128
rooms = {
    "usual": 16,
    "head_part": 44,
    "forward": 60,
    "aux_forward": 60,
    "stack_weights": 60,
    "frozen_block": 30,
    "final_update": 52,
    "back_pass": 40,
    "add_dec": 36,
    "form_enc": 36,
    "part_dec": 60,
    "aux_back": 60,
    "err_left": 60,
    "right_part": 60,
    "cut_weights": 20,
    "rounded": 60,
    "factor_products": 24,
}
contract_cols = (((1,), (1,)), ((), ()))
contract_rows = (((0,), (0,)), ((), ()))
contract_plain = (((1,), (0,)), ((), ()))
f32 = jnp.float32
bf16 = jnp.bfloat16


def swap(values, axis, bit):
    count = lax.axis_size(axis)
    return lax.ppermute(values, axis, [(i, i ^ bit) for i in range(count)])


def bits_of(axis):
    count = lax.axis_size(axis)
    return [1 << k for k in range(count.bit_length() - 1)]


def even_order():
    count = lax.axis_size("lat")
    return [2, 6, 4, 0] if count == 8 else list(range(count - 2, -1, -2))


def gather_even(own):
    if lax.axis_size("lat") == 8:
        half = own.shape[0] // 2
        by_two, by_four = swap(own, "lat", 2), swap(own, "lat", 4)
        return jnp.concatenate(
            [by_two, swap(by_four[:half], "lat", 2), swap(by_two[half:], "lat", 4), by_four, own], axis=0
        )
    blocks = {0: own}
    for bit in bits_of("lat")[1:]:
        order = sorted(blocks)
        moved = swap(jnp.stack([blocks[j] for j in order]), "lat", bit)
        for at, j in enumerate(order):
            blocks[j ^ bit] = moved[at]
    return jnp.concatenate([blocks[j] for j in even_order()], axis=0)


def gather_tokens(own):
    even = gather_even(own)
    return even, swap(even, "lat", 1)


def scatter_paths():
    others = bits_of("lat")[1:]
    if len(others) == 2:
        return [(0, 2, others), (1, 2, others[::-1])]
    return [(0, 1, others)]


def take_blocks(values, part, parts):
    rows, width = values.shape[0] // len(even_order()), values.shape[1] // parts
    return {
        j: values[at * rows : (at + 1) * rows, part * width : (part + 1) * width]
        for at, j in enumerate(even_order())
    }


def scatter_sum(even, odd_moved):
    chip = even + odd_moved
    done = []
    for part, parts, order in scatter_paths():
        held = take_blocks(chip, part, parts)
        for bit in order:
            sent = [j for j in even_order() if j in held and j & bit]
            got = swap(jnp.concatenate([held[j] for j in sent], axis=0).astype(bf16), "lat", bit)
            rows = held[0].shape[0]
            for at, j in enumerate(sent):
                held[j ^ bit] = held[j ^ bit] + got[at * rows : (at + 1) * rows].astype(f32)
                del held[j]
        done.append(held[0])
    return jnp.concatenate(done, axis=1)


def merge(mean_a, lse_a, mean_b, lse_b):
    top = jnp.maximum(lse_a, lse_b)
    exp_a, exp_b = jnp.exp(lse_a - top), jnp.exp(lse_b - top)
    total = exp_a + exp_b
    mixed = mean_a.astype(f32) * (exp_a / total) + mean_b.astype(f32) * (exp_b / total)
    return mixed, top + jnp.log(total)


def scatter_mean(even, even_lse, odd_moved, odd_lse_moved):
    chip, chip_lse = merge(even, even_lse, odd_moved, odd_lse_moved)
    done = []
    for part, parts, order in scatter_paths():
        means, lses = take_blocks(chip, part, parts), take_blocks(chip_lse, 0, 1)
        held = {j: (means[j], lses[j]) for j in means}
        for bit in order:
            sent = [j for j in even_order() if j in held and j & bit]
            rows = held[0][0].shape[0]
            got = swap(jnp.concatenate([held[j][0] for j in sent], axis=0).astype(bf16), "lat", bit)
            got_lse = swap(jnp.concatenate([held[j][1] for j in sent], axis=0), "lat", bit)
            for at, j in enumerate(sent):
                span = slice(at * rows, (at + 1) * rows)
                held[j ^ bit] = merge(*held[j ^ bit], got[span], got_lse[span])
                del held[j]
        done.append(held[0])
    return jnp.concatenate([mean for mean, _ in done], axis=1), done[0][1]


def sum_round(values, axis, bits, sent_as=None):
    if sent_as is not None:
        values = values.astype(sent_as)
    if len(bits) == 2:
        one, two, both = (swap(values, axis, bit) for bit in (bits[0], bits[1], bits[0] | bits[1]))
        return (values.astype(f32) + one.astype(f32)) + (two.astype(f32) + both.astype(f32))
    for bit in bits:
        values = values.astype(f32) + swap(values, axis, bit).astype(f32)
    return values


untouched = pl.BlockSpec(memory_space=pl.ANY)
in_vmem = pl.BlockSpec(memory_space=pltpu.VMEM)


def dot(a, b, numbers):
    return lax.dot_general(a, b, numbers, preferred_element_type=f32)


made_with = []


def marker(value):
    for made, small in made_with:
        if made is value:
            return small
    return value


def call(kernel, name, args, out_shape, grid=(), in_specs=None, out_specs=None, deps=(), cost=(0, 0), aliases=None, scratch=()):
    deps = [marker(dep) for dep in deps]
    count, skipped = len(args), len(deps)
    single = not isinstance(out_shape, (tuple, list))
    out_shapes = [out_shape] if single else list(out_shape)
    if in_specs is None:
        in_specs, out_specs = [in_vmem] * count, [in_vmem] * len(out_shapes)
    else:
        out_specs = [out_specs] if single else list(out_specs)
    results = len(out_shapes)

    def body(*refs):
        own = refs[count + skipped :]
        kernel(*refs[:count], *own[:results], *own[results + 1 :])

    flops, moved = cost
    *outs, small = pl.pallas_call(
        body,
        out_shape=out_shapes + [like((8, lanes))],
        grid=grid,
        in_specs=list(in_specs) + [untouched] * skipped,
        out_specs=out_specs + [untouched],
        scratch_shapes=list(scratch),
        input_output_aliases=aliases or {},
        compiler_params=pltpu.CompilerParams(vmem_limit_bytes=rooms.get(name, rooms["usual"]) * 2**20),
        cost_estimate=pl.CostEstimate(flops=flops, bytes_accessed=moved, transcendentals=0),
        name=name,
    )(*args, *deps)
    made_with.extend((out, small) for out in outs)
    return outs[0] if single else outs


def like(shape, dtype=f32):
    return jax.ShapeDtypeStruct(shape, dtype)


def clear_at_start(*refs):
    @pl.when(pl.program_id(0) == 0)
    def _():
        for ref in refs:
            ref[...] = jnp.zeros_like(ref)


def mask_kernel(tokens, hi_count, aux_count, top_count, *refs):
    packed = refs[0][...]
    dead_ref, own_ref, partner_ref, valid_ref, ids_ref, top_ref, scratch = refs[1], *refs[-6:]
    me, lat_dev = lax.axis_index("lat"), hi_count * lanes
    half, rows = aux_count // 2, 2 * hi_count

    def placed(ids):
        from_own, from_partner = ids - me * lat_dev, ids - (me ^ 1) * lat_dev
        return jnp.where(
            (from_own >= 0) & (from_own < lat_dev),
            from_own,
            jnp.where((from_partner >= 0) & (from_partner < lat_dev), from_partner + lat_dev, -(2**20)),
        )

    ids_ref[:, :half] = placed(packed[:, :half] >> 15)
    ids_ref[:, half:] = placed(packed[:, :half] & (pack_base - 1))
    joint_count = lanes // top_count
    tops = packed[:, half:]
    lane = lax.broadcasted_iota(jnp.int32, tops.shape, 1)
    repeated = tops
    for k in range(1, joint_count):
        repeated = jnp.where(lane // top_count == k, pltpu.roll(tops, k * top_count, 1), repeated)
    top_ref[...] = placed(repeated) + (lane // top_count) * (rows * lanes)
    counted = jnp.where(lane == top_count, -1 - tops, 0).astype(f32)
    valid = jnp.sum(jnp.sum(counted, axis=0, keepdims=True), axis=1, keepdims=True)
    clear_at_start(valid_ref)
    valid_ref[...] += jnp.broadcast_to(valid, valid_ref.shape)

    def hot(count, width, index):
        return jnp.where(lax.broadcasted_iota(jnp.int32, (count, width), 0) == index, 1.0, 0.0).astype(bf16)

    def some_tokens(group, carry):
        base = group * joint_count
        for k in range(joint_count):
            row = ids_ref[pl.ds(base + k, 1), :]
            picked = dot(hot(rows, aux_count, row >> 7), hot(lanes, aux_count, row & 127), contract_cols)
            scratch[pl.ds(pl.multiple_of((base + k) * rows, rows), rows), :] = 2.0 * picked
        joint_row = top_ref[pl.ds(base, 1), :]
        for k in range(1, joint_count):
            joint_row = jnp.where(lane[:1] // top_count == k, top_ref[pl.ds(base + k, 1), :], joint_row)
        picked = dot(hot(joint_count * rows, lanes, joint_row >> 7), hot(lanes, lanes, joint_row & 127), contract_cols)
        scratch[pl.ds(pl.multiple_of(base * rows, rows), joint_count * rows), :] += picked
        return carry

    lax.fori_loop(0, tokens // joint_count, some_tokens, 0, unroll=4)
    for hi in range(2 * hi_count):
        code = scratch[pl.ds(hi, tokens, stride=2 * hi_count), :]
        aux = jnp.where(code >= 2.0, 2.0, 0.0)
        code = (code - aux + aux * dead_ref[:, hi * lanes : (hi + 1) * lanes]).astype(bf16)
        if hi < hi_count:
            own_ref[:, hi * lanes : (hi + 1) * lanes] = code
        else:
            partner_ref[:, (hi - hi_count) * lanes : (hi - hi_count + 1) * lanes] = code


def build_mask(packed, dead_pair, aux_count, top_count, rows, first, so_far=(), deps=()):
    width = packed.shape[1]
    lat_dev = dead_pair.shape[1] // 2
    hi_count, tokens = lat_dev // lanes, 64
    steps = packed.shape[0] // tokens
    out_block = pl.BlockSpec((tokens, lat_dev), lambda i: (i + first // tokens, 0))
    *masks, valid = call(
        functools.partial(mask_kernel, tokens, hi_count, aux_count, top_count),
        "build_mask",
        (packed, dead_pair, *so_far),
        (like((rows, lat_dev), bf16), like((rows, lat_dev), bf16), like((1, lanes))),
        (steps,),
        [row_block(tokens, width), whole_of((1, 2 * lat_dev))] + [untouched] * len(so_far),
        (out_block, out_block, whole_of((1, lanes))),
        deps,
        (16 * steps * tokens * 2 * lat_dev * aux_count, 4 * steps * tokens * lat_dev),
        aliases={2 + k: k for k in range(len(so_far))},
        scratch=[
            pltpu.VMEM((tokens, aux_count), jnp.int32),
            pltpu.VMEM((tokens, lanes), jnp.int32),
            pltpu.VMEM((tokens * 2 * hi_count, lanes), f32),
        ],
    )
    return masks, valid


def pass_kernel(in_ref, out_ref):
    pass


def pass_after(value, *deps):
    return call(
        pass_kernel, "pass_after", (value,), like(value.shape, value.dtype), (), [untouched], untouched, deps, aliases={0: 0}
    )


def split_three(values):
    first = values.astype(bf16)
    rest = values - first.astype(f32)
    second = rest.astype(bf16)
    return first, second, (rest - second.astype(f32)).astype(bf16)


def split_floats(values):
    return [piece.astype(f32) for piece in split_three(values)]


def residual_kernel(weight, stream_ref, rebuilt_ref, aux_ref, weight_ref, pull_ref, rounded_ref, square_ref):
    err = stream_ref[...] - rebuilt_ref[...] - aux_ref[...]
    pull = -(2.0 * weight) * weight_ref[...] * err
    pull_ref[...] = pull
    rounded_ref[...] = pull.astype(bf16)
    square_ref[...] = jnp.sum(err * err, axis=1, keepdims=True)


def residual_pull(stream, rebuilt, aux, weight_own, *deps):
    shape = stream.shape
    return call(
        functools.partial(residual_kernel, aux_weight),
        "residual_pull",
        (stream, rebuilt, aux, weight_own),
        (like(shape), like(shape, bf16), like((shape[0], 1))),
        deps=deps,
    )


def high_low(values):
    high = values.astype(bf16)
    return high, (values - high.astype(f32)).astype(bf16)


def assemble_kernel(*refs):
    *blocks, even_ref = refs
    rows = blocks[0].shape[0]
    for at, block in enumerate(blocks):
        even_ref[at * rows : (at + 1) * rows, :] = block[...]


class Gather:
    def __init__(self, own):
        self.own, self.plain = own, lax.axis_size("lat") != 8
        if not self.plain:
            self.blocks = [swap(own, "lat", j) if j else own for j in even_order()]

    def end(self, *deps):
        if self.plain:
            return gather_tokens(self.own)
        rows, width = self.own.shape
        even = call(assemble_kernel, "assemble", self.blocks, like((4 * rows, width), self.own.dtype), deps=deps)
        return even, swap(even, "lat", 1)


def reorder_kernel(blocks_ref, even_ref, odd_ref):
    me, rows = lax.axis_index("lat"), blocks_ref.shape[1]
    for at, j in enumerate(even_order()):
        even_ref[at * rows : (at + 1) * rows, :] = blocks_ref[me ^ j]
        odd_ref[at * rows : (at + 1) * rows, :] = blocks_ref[me ^ (j ^ 1)]


def gather_behind(own, *deps):
    blocks = lax.all_gather(own, "lat", axis=0)
    count, rows, width = blocks.shape
    half = like((count // 2 * rows, width), own.dtype)
    return call(reorder_kernel, "reorder", (blocks,), (half, half), deps=deps)


def joint(parts, tail):
    if not tail:
        return sum(parts[1:], parts[0])
    lses = [part[:, -tail:] for part in parts]
    top = functools.reduce(jnp.maximum, lses)
    weights = [jnp.exp(lse - top) for lse in lses]
    total = sum(weights[1:], weights[0])
    means = [part[:, :-tail] * (weight / total)[:, :1] for part, weight in zip(parts, weights)]
    return jnp.concatenate([sum(means[1:], means[0]), top + jnp.log(total)], axis=1)


def to_send(values, tail):
    if not tail:
        return values.astype(bf16)
    lane = lax.broadcasted_iota(jnp.int32, (values.shape[0], tail), 1)
    one, two, three = split_floats(values[:, -tail:])
    logs = jnp.where(lane < 32, one, jnp.where(lane < 64, two, three))
    return jnp.concatenate([values[:, :-tail], logs], axis=1).astype(bf16)


def received(ref, tail):
    values = ref[...].astype(f32)
    if not tail:
        return values
    logs = values[:, -tail:]
    lse = logs[:, :1] + logs[:, 32:33] + logs[:, 64:65]
    return jnp.concatenate([values[:, :-tail], jnp.broadcast_to(lse, logs.shape)], axis=1)


def chip_kernel(tail, even_ref, odd_ref, *outs):
    rows = outs[0].shape[0]
    for at, out in enumerate(outs):
        span = slice(at * rows, (at + 1) * rows)
        total = joint([even_ref[span, :], odd_ref[span, :]], tail)
        out[...] = total if at == len(outs) - 1 else to_send(total, tail)


def last_kernel(tail, *refs):
    *got, keep, total_ref = refs
    total_ref[...] = joint([keep[...]] + [received(ref, tail) for ref in got], tail)


class Scatter:
    def __init__(self, odd, tail=0):
        self.moved, self.tail, self.plain = swap(odd, "lat", 1), tail, lax.axis_size("lat") != 8

    def chip(self, even, *deps):
        self.even = even
        if self.plain:
            return even
        rows, width = even.shape[0] // 4, even.shape[1]
        shapes = [like((rows, width), bf16)] * 3 + [like((rows, width))]
        *sends, keep = call(
            functools.partial(chip_kernel, self.tail), "chip_sum", (even, self.moved), shapes, deps=deps
        )
        self.pending = [swap(send, "lat", j) for send, j in zip(sends, even_order())] + [keep]
        return keep

    def last(self, *deps):
        if self.plain:
            if not self.tail:
                return scatter_sum(self.even, self.moved)
            width = self.even.shape[1] - self.tail
            mean, lse = scatter_mean(
                self.even[:, :width], self.even[:, width : width + 1], self.moved[:, :width], self.moved[:, width : width + 1]
            )
            return jnp.concatenate([mean, jnp.broadcast_to(lse, (lse.shape[0], self.tail))], axis=1)
        return call(
            functools.partial(last_kernel, self.tail), "last_sum", self.pending, like(self.pending[-1].shape), deps=deps
        )


def head_kernel(cuts, steps, normed_ref, table_hbm, out_ref, table_ref, sems):
    def piece(c):
        span = pl.ds(cuts[c], cuts[c + 1] - cuts[c])
        return pltpu.make_async_copy(table_hbm.at[span, :], table_ref.at[span, :], sems.at[c])

    def at_start(action):
        if steps == 1:
            action()
        else:
            pl.when(pl.program_id(0) == 0)(action)

    chunks = len(cuts) - 1
    at_start(lambda: [piece(c).start() for c in range(chunks)] and None)
    normed = normed_ref[...]

    def logits_of(c):
        at_start(lambda: piece(c).wait())
        return dot(normed, table_ref[cuts[c] : cuts[c + 1], :], contract_cols)

    def fold(values, op):
        folded = values[:, :lanes]
        for k in range(lanes, values.shape[1], lanes):
            folded = op(folded, values[:, k : k + lanes])
        return folded

    top = total = mean = None
    logits = logits_of(0)
    for c in range(chunks):
        later = logits_of(c + 1) if c + 1 < chunks else None
        chunk_top = jnp.max(fold(logits, jnp.maximum), axis=1, keepdims=True)
        new_top = chunk_top if top is None else jnp.maximum(top, chunk_top)
        grown = jnp.exp(logits - new_top).astype(bf16)
        chunk_total = fold(grown.astype(f32), jnp.add)
        chunk_mean = dot(grown, table_ref[cuts[c] : cuts[c + 1], :], contract_plain)
        if top is None:
            total, mean = chunk_total, chunk_mean
        else:
            shrink = jnp.exp(top - new_top)
            total, mean = total * shrink + chunk_total, mean * shrink + chunk_mean
        top, logits = new_top, later
    total = jnp.sum(total, axis=1, keepdims=True)
    width = mean.shape[1]
    out_ref[:, :width] = mean / total
    out_ref[:, width:] = jnp.broadcast_to(top + jnp.log(total), (mean.shape[0], lanes))


def head_cuts(entries):
    unit = 256 if entries % 256 == 0 else lanes
    tiles = entries // unit
    ends = sorted({max(1, tiles * part // 26) for part in HEAD_PARTS} | {tiles})
    return [0] + [unit * end for end in ends]


def head_part(normed, table, *deps):
    rows, width = normed.shape
    entries = table.shape[0]
    block = min(512, rows)
    cuts = head_cuts(entries)
    return call(
        functools.partial(head_kernel, cuts, rows // block),
        "head_part",
        (normed, table),
        like((rows, width + lanes)),
        (rows // block,),
        [pl.BlockSpec((block, width), lambda i: (i, 0)), untouched],
        pl.BlockSpec((block, width + lanes), lambda i: (i, 0)),
        deps,
        (6 * rows * entries * width, 2 * entries * width),
        scratch=[pltpu.VMEM(table.shape, bf16), pltpu.SemaphoreType.DMA((len(cuts) - 1,))],
    )


def round_kernel(values_ref, out_ref):
    out_ref[...] = values_ref[...].astype(bf16)


def rounded(values, by_rows, *deps):
    latents = values.shape[0 if by_rows else 1]
    block = min(1024, latents)
    spec = row_block(block, values.shape[1]) if by_rows else column_block(values.shape[0], block)
    return call(
        round_kernel,
        "rounded",
        (values,),
        like(values.shape, bf16),
        (latents // block,),
        [spec],
        spec,
        deps,
        (0, 6 * values.size),
    )


def pieces_kernel(factor_ref, rows_ref, columns_ref):
    one, two, three = split_floats(factor_ref[...])
    rank, latents = one.shape
    rows_ref[...] = jnp.concatenate([one, two, three, jnp.zeros_like(one)], axis=0).astype(bf16)
    tall = jnp.concatenate([one, two, three, jnp.zeros((lanes - 3 * rank, latents), f32)], axis=0)
    columns_ref[...] = tall.T.astype(bf16)


def factor_pieces(factor, *deps):
    rank, latents = factor.shape
    block = min(1024, latents)
    return call(
        pieces_kernel,
        "factor_pieces",
        (factor,),
        (like((4 * rank, latents), bf16), like((latents, lanes), bf16)),
        (latents // block,),
        [column_block(rank, block)],
        (column_block(4 * rank, block), row_block(block, lanes)),
        deps,
        (0, 1024 * latents),
    )


def column_block(rows, block):
    return pl.BlockSpec((rows, block), lambda i: (0, i))


def row_block(block, width):
    return pl.BlockSpec((block, width), lambda i: (i, 0))


def whole_of(shape):
    return pl.BlockSpec(shape, lambda i: (0,) * len(shape))


def forward_kernel(inputs_ref, enc_ref, bias_ref, mask_ref, dec_ref, tops_ref, auxes_ref, part_ref):
    clear_at_start(part_ref)
    code = (dot(inputs_ref[...], enc_ref[...], contract_plain) + bias_ref[...]).astype(bf16)
    mask = mask_ref[...]
    nothing = jnp.zeros((), bf16)
    tops = jnp.where((mask == 1.0) | (mask == 3.0), code, nothing)
    tops_ref[...] = tops
    auxes_ref[...] = jnp.where(mask >= 2.0, code, nothing)
    part_ref[...] += dot(tops, dec_ref[...], contract_plain)


def forward(inputs, enc, bias, mask, dec, *deps):
    rows, width = inputs.shape
    latents = enc.shape[1]
    block = min(1024, latents)
    column = column_block(rows, block)
    return call(
        forward_kernel,
        "forward",
        (inputs, enc, bias, mask, dec),
        (like((rows, latents), bf16), like((rows, latents), bf16), like((rows, width))),
        (latents // block,),
        [whole_of((rows, width)), column_block(width, block), column_block(1, block), column, row_block(block, width)],
        (column, column, whole_of((rows, width))),
        deps,
        (4 * rows * latents * width, 2 * latents * (2 * width + 3 * rows)),
    )


def aux_forward_kernel(odd_ref, even_ref, dec_ref, out_ref, odd_sum, even_sum):
    clear_at_start(odd_sum, even_sum)
    odd_sum[...] += dot(odd_ref[...], dec_ref[...], contract_plain)
    even_sum[...] += dot(even_ref[...], dec_ref[...], contract_plain)

    @pl.when(pl.program_id(0) == pl.num_programs(0) - 1)
    def _():
        me, rows = lax.axis_index("lat"), out_ref.shape[1]
        for at, j in enumerate(even_order()):
            out_ref[me ^ j] = even_sum[at * rows : (at + 1) * rows, :]
            out_ref[me ^ (j ^ 1)] = odd_sum[at * rows : (at + 1) * rows, :]


def aux_forward(odd, even, dec, *deps):
    latents, width = dec.shape
    rows, count = odd.shape[0], lax.axis_size("lat")
    block = min(1024, latents)
    column, shape = column_block(rows, block), (count, 2 * rows // count, width)
    return call(
        aux_forward_kernel,
        "aux_forward",
        (odd, even, dec),
        like(shape),
        (latents // block,),
        [column, column, row_block(block, width)],
        whole_of(shape),
        deps,
        (4 * rows * latents * width, 2 * latents * (width + 2 * rows)),
        scratch=[pltpu.VMEM((rows, width), f32)] * 2,
    )


def aux_back_kernel(odd_ref, even_ref, dec_ref, odd_mask, even_mask, odd_out, even_out):
    dec = dec_ref[...]
    for grads, mask, out in ((odd_ref, odd_mask, odd_out), (even_ref, even_mask, even_out)):
        pulled = dot(grads[...], dec, contract_cols).astype(bf16)
        out[...] = jnp.where(mask[...] >= 2.0, pulled, jnp.zeros((), bf16))


def aux_back(odd, even, dec, odd_mask, even_mask, *deps):
    latents, width = dec.shape
    rows = odd.shape[0]
    block = min(1024, latents)
    column, whole = column_block(rows, block), whole_of((rows, width))
    return call(
        aux_back_kernel,
        "aux_back",
        (odd, even, dec, odd_mask, even_mask),
        (like((rows, latents), bf16),) * 2,
        (latents // block,),
        [whole, whole, row_block(block, width), column, column],
        (column, column),
        deps,
        (4 * rows * latents * width, 2 * latents * (width + 4 * rows)),
    )


def product_kernel(odd_ref, even_ref, factor_ref, odd_out, even_out):
    clear_at_start(odd_out, even_out)
    odd_out[...] += dot(odd_ref[...], factor_ref[...], contract_plain)
    even_out[...] += dot(even_ref[...], factor_ref[...], contract_plain)


def factor_products(odd, even, factor, *deps):
    rows, latents = odd.shape
    block = min(1024, latents)
    column, out = column_block(rows, block), whole_of((rows, lanes))
    return call(
        product_kernel,
        "factor_products",
        (odd, even, factor),
        (like((rows, lanes)),) * 2,
        (latents // block,),
        [column, column, row_block(block, lanes)],
        (out, out),
        deps,
        (4 * rows * latents * lanes, 4 * latents * rows),
    )


def add_left(ref, pieces, values, numbers):
    high, low = high_low(values)
    by_high, by_low = dot(pieces, high, numbers), dot(pieces, low, numbers)
    ref[...] += (by_high[:8] + by_high[8:16] + by_high[16:24]) + (by_low[:8] + by_low[8:16])


def err_left_kernel(pieces_ref, err_ref, out_ref):
    clear_at_start(out_ref)
    add_left(out_ref, pieces_ref[...], err_ref[...], contract_cols)


def err_left(pieces, err, *deps):
    width, latents = err.shape
    block = min(1024, latents)
    return call(
        err_left_kernel,
        "err_left",
        (pieces, err),
        like((8, width)),
        (latents // block,),
        [column_block(32, block), column_block(width, block)],
        whole_of((8, width)),
        deps,
        (128 * latents * width, 4 * latents * width),
    )


def part_dec_kernel(odd_codes, even_codes, odd_grads, even_grads, err_ref, pieces_ref, part_ref, left_ref):
    total = err_ref[...] + dot(odd_codes[...], odd_grads[...], contract_rows)
    total = total + dot(even_codes[...], even_grads[...], contract_rows)
    part_ref[...] = total
    clear_at_start(left_ref)
    add_left(left_ref, pieces_ref[...], total, contract_plain)


def part_dec(codes, grads, err, pieces, *deps):
    latents, width = err.shape
    rows = codes[0].shape[0]
    block = min(1024, latents)
    column, whole, big = column_block(rows, block), whole_of((rows, width)), row_block(block, width)
    return call(
        part_dec_kernel,
        "part_dec",
        (*codes, *grads, err, pieces),
        (like((latents, width)), like((8, width))),
        (latents // block,),
        [column, column, whole, whole, big, column_block(32, block)],
        (big, whole_of((8, width))),
        deps,
        (4 * rows * latents * width, latents * (8 * width + 4 * rows)),
    )


def add_dec_kernel(odd_codes, even_codes, odd_grads, even_grads, base_ref, out_ref):
    total = base_ref[...] + dot(odd_codes[...], odd_grads[...], contract_rows)
    out_ref[...] = total + dot(even_codes[...], even_grads[...], contract_rows)


def add_dec(codes, grads, base, part, parts, *deps):
    latents, width = base.shape
    rows = codes[0].shape[0]
    block = min(1024, latents // parts)
    steps = latents // parts // block
    column = pl.BlockSpec((rows, block), lambda i: (0, i + part * steps))
    big = pl.BlockSpec((block, width), lambda i: (i + part * steps, 0))
    whole = whole_of((rows, width))
    return call(
        add_dec_kernel,
        "add_dec",
        (*codes, *grads, base),
        like((latents, width)),
        (steps,),
        [column, column, whole, whole, big],
        big,
        deps,
        (4 * rows * latents * width // parts, latents * (8 * width + 4 * rows) // parts),
        aliases={4: 0},
    )


def form_enc_kernel(odd_inputs, even_inputs, odd_grads, even_grads, err_ref, out_ref):
    total = err_ref[...] + dot(odd_inputs[...], odd_grads[...], contract_rows)
    out_ref[...] = total + dot(even_inputs[...], even_grads[...], contract_rows)


def form_enc(inputs, grads, err, *deps):
    width, latents = err.shape
    rows = grads[0].shape[0]
    block = min(1024, latents)
    column, whole, big = column_block(rows, block), whole_of((rows, width)), column_block(width, block)
    return call(
        form_enc_kernel,
        "form_enc",
        (*inputs, *grads, err),
        like((width, latents)),
        (latents // block,),
        [whole, whole, column, column, big],
        big,
        deps,
        (4 * rows * latents * width, latents * (8 * width + 4 * rows)),
    )


def back_kernel(odd_ref, even_ref, dec_ref, enc_ref, odd_mask, even_mask, odd_aux, even_aux, factor_ref, *outs):
    odd_out, even_out, bias_ref, pull_ref, odd_sums, even_sums = outs
    dec, factor = dec_ref[...], factor_ref[...]
    clear_at_start(pull_ref, odd_sums, even_sums)
    nothing = jnp.zeros((), bf16)
    bias = None
    for grads, mask, aux, out, sums in (
        (odd_ref, odd_mask, odd_aux, odd_out, odd_sums),
        (even_ref, even_mask, even_aux, even_out, even_sums),
    ):
        pulled = dot(grads[...], dec, contract_cols).astype(bf16)
        mask = mask[...]
        total = jnp.where((mask == 1.0) | (mask == 3.0), pulled, nothing).astype(f32) + aux[...].astype(f32)
        column = jnp.sum(total, axis=0, keepdims=True)
        bias = column if bias is None else bias + column
        rounded = total.astype(bf16)
        out[...] = rounded
        sums[...] += dot(rounded, factor, contract_plain)
    bias_ref[...] = bias
    one, two, three = split_floats(bias)
    pieces = jnp.concatenate([one, two, three, jnp.zeros((13, bias.shape[1]), f32)], axis=0).astype(bf16)
    pull_ref[...] += dot(pieces, enc_ref[...], contract_cols)


def back_pass(odd, even, dec, enc, odd_mask, even_mask, odd_aux, even_aux, factor, *deps):
    latents, width = dec.shape
    rows = odd.shape[0]
    block = min(1024, latents)
    column, whole = column_block(rows, block), whole_of((rows, width))
    return call(
        back_kernel,
        "back_pass",
        (odd, even, dec, enc, odd_mask, even_mask, odd_aux, even_aux, factor),
        (
            like((rows, latents), bf16),
            like((rows, latents), bf16),
            like((1, latents)),
            like((16, width)),
            like((rows, lanes)),
            like((rows, lanes)),
        ),
        (latents // block,),
        [whole, whole, row_block(block, width), column_block(width, block)]
        + [column] * 4
        + [row_block(block, lanes)],
        (
            column,
            column,
            column_block(1, block),
            whole_of((16, width)),
            whole_of((rows, lanes)),
            whole_of((rows, lanes)),
        ),
        deps,
        (4 * rows * latents * (width + lanes), 2 * latents * (2 * width + 6 * rows)),
    )


def left_sums_kernel(
    rank,
    enc_odd,
    enc_even,
    odd_inputs,
    even_inputs,
    dec_odd,
    dec_even,
    odd_grads,
    even_grads,
    enc_base,
    dec_base,
    own_grads,
    pull_ref,
    loss_ref,
    out_ref,
):
    def against(products, inputs):
        total = None
        for piece in split_three(products[...]):
            wide = dot(piece, inputs[...], contract_rows)
            total = wide if total is None else total + wide
        return total[:rank] + total[rank : 2 * rank] + total[2 * rank : 3 * rank]

    out_ref[:rank, :] = enc_base[...] + against(enc_odd, odd_inputs) + against(enc_even, even_inputs)
    out_ref[rank : 2 * rank, :] = dec_base[...] + against(dec_odd, odd_grads) + against(dec_even, even_grads)
    bias = jnp.sum(own_grads[...].astype(f32), axis=0, keepdims=True)
    bias = bias - jnp.sum(pull_ref[...], axis=0, keepdims=True)
    index = lax.broadcasted_iota(jnp.int32, (8, bias.shape[1]), 0)
    out_ref[2 * rank :, :] = jnp.where(index == 0, bias, jnp.where(index == 1, jnp.sum(loss_ref[...], axis=1, keepdims=True), 0.0))


def ortho_kernel(rank, left_ref, enc_ref, dec_ref):
    def spread(rows):
        index = lax.broadcasted_iota(jnp.int32, rows.shape, 0)
        for i in range(rank):
            unit = rows[i : i + 1, :]
            unit = unit * lax.rsqrt(jnp.sum(unit * unit, axis=1, keepdims=True))
            along = jnp.sum(rows * unit, axis=1, keepdims=True)
            rows = jnp.where(index == i, unit, jnp.where(index > i, rows - along * unit, rows))
        one, two, three = split_floats(rows)
        return jnp.concatenate([one, one, two, two, one, three], axis=0).astype(bf16)

    enc_ref[...] = spread(left_ref[:rank, :])
    dec_ref[...] = spread(left_ref[rank : 2 * rank, :])


def orthonormal(left, rank):
    shape = jax.ShapeDtypeStruct((6 * rank, left.shape[1]), bf16)
    return pl.pallas_call(
        functools.partial(ortho_kernel, rank), out_shape=(shape, shape), name="orthonormal"
    )(left)


def right_kernel(numbers, rank, left_ref, full_ref, out_ref):
    high, low = high_low(full_ref[...])
    left = left_ref[...]
    by_high, by_low = dot(left, high, numbers), dot(left, low, numbers)
    one, two, three = slice(0, rank), slice(2 * rank, 3 * rank), slice(5 * rank, 6 * rank)
    total = by_high[one] + by_high[two] + by_high[three] + by_low[one] + by_low[two]
    out_ref[...] = total.astype(out_ref.dtype)


def right_part(left, full, by_rows, dtype, *deps):
    latents, width = full.shape if by_rows else full.shape[::-1]
    rank = left.shape[0] // 6
    block = min(1024, latents)
    return call(
        functools.partial(right_kernel, contract_cols if by_rows else contract_plain, rank),
        "right_part",
        (left, full),
        like((rank, latents), dtype),
        (latents // block,),
        [whole_of(left.shape), row_block(block, width) if by_rows else column_block(width, block)],
        column_block(rank, block),
        deps,
        (24 * rank * latents * width, 4 * latents * width),
    )


def stack_kernel(right_ref, bias_ref, out_ref):
    index = lax.broadcasted_iota(jnp.int32, right_ref.shape, 0)
    bias = jnp.where(index == 0, bias_ref[...], 0.0)
    out_ref[...] = jnp.concatenate([right_ref[...], bias], axis=0).astype(bf16)


def pieces_of_right(right):
    one, two, three = split_floats(right)
    return jnp.concatenate([one, two, one, two, three, one], axis=0).astype(bf16)


def enc_final_kernel(rep_count, left_ref, right_ref, full_ref, mom_ref, w_ref, w_out, mom_out, err_out):
    approx = dot(left_ref[...], pieces_of_right(right_ref[:8, :]), contract_rows)
    err_out[...] = full_ref[...] - approx * (1.0 / rep_count)
    mom = momentum_decay * mom_ref[...] + approx
    mom_out[...] = mom
    w_out[...] = w_ref[...] - rate_enc * mom


def dec_final_kernel(rep_count, left_ref, right_ref, full_ref, mom_ref, w_ref, w_out, mom_out, err_out):
    approx = dot(pieces_of_right(right_ref[:8, :]), left_ref[...], contract_rows)
    err_out[...] = full_ref[...] - approx * (1.0 / rep_count)
    mom = momentum_decay * mom_ref[...] + approx
    mom_out[...] = mom
    step = w_ref[...] - rate_dec * mom
    w_out[...] = step * lax.rsqrt(jnp.sum(step * step, axis=1, keepdims=True) + 1e-06)


def final_update(kernel, by_rows, rep_count, left, right, full, mom, weight, *deps):
    latents, width = right.shape[1], left.shape[1]
    block = min(1024, latents)
    big = row_block(block, width) if by_rows else column_block(width, block)
    return call(
        functools.partial(kernel, rep_count),
        "final_update",
        (left, right, full, mom, weight),
        (like(full.shape),) * 3,
        (latents // block,),
        [whole_of(left.shape), column_block(right.shape[0], block), big, big, big],
        (big, big, big),
        deps,
        (2 * 48 * latents * width, 24 * latents * width),
    )


def stack_weights_kernel(qkv_ref, out_ref, fc_ref, proj_ref, stacked_ref):
    share, width = out_ref.shape
    squares = [qkv_ref[:, k * width : (k + 1) * width] for k in range(3)] + [out_ref[...]]
    squares += [fc_ref[:, k * width : (k + 1) * width] for k in range(fc_ref.shape[1] // width)]
    for k, square in enumerate(squares):
        stacked_ref[k * share : (k + 1) * share, :] = square
    stacked_ref[len(squares) * share :, :] = proj_ref[...]


def stack_weights(w_qkv, w_out, w_fc, w_proj):
    share, width = w_out.shape
    rows = share * (4 + w_fc.shape[1] // width) + w_proj.shape[0]
    return call(stack_weights_kernel, "stack_weights", (w_qkv, w_out, w_fc, w_proj), like((rows, width), bf16))


def cut_kernel(four_ref, two_ref, top_ref, bottom_ref):
    rows = top_ref.shape[0]
    top_ref[...] = four_ref[:rows, :]
    bottom_ref[...] = two_ref[rows:, :]


def cut_weights(by_four, by_two, *deps):
    half = like((by_four.shape[0] // 2, by_four.shape[1]), bf16)
    return call(cut_kernel, "cut_weights", (by_four, by_two), (half, half), deps=deps)


def frozen_kernel(share, *refs):
    residual_ref, norm_ref, bias_ref, dec_bias_ref = refs[:4]
    count = refs[-2].shape[0]
    *pieces, stream_out, centered_out, orig_out, weights, sems = refs[4:]
    me = lax.axis_index("lat")
    total_rows, width = weights.shape[1:]
    hidden = (total_rows // share - 8) * share * count
    cuts = [0, 3 * share, total_rows // 2, total_rows]
    copies = [[] for _ in cuts[1:]]
    pieces = iter(pieces)
    for j in range(count):
        parts = [(next(pieces), 0)] * 3 if j & 6 != 6 else [(next(pieces), 0)] * 2 + [(next(pieces), total_rows // 2)]
        for k, (piece, start) in enumerate(parts):
            rows = cuts[k + 1] - cuts[k]
            copies[k].append(
                pltpu.make_async_copy(
                    piece.at[pl.ds(cuts[k] - start, rows), :],
                    weights.at[me ^ j, pl.ds(cuts[k], rows), :],
                    sems.at[k, j],
                )
            )
    for group in copies:
        for copy in group:
            copy.start()

    def square(k):
        return weights[:, k * share : (k + 1) * share, :].reshape(width, width)

    def norm(values, row):
        return layer_norm(values, norm_ref[row : row + 1, :], norm_ref[row + 1 : row + 2, :])

    def bias(k, count=1):
        return bias_ref[:, k * width : (k + count) * width]

    stream = residual_ref[...].astype(f32)
    normed = norm(stream, 0).astype(bf16)
    for copy in copies[0]:
        copy.wait()
    queries, keys, values = [
        (dot(normed, square(k), contract_plain) + bias(k)).astype(bf16) for k in range(3)
    ]
    seq_len = stream.shape[0]
    early = lax.broadcasted_iota(jnp.int32, (seq_len, lanes), 1) < width // HEADS
    causal = lax.broadcasted_iota(jnp.int32, (seq_len, seq_len), 0) >= lax.broadcasted_iota(
        jnp.int32, (seq_len, seq_len), 1
    )
    nothing = jnp.zeros((), bf16)
    attended = []
    for k in range(0, width, lanes):
        pair_q, pair_k, pair_v = (part[:, k : k + lanes] for part in (queries, keys, values))
        outs = []
        for is_early in (True, False):
            head_q = jnp.where(early == is_early, pair_q, nothing)
            scores = dot(head_q, pair_k, contract_cols) / math.sqrt(width // HEADS)
            scores = jnp.where(causal, scores, -1e30)
            grown = jnp.exp(scores - jnp.max(scores, axis=1, keepdims=True))
            share_of = (grown / jnp.sum(grown, axis=1, keepdims=True)).astype(bf16)
            outs.append(dot(share_of, pair_v, contract_plain))
        attended.append(jnp.where(early, outs[0], outs[1]).astype(bf16))
    attended = jnp.concatenate(attended, axis=1)
    for copy in copies[1]:
        copy.wait()
    stream = stream + dot(attended, square(3), contract_plain) + bias(3)
    normed = norm(stream, 2).astype(bf16)
    for copy in copies[2]:
        copy.wait()
    out = None
    for k in range(hidden // width):
        inner = dot(normed, square(4 + k), contract_plain) + bias(4 + k)
        activated = jax.nn.gelu(inner, approximate=True).astype(bf16)
        per = width // (hidden // weights.shape[0])
        block = weights[k * per : (k + 1) * per, 8 * share :, :].reshape(width, width)
        part = dot(activated, block, contract_plain)
        out = part if out is None else out + part
    stream = stream + out + bias(4 + hidden // width)
    stream_out[...] = stream
    centered_out[...] = (stream - dec_bias_ref[...]).astype(bf16)
    orig_out[...] = norm(stream, 4).astype(bf16)


def frozen_whole(residual, norm_params, biases, dec_bias, pieces, share, *deps):
    rows, width = residual.shape
    total, count = pieces[0].shape[0], 8
    return call(
        functools.partial(frozen_kernel, share),
        "frozen_block",
        (residual, norm_params, biases[None, :], dec_bias[None, :], *pieces),
        (like((rows, width)), like((rows, width), bf16), like((rows, width), bf16)),
        (),
        [in_vmem] * 4 + [untouched] * len(pieces),
        (in_vmem,) * 3,
        deps,
        (2 * rows * count * total * width, 2 * count * total * width),
        scratch=[pltpu.VMEM((count, total, width), bf16), pltpu.SemaphoreType.DMA((3, count))],
    )


def layer_norm(values, gain_row, shift_row):
    center = values - jnp.mean(values, axis=-1, keepdims=True)
    spread = jnp.mean(center * center, axis=-1, keepdims=True)
    return center * lax.rsqrt(spread + 1e-05) * gain_row + shift_row


def frozen_block(residual, norm_params, biases, qkv, w_out, fc, w_proj):
    seq_len = residual.shape[0]
    model_width = residual.shape[1]
    hidden_units = w_proj.shape[0]
    head_dim = model_width // HEADS
    stream = residual.astype(f32)
    normed = layer_norm(stream, norm_params[0], norm_params[1]).astype(bf16)

    def times(values, parts, bias):
        width = parts[0].shape[1]
        return [
            jnp.dot(values, part, preferred_element_type=f32) + bias[k * width : (k + 1) * width]
            for k, part in enumerate(parts)
        ]

    queries, keys, values = [
        part.astype(bf16).reshape(seq_len, HEADS, head_dim)
        for part in times(normed, qkv, biases[: 3 * model_width])
    ]
    scores = jnp.einsum("qhd,khd->hqk", queries, keys, preferred_element_type=f32) / math.sqrt(head_dim)
    causal = jnp.arange(seq_len)[:, None] >= jnp.arange(seq_len)[None, :]
    scores = jnp.where(causal, scores, -1e30)
    weights = jax.nn.softmax(scores, axis=-1).astype(bf16)
    attended = jnp.einsum("hqk,khd->qhd", weights, values, preferred_element_type=f32)
    attended = attended.astype(bf16).reshape(seq_len, model_width)
    stream = (
        stream
        + jnp.dot(attended, w_out, preferred_element_type=f32)
        + biases[3 * model_width : 4 * model_width]
    )
    normed = layer_norm(stream, norm_params[2], norm_params[3]).astype(bf16)
    inner_in = times(normed, fc, biases[4 * model_width : 4 * model_width + hidden_units])
    activated = jnp.concatenate(
        [jax.nn.gelu(part, approximate=True).astype(bf16) for part in inner_in], axis=1
    )
    return (
        stream
        + jnp.dot(activated, w_proj, preferred_element_type=f32)
        + biases[4 * model_width + hidden_units :]
    )


def per_device(
    residual,
    valid_mask,
    top_idx,
    aux_idx,
    dead_flags,
    norm_params,
    biases,
    w_qkv,
    w_out,
    w_fc,
    w_proj,
    head_table,
    w_enc,
    encoder_bias_vec,
    w_dec,
    decoder_bias_vec,
    mom_enc,
    mom_benc,
    mom_dec,
    mom_bdec,
    q_enc,
    q_dec,
    err_enc,
    err_dec,
):
    rep_count = lax.axis_size("rep")
    made_with.clear()
    lat_index = lax.axis_index("lat")
    model_width = residual.shape[1]
    hidden_units = w_fc.shape[1]
    lat_dev = w_enc.shape[1]
    top_count, aux_count = top_idx.shape[1], aux_idx.shape[1]
    rank = q_enc.shape[1]
    err_enc, err_dec = err_enc[0], err_dec[0]

    half = aux_count // 2
    valid_float = valid_mask.astype(f32)
    packed = jnp.concatenate(
        [
            aux_idx[:, :half] * pack_base + aux_idx[:, half:],
            top_idx,
            jnp.broadcast_to(-1 - valid_mask[:, None], (valid_mask.shape[0], lanes - top_count)),
        ],
        axis=1,
    )
    dead_pair = jnp.concatenate(
        [
            lax.dynamic_slice_in_dim(dead_flags, base * lat_dev, lat_dev)
            for base in (lat_index, lat_index ^ 1)
        ]
    ).astype(f32)[None, :]
    share = w_qkv.shape[0]
    by_piece = lax.axis_size("lat") == 8 and share % 16 == 0
    if by_piece:
        stacked = stack_weights(w_qkv, w_out, w_fc, w_proj)
        picks = Gather(packed)
        two_rows, four_rows = swap(stacked, "lat", 2), swap(stacked, "lat", 4)
        rows = packed.shape[0]
        masks, valid_0 = build_mask(packed, dead_pair, aux_count, top_count, 4 * rows, 3 * rows, deps=(stacked,))
        by_two, by_six, by_four, _ = picks.blocks
        masks, valid_1 = build_mask(
            by_two, dead_pair, aux_count, top_count, 4 * rows, 0, masks, deps=(by_six, by_four)
        )
        masks, valid_2 = build_mask(by_four, dead_pair, aux_count, top_count, 4 * rows, 2 * rows, masks)
        masks, valid_3 = build_mask(by_six, dead_pair, aux_count, top_count, 4 * rows, rows, masks)
        valid_total = valid_0 + valid_1 + valid_2 + valid_3
        top, bottom = cut_weights(four_rows, two_rows, masks[0])
        top, bottom = swap(top, "lat", 2), swap(bottom, "lat", 4)
        enc_weight = rounded(w_enc, False, masks[0])
        dec_weight = rounded(w_dec, True, enc_weight)
        q_enc_rows, q_enc_columns = factor_pieces(q_enc.T, dec_weight)
        left_enc = err_left(q_enc_rows, err_enc)
        top, bottom = pass_after(top, left_enc), pass_after(bottom, left_enc)
        pieces = []
        for piece in ((stacked,), (two_rows,), (four_rows,), (top, bottom)):
            pieces += [*piece, *(swap(part, "lat", 1) for part in piece)]
    else:
        joined = lax.all_gather(jnp.concatenate([w_qkv, w_out, w_fc], axis=1), "lat", axis=0, tiled=True)
        proj_all = lax.all_gather(w_proj, "lat", axis=0, tiled=True)
        squares = [joined[:, k : k + model_width] for k in range(0, joined.shape[1], model_width)]
        packed = gather_even(packed)
        masks, valid_total = build_mask(packed, dead_pair, aux_count, top_count, packed.shape[0], 0)
        enc_weight, dec_weight = rounded(w_enc, False), rounded(w_dec, True)
        q_enc_rows, q_enc_columns = factor_pieces(q_enc.T)
        left_enc = err_left(q_enc_rows, err_enc)
    mask_even, mask_partner = masks
    valid_total = sum_round(valid_total, "lat", [1])
    def final_norm(values):
        return layer_norm(values, norm_params[4], norm_params[5])

    if by_piece:
        stream, centered_own, orig_blocks = frozen_whole(
            residual,
            norm_params,
            biases,
            decoder_bias_vec,
            pieces,
            share,
            left_enc,
            valid_total,
        )
        mask_partner = pass_after(mask_partner, centered_own)
    else:
        stream = frozen_block(residual, norm_params, biases, squares[:3], squares[3], squares[4:], proj_all)
        centered_own = (stream - decoder_bias_vec).astype(bf16)
        orig_blocks = final_norm(stream).astype(bf16)
    gather = Gather(centered_own)
    mask_odd = swap(mask_partner, "lat", 1)
    valid_total = sum_round(pass_after(valid_total, centered_own), "rep", bits_of("rep"))
    weight_own = (valid_float / valid_total[0, 0])[:, None]
    q_dec_rows, q_dec_columns = factor_pieces(q_dec.T, valid_total)
    centered = gather.end(q_dec_rows)

    bias_row = encoder_bias_vec[None, :]
    tops_odd, auxes_odd, top_odd = forward(
        centered[1], enc_weight, bias_row, mask_odd, dec_weight, q_dec_rows
    )
    rebuilt = Scatter(top_odd)
    tops_even, auxes_even, top_even = forward(centered[0], enc_weight, bias_row, mask_even, dec_weight, top_odd)
    sent = rebuilt.chip(top_even)
    aux_part = aux_forward(auxes_odd, auxes_even, dec_weight, sent)
    auxiliary_rebuilt = lax.psum_scatter(aux_part, "lat", scatter_dimension=0, tiled=False)
    orig_group = gather_behind(orig_blocks, aux_part)
    rebuilt_input = rebuilt.last(orig_group[0]) + decoder_bias_vec
    rec_float, norm_back = jax.vjp(final_norm, rebuilt_input)
    gather = Gather(rec_float.astype(bf16))
    orig_odd = head_part(orig_group[1], head_table, gather.own)
    rec_group = gather.end(orig_odd)
    orig_mean = Scatter(pass_after(orig_odd, rec_group[0]), lanes)
    orig_even = head_part(orig_group[0], head_table, rec_group[0])
    sent = orig_mean.chip(orig_even)
    rec_odd = head_part(rec_group[1], head_table, sent)
    orig_mean = orig_mean.last(rec_odd)
    rec_odd = pass_after(rec_odd, orig_mean)
    rec_mean = Scatter(rec_odd, lanes)
    aux_pull, aux_blocks, err_square = residual_pull(
        stream, rebuilt_input, auxiliary_rebuilt, weight_own, orig_mean
    )
    rec_even = head_part(rec_group[0], head_table, aux_blocks)
    sent = rec_mean.chip(rec_even)

    products_dec = factor_products(tops_odd, tops_even, q_dec_columns, sent)
    aux_group = gather_behind(aux_blocks, products_dec[0])
    pre_odd, pre_even = aux_back(aux_group[1], aux_group[0], dec_weight, mask_odd, mask_even)
    rec_mean = rec_mean.last(pre_odd)

    orig_lse, rec_lse = orig_mean[:, model_width], rec_mean[:, model_width]
    orig_mean, rec_mean = orig_mean[:, :model_width], rec_mean[:, :model_width]
    (grad_head,) = norm_back(weight_own * (rec_mean - orig_mean))
    grad_recon = (grad_head + aux_pull).astype(bf16)
    gather = Gather(grad_recon)
    dec_part, left_dec = part_dec(
        (auxes_odd, auxes_even), (aux_group[1], aux_group[0]), err_dec, q_dec_rows, grad_recon
    )
    recon_group = gather.end(dec_part)
    gap = orig_blocks.astype(f32) - rec_float.astype(bf16).astype(f32)
    kl_own = jnp.sum(gap * orig_mean, axis=1) - orig_lse + rec_lse
    loss_tokens = (valid_float * (kl_own + aux_weight * err_square[:, 0]))[None, :]

    pre_odd, pre_even, grad_benc, bias_pull, enc_odd, enc_even = back_pass(
        recon_group[1],
        recon_group[0],
        dec_weight,
        enc_weight,
        mask_odd,
        mask_even,
        pre_odd,
        pre_even,
        q_enc_columns,
    )
    small = call(
        functools.partial(left_sums_kernel, rank),
        "left_sums",
        (
            enc_odd,
            enc_even,
            centered[1],
            centered[0],
            *products_dec,
            recon_group[1],
            recon_group[0],
            left_enc,
            left_dec,
            grad_recon,
            bias_pull,
            loss_tokens,
        ),
        like((2 * rank + 8, model_width)),
    )
    codes, grads = (tops_odd, tops_even), (recon_group[1], recon_group[0])
    full_dec = add_dec(codes, grads, dec_part, 0, 2, small)
    small = sum_round(small, "lat", [1])
    full_dec = add_dec(codes, grads, full_dec, 1, 2, small)
    small = sum_round(small, "lat", bits_of("lat")[1:])
    full_enc = form_enc((centered[1], centered[0]), (pre_odd, pre_even), err_enc, small, full_dec)
    small = sum_round(small, "rep", bits_of("rep"))
    grad_bdec, loss_sum = small[2 * rank], small[2 * rank + 1, 0]

    ortho_enc, ortho_dec = orthonormal(small[: 2 * rank], rank)
    right_enc = right_part(ortho_enc, full_enc, False, bf16)
    right_dec = right_part(ortho_dec, full_dec, True, f32, right_enc)
    right_enc = sum_round(right_enc, "rep", bits_of("rep"), sent_as=bf16)
    right_dec = call(
        stack_kernel, "stack", (right_dec, grad_benc), like((2 * rank, lat_dev), bf16), deps=(right_enc,)
    )
    right_dec = sum_round(right_dec, "rep", bits_of("rep"), sent_as=bf16)
    grad_benc = right_dec[rank]

    w_enc_new, mom_enc_new, err_enc_new = final_update(
        enc_final_kernel, False, rep_count, ortho_enc, right_enc, full_enc, mom_enc, w_enc
    )
    w_dec_new, mom_dec_new, err_dec_new = final_update(
        dec_final_kernel, True, rep_count, ortho_dec, right_dec, full_dec, mom_dec, w_dec, w_enc_new
    )
    mom_benc_new = momentum_decay * mom_benc + grad_benc
    mom_bdec_new = momentum_decay * mom_bdec + grad_bdec
    b_enc_new = encoder_bias_vec - rate_benc * mom_benc_new
    b_dec_new = decoder_bias_vec - rate_bdec * mom_bdec_new
    return (
        loss_sum,
        valid_total[0, 0],
        w_enc_new,
        b_enc_new,
        w_dec_new,
        b_dec_new,
        mom_enc_new,
        mom_benc_new,
        mom_dec_new,
        mom_bdec_new,
        right_enc.T,
        right_dec[:rank].T,
        err_enc_new[None],
        err_dec_new[None],
    )


def solution(mesh):
    in_specs = (
        P(("rep", "lat"), None),
        P(("rep", "lat")),
        P(("rep", "lat"), None),
        P(("rep", "lat"), None),
        P(),
        P(),
        P(),
        P("lat", None),
        P("lat", None),
        P("lat", None),
        P("lat", None),
        P("lat", None),
        P(None, "lat"),
        P("lat"),
        P("lat", None),
        P(),
        P(None, "lat"),
        P("lat"),
        P("lat", None),
        P(),
        P("lat", None),
        P("lat", None),
        P("rep", None, "lat"),
        P("rep", "lat", None),
    )
    out_specs = (
        P(),
        P(),
        P(None, "lat"),
        P("lat"),
        P("lat", None),
        P(),
        P(None, "lat"),
        P("lat"),
        P("lat", None),
        P(),
        P("lat", None),
        P("lat", None),
        P("rep", None, "lat"),
        P("rep", "lat", None),
    )
    return jax.shard_map(
        per_device, mesh=mesh, in_specs=in_specs, out_specs=out_specs, check_vma=False
    )
```

```python
import functools
import math

import jax
import jax.numpy as jnp
from jax import lax
from jax.experimental import pallas as pl
from jax.experimental.pallas import tpu as pltpu
from jax.sharding import PartitionSpec as P

HEADS = 12
HEAD_PARTS = (3, 13)

pack_base = 32768
aux_weight = 1.0 / 32.0
momentum_decay = 0.9
rate_enc = 3000.0
rate_dec = 3000.0
rate_benc = 10000.0
rate_bdec = 500.0
lanes = 128
rooms = {
    "usual": 16,
    "head_part": 44,
    "forward": 60,
    "aux_forward": 60,
    "stack_weights": 60,
    "frozen_block": 30,
    "final_update": 52,
    "back_pass": 40,
    "add_dec": 36,
    "form_enc": 36,
    "part_dec": 60,
    "aux_back": 60,
    "err_left": 60,
    "right_part": 60,
    "cut_weights": 20,
    "rounded": 60,
    "factor_products": 24,
}
contract_cols = (((1,), (1,)), ((), ()))
contract_rows = (((0,), (0,)), ((), ()))
contract_plain = (((1,), (0,)), ((), ()))
f32 = jnp.float32
bf16 = jnp.bfloat16


def swap(values, axis, bit):
    count = lax.axis_size(axis)
    return lax.ppermute(values, axis, [(i, i ^ bit) for i in range(count)])


def bits_of(axis):
    count = lax.axis_size(axis)
    return [1 << k for k in range(count.bit_length() - 1)]


def even_order():
    count = lax.axis_size("lat")
    return [2, 6, 4, 0] if count == 8 else list(range(count - 2, -1, -2))


def gather_even(own):
    if lax.axis_size("lat") == 8:
        half = own.shape[0] // 2
        by_two, by_four = swap(own, "lat", 2), swap(own, "lat", 4)
        return jnp.concatenate(
            [by_two, swap(by_four[:half], "lat", 2), swap(by_two[half:], "lat", 4), by_four, own], axis=0
        )
    blocks = {0: own}
    for bit in bits_of("lat")[1:]:
        order = sorted(blocks)
        moved = swap(jnp.stack([blocks[j] for j in order]), "lat", bit)
        for at, j in enumerate(order):
            blocks[j ^ bit] = moved[at]
    return jnp.concatenate([blocks[j] for j in even_order()], axis=0)


def gather_tokens(own):
    even = gather_even(own)
    return even, swap(even, "lat", 1)


def scatter_paths():
    others = bits_of("lat")[1:]
    if len(others) == 2:
        return [(0, 2, others), (1, 2, others[::-1])]
    return [(0, 1, others)]


def take_blocks(values, part, parts):
    rows, width = values.shape[0] // len(even_order()), values.shape[1] // parts
    return {
        j: values[at * rows : (at + 1) * rows, part * width : (part + 1) * width]
        for at, j in enumerate(even_order())
    }


def scatter_sum(even, odd_moved):
    chip = even + odd_moved
    done = []
    for part, parts, order in scatter_paths():
        held = take_blocks(chip, part, parts)
        for bit in order:
            sent = [j for j in even_order() if j in held and j & bit]
            got = swap(jnp.concatenate([held[j] for j in sent], axis=0).astype(bf16), "lat", bit)
            rows = held[0].shape[0]
            for at, j in enumerate(sent):
                held[j ^ bit] = held[j ^ bit] + got[at * rows : (at + 1) * rows].astype(f32)
                del held[j]
        done.append(held[0])
    return jnp.concatenate(done, axis=1)


def merge(mean_a, lse_a, mean_b, lse_b):
    top = jnp.maximum(lse_a, lse_b)
    exp_a, exp_b = jnp.exp(lse_a - top), jnp.exp(lse_b - top)
    total = exp_a + exp_b
    mixed = mean_a.astype(f32) * (exp_a / total) + mean_b.astype(f32) * (exp_b / total)
    return mixed, top + jnp.log(total)


def scatter_mean(even, even_lse, odd_moved, odd_lse_moved):
    chip, chip_lse = merge(even, even_lse, odd_moved, odd_lse_moved)
    done = []
    for part, parts, order in scatter_paths():
        means, lses = take_blocks(chip, part, parts), take_blocks(chip_lse, 0, 1)
        held = {j: (means[j], lses[j]) for j in means}
        for bit in order:
            sent = [j for j in even_order() if j in held and j & bit]
            rows = held[0][0].shape[0]
            got = swap(jnp.concatenate([held[j][0] for j in sent], axis=0).astype(bf16), "lat", bit)
            got_lse = swap(jnp.concatenate([held[j][1] for j in sent], axis=0), "lat", bit)
            for at, j in enumerate(sent):
                span = slice(at * rows, (at + 1) * rows)
                held[j ^ bit] = merge(*held[j ^ bit], got[span], got_lse[span])
                del held[j]
        done.append(held[0])
    return jnp.concatenate([mean for mean, _ in done], axis=1), done[0][1]


def sum_round(values, axis, bits, sent_as=None):
    if sent_as is not None:
        values = values.astype(sent_as)
    if len(bits) == 2:
        one, two, both = (swap(values, axis, bit) for bit in (bits[0], bits[1], bits[0] | bits[1]))
        return (values.astype(f32) + one.astype(f32)) + (two.astype(f32) + both.astype(f32))
    for bit in bits:
        values = values.astype(f32) + swap(values, axis, bit).astype(f32)
    return values


untouched = pl.BlockSpec(memory_space=pl.ANY)
in_vmem = pl.BlockSpec(memory_space=pltpu.VMEM)


def dot(a, b, numbers):
    return lax.dot_general(a, b, numbers, preferred_element_type=f32)


made_with = []


def marker(value):
    for made, small in made_with:
        if made is value:
            return small
    return value


def call(kernel, name, args, out_shape, grid=(), in_specs=None, out_specs=None, deps=(), cost=(0, 0), aliases=None, scratch=()):
    deps = [marker(dep) for dep in deps]
    count, skipped = len(args), len(deps)
    single = not isinstance(out_shape, (tuple, list))
    out_shapes = [out_shape] if single else list(out_shape)
    if in_specs is None:
        in_specs, out_specs = [in_vmem] * count, [in_vmem] * len(out_shapes)
    else:
        out_specs = [out_specs] if single else list(out_specs)
    results = len(out_shapes)

    def body(*refs):
        own = refs[count + skipped :]
        kernel(*refs[:count], *own[:results], *own[results + 1 :])

    flops, moved = cost
    *outs, small = pl.pallas_call(
        body,
        out_shape=out_shapes + [like((8, lanes))],
        grid=grid,
        in_specs=list(in_specs) + [untouched] * skipped,
        out_specs=out_specs + [untouched],
        scratch_shapes=list(scratch),
        input_output_aliases=aliases or {},
        compiler_params=pltpu.CompilerParams(vmem_limit_bytes=rooms.get(name, rooms["usual"]) * 2**20),
        cost_estimate=pl.CostEstimate(flops=flops, bytes_accessed=moved, transcendentals=0),
        name=name,
    )(*args, *deps)
    made_with.extend((out, small) for out in outs)
    return outs[0] if single else outs


def like(shape, dtype=f32):
    return jax.ShapeDtypeStruct(shape, dtype)


def clear_at_start(*refs):
    @pl.when(pl.program_id(0) == 0)
    def _():
        for ref in refs:
            ref[...] = jnp.zeros_like(ref)


def mask_kernel(tokens, hi_count, aux_count, top_count, *refs):
    packed = refs[0][...]
    dead_ref, own_ref, partner_ref, valid_ref, ids_ref, top_ref, scratch = refs[1], *refs[-6:]
    me, lat_dev = lax.axis_index("lat"), hi_count * lanes
    half, rows = aux_count // 2, 2 * hi_count

    def placed(ids):
        from_own, from_partner = ids - me * lat_dev, ids - (me ^ 1) * lat_dev
        return jnp.where(
            (from_own >= 0) & (from_own < lat_dev),
            from_own,
            jnp.where((from_partner >= 0) & (from_partner < lat_dev), from_partner + lat_dev, -(2**20)),
        )

    ids_ref[:, :half] = placed(packed[:, :half] >> 15)
    ids_ref[:, half:] = placed(packed[:, :half] & (pack_base - 1))
    joint_count = lanes // top_count
    tops = packed[:, half:]
    lane = lax.broadcasted_iota(jnp.int32, tops.shape, 1)
    repeated = tops
    for k in range(1, joint_count):
        repeated = jnp.where(lane // top_count == k, pltpu.roll(tops, k * top_count, 1), repeated)
    top_ref[...] = placed(repeated) + (lane // top_count) * (rows * lanes)
    counted = jnp.where(lane == top_count, -1 - tops, 0).astype(f32)
    valid = jnp.sum(jnp.sum(counted, axis=0, keepdims=True), axis=1, keepdims=True)
    clear_at_start(valid_ref)
    valid_ref[...] += jnp.broadcast_to(valid, valid_ref.shape)

    def hot(count, width, index):
        return jnp.where(lax.broadcasted_iota(jnp.int32, (count, width), 0) == index, 1.0, 0.0).astype(jnp.float8_e4m3fn)

    def some_tokens(group, carry):
        base = group * joint_count
        for k in range(joint_count):
            row = ids_ref[pl.ds(base + k, 1), :]
            picked = dot(hot(rows, aux_count, row >> 7), hot(lanes, aux_count, row & 127), contract_cols)
            scratch[pl.ds(pl.multiple_of((base + k) * rows, rows), rows), :] = 2.0 * picked
        joint_row = top_ref[pl.ds(base, 1), :]
        for k in range(1, joint_count):
            joint_row = jnp.where(lane[:1] // top_count == k, top_ref[pl.ds(base + k, 1), :], joint_row)
        picked = dot(hot(joint_count * rows, lanes, joint_row >> 7), hot(lanes, lanes, joint_row & 127), contract_cols)
        scratch[pl.ds(pl.multiple_of(base * rows, rows), joint_count * rows), :] += picked
        return carry

    lax.fori_loop(0, tokens // joint_count, some_tokens, 0, unroll=4)
    for hi in range(2 * hi_count):
        code = scratch[pl.ds(hi, tokens, stride=2 * hi_count), :]
        aux = jnp.where(code >= 2.0, 2.0, 0.0)
        code = (code - aux + aux * dead_ref[:, hi * lanes : (hi + 1) * lanes]).astype(bf16)
        if hi < hi_count:
            own_ref[:, hi * lanes : (hi + 1) * lanes] = code
        else:
            partner_ref[:, (hi - hi_count) * lanes : (hi - hi_count + 1) * lanes] = code


def pack_kernel(aux_ref, top_ref, valid_ref, out_ref):
    half = aux_ref.shape[1] // 2
    out_ref[:, :half] = aux_ref[:, :half] * pack_base + aux_ref[:, half:]
    rest = (lanes - top_ref.shape[0], top_ref.shape[1])
    out_ref[:, half:] = jnp.concatenate([top_ref[...], jnp.broadcast_to(-1 - valid_ref[...], rest)], axis=0).T


def pack_picks(aux_idx, top_rows, valid_row):
    shape = (aux_idx.shape[0], aux_idx.shape[1] // 2 + lanes)
    return call(pack_kernel, "pack_picks", (aux_idx, top_rows, valid_row), like(shape, jnp.int32))


def build_mask(packed, dead_pair, aux_count, top_count, rows, first, so_far=(), deps=()):
    width = packed.shape[1]
    lat_dev = dead_pair.shape[1] // 2
    hi_count, tokens = lat_dev // lanes, 64
    steps = packed.shape[0] // tokens
    out_block = pl.BlockSpec((tokens, lat_dev), lambda i: (i + first // tokens, 0))
    *masks, valid = call(
        functools.partial(mask_kernel, tokens, hi_count, aux_count, top_count),
        "build_mask",
        (packed, dead_pair, *so_far),
        (like((rows, lat_dev), bf16), like((rows, lat_dev), bf16), like((1, lanes))),
        (steps,),
        [row_block(tokens, width), whole_of((1, 2 * lat_dev))] + [untouched] * len(so_far),
        (out_block, out_block, whole_of((1, lanes))),
        deps,
        (16 * steps * tokens * 2 * lat_dev * aux_count, 4 * steps * tokens * lat_dev),
        aliases={2 + k: k for k in range(len(so_far))},
        scratch=[
            pltpu.VMEM((tokens, aux_count), jnp.int32),
            pltpu.VMEM((tokens, lanes), jnp.int32),
            pltpu.VMEM((tokens * 2 * hi_count, lanes), f32),
        ],
    )
    return masks, valid


def pass_kernel(in_ref, out_ref):
    pass


def pass_after(value, *deps):
    return call(
        pass_kernel, "pass_after", (value,), like(value.shape, value.dtype), (), [untouched], untouched, deps, aliases={0: 0}
    )


def split_three(values):
    first = values.astype(bf16)
    rest = values - first.astype(f32)
    second = rest.astype(bf16)
    return first, second, (rest - second.astype(f32)).astype(bf16)


def split_floats(values):
    return [piece.astype(f32) for piece in split_three(values)]


def residual_kernel(weight, stream_ref, rebuilt_ref, aux_ref, weight_ref, pull_ref, rounded_ref, square_ref):
    err = stream_ref[...] - rebuilt_ref[...] - aux_ref[...]
    pull = -(2.0 * weight) * weight_ref[...] * err
    pull_ref[...] = pull
    rounded_ref[...] = pull.astype(bf16)
    square_ref[...] = jnp.sum(err * err, axis=1, keepdims=True)


def residual_pull(stream, rebuilt, aux, weight_own, *deps):
    shape = stream.shape
    return call(
        functools.partial(residual_kernel, aux_weight),
        "residual_pull",
        (stream, rebuilt, aux, weight_own),
        (like(shape), like(shape, bf16), like((shape[0], 1))),
        deps=deps,
    )


def high_low(values):
    high = values.astype(bf16)
    return high, (values - high.astype(f32)).astype(bf16)


def assemble_kernel(*refs):
    *blocks, even_ref = refs
    rows = blocks[0].shape[0]
    for at, block in enumerate(blocks):
        even_ref[at * rows : (at + 1) * rows, :] = block[...]


class Gather:
    def __init__(self, own):
        self.own, self.plain = own, lax.axis_size("lat") != 8
        if not self.plain:
            self.blocks = [swap(own, "lat", j) if j else own for j in even_order()]

    def end(self, *deps):
        if self.plain:
            return gather_tokens(self.own)
        rows, width = self.own.shape
        even = call(assemble_kernel, "assemble", self.blocks, like((4 * rows, width), self.own.dtype), deps=deps)
        return even, swap(even, "lat", 1)


def reorder_kernel(blocks_ref, even_ref, odd_ref):
    me, rows = lax.axis_index("lat"), blocks_ref.shape[1]
    for at, j in enumerate(even_order()):
        even_ref[at * rows : (at + 1) * rows, :] = blocks_ref[me ^ j]
        odd_ref[at * rows : (at + 1) * rows, :] = blocks_ref[me ^ (j ^ 1)]


def gather_behind(own, *deps):
    blocks = lax.all_gather(own, "lat", axis=0)
    count, rows, width = blocks.shape
    half = like((count // 2 * rows, width), own.dtype)
    return call(reorder_kernel, "reorder", (blocks,), (half, half), deps=deps)


def joint(parts, tail):
    if not tail:
        return sum(parts[1:], parts[0])
    lses = [part[:, -tail:] for part in parts]
    top = functools.reduce(jnp.maximum, lses)
    weights = [jnp.exp(lse - top) for lse in lses]
    total = sum(weights[1:], weights[0])
    means = [part[:, :-tail] * (weight / total)[:, :1] for part, weight in zip(parts, weights)]
    return jnp.concatenate([sum(means[1:], means[0]), top + jnp.log(total)], axis=1)


def to_send(values, tail):
    if not tail:
        return values.astype(bf16)
    lane = lax.broadcasted_iota(jnp.int32, (values.shape[0], tail), 1)
    one, two, three = split_floats(values[:, -tail:])
    logs = jnp.where(lane < 32, one, jnp.where(lane < 64, two, three))
    return jnp.concatenate([values[:, :-tail], logs], axis=1).astype(bf16)


def received(ref, tail):
    values = ref[...].astype(f32)
    if not tail:
        return values
    logs = values[:, -tail:]
    lse = logs[:, :1] + logs[:, 32:33] + logs[:, 64:65]
    return jnp.concatenate([values[:, :-tail], jnp.broadcast_to(lse, logs.shape)], axis=1)


def chip_kernel(tail, even_ref, odd_ref, *outs):
    rows = outs[0].shape[0]
    for at, out in enumerate(outs):
        span = slice(at * rows, (at + 1) * rows)
        total = joint([even_ref[span, :], odd_ref[span, :]], tail)
        out[...] = total if at == len(outs) - 1 else to_send(total, tail)


def last_kernel(tail, *refs):
    *got, keep, total_ref = refs
    total_ref[...] = joint([keep[...]] + [received(ref, tail) for ref in got], tail)


class Scatter:
    def __init__(self, odd, tail=0):
        self.moved, self.tail, self.plain = swap(odd, "lat", 1), tail, lax.axis_size("lat") != 8

    def chip(self, even, *deps):
        self.even = even
        if self.plain:
            return even
        rows, width = even.shape[0] // 4, even.shape[1]
        shapes = [like((rows, width), bf16)] * 3 + [like((rows, width))]
        *sends, keep = call(
            functools.partial(chip_kernel, self.tail), "chip_sum", (even, self.moved), shapes, deps=deps
        )
        self.pending = [swap(send, "lat", j) for send, j in zip(sends, even_order())] + [keep]
        return keep

    def last(self, *deps):
        if self.plain:
            if not self.tail:
                return scatter_sum(self.even, self.moved)
            width = self.even.shape[1] - self.tail
            mean, lse = scatter_mean(
                self.even[:, :width], self.even[:, width : width + 1], self.moved[:, :width], self.moved[:, width : width + 1]
            )
            return jnp.concatenate([mean, jnp.broadcast_to(lse, (lse.shape[0], self.tail))], axis=1)
        return call(
            functools.partial(last_kernel, self.tail), "last_sum", self.pending, like(self.pending[-1].shape), deps=deps
        )


def head_kernel(cuts, steps, normed_ref, table_hbm, out_ref, table_ref, sems):
    def piece(c):
        span = pl.ds(cuts[c], cuts[c + 1] - cuts[c])
        return pltpu.make_async_copy(table_hbm.at[span, :], table_ref.at[span, :], sems.at[c])

    def at_start(action):
        if steps == 1:
            action()
        else:
            pl.when(pl.program_id(0) == 0)(action)

    chunks = len(cuts) - 1
    at_start(lambda: [piece(c).start() for c in range(chunks)] and None)
    normed = normed_ref[...]

    def logits_of(c):
        at_start(lambda: piece(c).wait())
        return dot(normed, table_ref[cuts[c] : cuts[c + 1], :], contract_cols)

    def fold(values, op):
        folded = values[:, :lanes]
        for k in range(lanes, values.shape[1], lanes):
            folded = op(folded, values[:, k : k + lanes])
        return folded

    top = total = mean = None
    logits = logits_of(0)
    for c in range(chunks):
        later = logits_of(c + 1) if c + 1 < chunks else None
        chunk_top = jnp.max(fold(logits, jnp.maximum), axis=1, keepdims=True)
        new_top = chunk_top if top is None else jnp.maximum(top, chunk_top)
        grown = jnp.exp(logits - new_top).astype(bf16)
        chunk_total = fold(grown.astype(f32), jnp.add)
        chunk_mean = dot(grown, table_ref[cuts[c] : cuts[c + 1], :], contract_plain)
        if top is None:
            total, mean = chunk_total, chunk_mean
        else:
            shrink = jnp.exp(top - new_top)
            total, mean = total * shrink + chunk_total, mean * shrink + chunk_mean
        top, logits = new_top, later
    total = jnp.sum(total, axis=1, keepdims=True)
    width = mean.shape[1]
    out_ref[:, :width] = mean / total
    out_ref[:, width:] = jnp.broadcast_to(top + jnp.log(total), (mean.shape[0], lanes))


def head_cuts(entries):
    unit = 256 if entries % 256 == 0 else lanes
    tiles = entries // unit
    ends = sorted({max(1, tiles * part // 26) for part in HEAD_PARTS} | {tiles})
    return [0] + [unit * end for end in ends]


def head_part(normed, table, *deps):
    rows, width = normed.shape
    entries = table.shape[0]
    block = min(512, rows)
    cuts = head_cuts(entries)
    return call(
        functools.partial(head_kernel, cuts, rows // block),
        "head_part",
        (normed, table),
        like((rows, width + lanes)),
        (rows // block,),
        [pl.BlockSpec((block, width), lambda i: (i, 0)), untouched],
        pl.BlockSpec((block, width + lanes), lambda i: (i, 0)),
        deps,
        (6 * rows * entries * width, 2 * entries * width),
        scratch=[pltpu.VMEM(table.shape, bf16), pltpu.SemaphoreType.DMA((len(cuts) - 1,))],
    )


def round_kernel(values_ref, out_ref):
    out_ref[...] = values_ref[...].astype(bf16)


def rounded(values, by_rows, *deps):
    latents = values.shape[0 if by_rows else 1]
    block = min(1024, latents)
    spec = row_block(block, values.shape[1]) if by_rows else column_block(values.shape[0], block)
    return call(
        round_kernel,
        "rounded",
        (values,),
        like(values.shape, bf16),
        (latents // block,),
        [spec],
        spec,
        deps,
        (0, 6 * values.size),
    )


def pieces_kernel(factor_ref, rows_ref, columns_ref):
    one, two, three = split_floats(factor_ref[...])
    rank, latents = one.shape
    rows_ref[...] = jnp.concatenate([one, two, three, jnp.zeros_like(one)], axis=0).astype(bf16)
    tall = jnp.concatenate([one, two, three, jnp.zeros((lanes - 3 * rank, latents), f32)], axis=0)
    columns_ref[...] = tall.T.astype(bf16)


def factor_pieces(factor, *deps):
    rank, latents = factor.shape
    block = min(1024, latents)
    return call(
        pieces_kernel,
        "factor_pieces",
        (factor,),
        (like((4 * rank, latents), bf16), like((latents, lanes), bf16)),
        (latents // block,),
        [column_block(rank, block)],
        (column_block(4 * rank, block), row_block(block, lanes)),
        deps,
        (0, 1024 * latents),
    )


def column_block(rows, block):
    return pl.BlockSpec((rows, block), lambda i: (0, i))


def row_block(block, width):
    return pl.BlockSpec((block, width), lambda i: (i, 0))


def whole_of(shape):
    return pl.BlockSpec(shape, lambda i: (0,) * len(shape))


def forward_kernel(inputs_ref, enc_ref, bias_ref, mask_ref, dec_ref, tops_ref, auxes_ref, part_ref):
    clear_at_start(part_ref)
    code = (dot(inputs_ref[...], enc_ref[...], contract_plain) + bias_ref[...]).astype(bf16)
    mask = mask_ref[...]
    nothing = jnp.zeros((), bf16)
    tops = jnp.where((mask == 1.0) | (mask == 3.0), code, nothing)
    tops_ref[...] = tops
    auxes_ref[...] = jnp.where(mask >= 2.0, code, nothing)
    part_ref[...] += dot(tops, dec_ref[...], contract_plain)


def forward(inputs, enc, bias, mask, dec, *deps):
    rows, width = inputs.shape
    latents = enc.shape[1]
    block = min(1024, latents)
    column = column_block(rows, block)
    return call(
        forward_kernel,
        "forward",
        (inputs, enc, bias, mask, dec),
        (like((rows, latents), bf16), like((rows, latents), bf16), like((rows, width))),
        (latents // block,),
        [whole_of((rows, width)), column_block(width, block), column_block(1, block), column, row_block(block, width)],
        (column, column, whole_of((rows, width))),
        deps,
        (4 * rows * latents * width, 2 * latents * (2 * width + 3 * rows)),
    )


def aux_forward_kernel(odd_ref, even_ref, dec_ref, out_ref, odd_sum, even_sum):
    clear_at_start(odd_sum, even_sum)
    odd_sum[...] += dot(odd_ref[...], dec_ref[...], contract_plain)
    even_sum[...] += dot(even_ref[...], dec_ref[...], contract_plain)

    @pl.when(pl.program_id(0) == pl.num_programs(0) - 1)
    def _():
        me, rows = lax.axis_index("lat"), out_ref.shape[1]
        for at, j in enumerate(even_order()):
            out_ref[me ^ j] = even_sum[at * rows : (at + 1) * rows, :]
            out_ref[me ^ (j ^ 1)] = odd_sum[at * rows : (at + 1) * rows, :]


def aux_forward(odd, even, dec, *deps):
    latents, width = dec.shape
    rows, count = odd.shape[0], lax.axis_size("lat")
    block = min(1024, latents)
    column, shape = column_block(rows, block), (count, 2 * rows // count, width)
    return call(
        aux_forward_kernel,
        "aux_forward",
        (odd, even, dec),
        like(shape),
        (latents // block,),
        [column, column, row_block(block, width)],
        whole_of(shape),
        deps,
        (4 * rows * latents * width, 2 * latents * (width + 2 * rows)),
        scratch=[pltpu.VMEM((rows, width), f32)] * 2,
    )


def aux_back_kernel(odd_ref, even_ref, dec_ref, odd_mask, even_mask, odd_out, even_out):
    dec = dec_ref[...]
    for grads, mask, out in ((odd_ref, odd_mask, odd_out), (even_ref, even_mask, even_out)):
        pulled = dot(grads[...], dec, contract_cols).astype(bf16)
        out[...] = jnp.where(mask[...] >= 2.0, pulled, jnp.zeros((), bf16))


def aux_back(odd, even, dec, odd_mask, even_mask, *deps):
    latents, width = dec.shape
    rows = odd.shape[0]
    block = min(1024, latents)
    column, whole = column_block(rows, block), whole_of((rows, width))
    return call(
        aux_back_kernel,
        "aux_back",
        (odd, even, dec, odd_mask, even_mask),
        (like((rows, latents), bf16),) * 2,
        (latents // block,),
        [whole, whole, row_block(block, width), column, column],
        (column, column),
        deps,
        (4 * rows * latents * width, 2 * latents * (width + 4 * rows)),
    )


def product_kernel(odd_ref, even_ref, factor_ref, odd_out, even_out):
    clear_at_start(odd_out, even_out)
    odd_out[...] += dot(odd_ref[...], factor_ref[...], contract_plain)
    even_out[...] += dot(even_ref[...], factor_ref[...], contract_plain)


def factor_products(odd, even, factor, *deps):
    rows, latents = odd.shape
    block = min(1024, latents)
    column, out = column_block(rows, block), whole_of((rows, lanes))
    return call(
        product_kernel,
        "factor_products",
        (odd, even, factor),
        (like((rows, lanes)),) * 2,
        (latents // block,),
        [column, column, row_block(block, lanes)],
        (out, out),
        deps,
        (4 * rows * latents * lanes, 4 * latents * rows),
    )


def add_left(ref, pieces, values, numbers):
    high, low = high_low(values)
    by_high, by_low = dot(pieces, high, numbers), dot(pieces, low, numbers)
    ref[...] += (by_high[:8] + by_high[8:16] + by_high[16:24]) + (by_low[:8] + by_low[8:16])


def err_left_kernel(pieces_ref, err_ref, out_ref):
    clear_at_start(out_ref)
    add_left(out_ref, pieces_ref[...], err_ref[...], contract_cols)


def err_left(pieces, err, *deps):
    width, latents = err.shape
    block = min(1024, latents)
    return call(
        err_left_kernel,
        "err_left",
        (pieces, err),
        like((8, width)),
        (latents // block,),
        [column_block(32, block), column_block(width, block)],
        whole_of((8, width)),
        deps,
        (128 * latents * width, 4 * latents * width),
    )


def part_dec_kernel(odd_codes, even_codes, odd_grads, even_grads, err_ref, pieces_ref, part_ref, left_ref):
    total = err_ref[...] + dot(odd_codes[...], odd_grads[...], contract_rows)
    total = total + dot(even_codes[...], even_grads[...], contract_rows)
    part_ref[...] = total
    clear_at_start(left_ref)
    add_left(left_ref, pieces_ref[...], total, contract_plain)


def part_dec(codes, grads, err, pieces, *deps):
    latents, width = err.shape
    rows = codes[0].shape[0]
    block = min(1024, latents)
    column, whole, big = column_block(rows, block), whole_of((rows, width)), row_block(block, width)
    return call(
        part_dec_kernel,
        "part_dec",
        (*codes, *grads, err, pieces),
        (like((latents, width)), like((8, width))),
        (latents // block,),
        [column, column, whole, whole, big, column_block(32, block)],
        (big, whole_of((8, width))),
        deps,
        (4 * rows * latents * width, latents * (8 * width + 4 * rows)),
    )


def add_dec_kernel(odd_codes, even_codes, odd_grads, even_grads, base_ref, out_ref):
    total = base_ref[...] + dot(odd_codes[...], odd_grads[...], contract_rows)
    out_ref[...] = total + dot(even_codes[...], even_grads[...], contract_rows)


def add_dec(codes, grads, base, part, parts, *deps):
    latents, width = base.shape
    rows = codes[0].shape[0]
    block = min(1024, latents // parts)
    steps = latents // parts // block
    column = pl.BlockSpec((rows, block), lambda i: (0, i + part * steps))
    big = pl.BlockSpec((block, width), lambda i: (i + part * steps, 0))
    whole = whole_of((rows, width))
    return call(
        add_dec_kernel,
        "add_dec",
        (*codes, *grads, base),
        like((latents, width)),
        (steps,),
        [column, column, whole, whole, big],
        big,
        deps,
        (4 * rows * latents * width // parts, latents * (8 * width + 4 * rows) // parts),
        aliases={4: 0},
    )


def form_enc_kernel(odd_inputs, even_inputs, odd_grads, even_grads, err_ref, out_ref):
    total = err_ref[...] + dot(odd_inputs[...], odd_grads[...], contract_rows)
    out_ref[...] = total + dot(even_inputs[...], even_grads[...], contract_rows)


def form_enc(inputs, grads, err, *deps):
    width, latents = err.shape
    rows = grads[0].shape[0]
    block = min(1024, latents)
    column, whole, big = column_block(rows, block), whole_of((rows, width)), column_block(width, block)
    return call(
        form_enc_kernel,
        "form_enc",
        (*inputs, *grads, err),
        like((width, latents)),
        (latents // block,),
        [whole, whole, column, column, big],
        big,
        deps,
        (4 * rows * latents * width, latents * (8 * width + 4 * rows)),
    )


def back_kernel(odd_ref, even_ref, dec_ref, enc_ref, odd_mask, even_mask, odd_aux, even_aux, factor_ref, *outs):
    odd_out, even_out, bias_ref, pull_ref, odd_sums, even_sums = outs
    dec, factor = dec_ref[...], factor_ref[...]
    clear_at_start(pull_ref, odd_sums, even_sums)
    nothing = jnp.zeros((), bf16)
    bias = None
    for grads, mask, aux, out, sums in (
        (odd_ref, odd_mask, odd_aux, odd_out, odd_sums),
        (even_ref, even_mask, even_aux, even_out, even_sums),
    ):
        pulled = dot(grads[...], dec, contract_cols).astype(bf16)
        mask = mask[...]
        total = jnp.where((mask == 1.0) | (mask == 3.0), pulled, nothing).astype(f32) + aux[...].astype(f32)
        column = jnp.sum(total, axis=0, keepdims=True)
        bias = column if bias is None else bias + column
        rounded = total.astype(bf16)
        out[...] = rounded
        sums[...] += dot(rounded, factor, contract_plain)
    bias_ref[...] = bias
    one, two, three = split_floats(bias)
    pieces = jnp.concatenate([one, two, three, jnp.zeros((13, bias.shape[1]), f32)], axis=0).astype(bf16)
    pull_ref[...] += dot(pieces, enc_ref[...], contract_cols)


def back_pass(odd, even, dec, enc, odd_mask, even_mask, odd_aux, even_aux, factor, *deps):
    latents, width = dec.shape
    rows = odd.shape[0]
    block = min(1024, latents)
    column, whole = column_block(rows, block), whole_of((rows, width))
    return call(
        back_kernel,
        "back_pass",
        (odd, even, dec, enc, odd_mask, even_mask, odd_aux, even_aux, factor),
        (
            like((rows, latents), bf16),
            like((rows, latents), bf16),
            like((1, latents)),
            like((16, width)),
            like((rows, lanes)),
            like((rows, lanes)),
        ),
        (latents // block,),
        [whole, whole, row_block(block, width), column_block(width, block)]
        + [column] * 4
        + [row_block(block, lanes)],
        (
            column,
            column,
            column_block(1, block),
            whole_of((16, width)),
            whole_of((rows, lanes)),
            whole_of((rows, lanes)),
        ),
        deps,
        (4 * rows * latents * (width + lanes), 2 * latents * (2 * width + 6 * rows)),
    )


def left_sums_kernel(
    rank,
    enc_odd,
    enc_even,
    odd_inputs,
    even_inputs,
    dec_odd,
    dec_even,
    odd_grads,
    even_grads,
    enc_base,
    dec_base,
    own_grads,
    pull_ref,
    loss_ref,
    out_ref,
):
    def against(products, inputs):
        total = None
        for piece in split_three(products[...]):
            wide = dot(piece, inputs[...], contract_rows)
            total = wide if total is None else total + wide
        return total[:rank] + total[rank : 2 * rank] + total[2 * rank : 3 * rank]

    out_ref[:rank, :] = enc_base[...] + against(enc_odd, odd_inputs) + against(enc_even, even_inputs)
    out_ref[rank : 2 * rank, :] = dec_base[...] + against(dec_odd, odd_grads) + against(dec_even, even_grads)
    bias = jnp.sum(own_grads[...].astype(f32), axis=0, keepdims=True)
    bias = bias - jnp.sum(pull_ref[...], axis=0, keepdims=True)
    index = lax.broadcasted_iota(jnp.int32, (8, bias.shape[1]), 0)
    out_ref[2 * rank :, :] = jnp.where(index == 0, bias, jnp.where(index == 1, jnp.sum(loss_ref[...], axis=1, keepdims=True), 0.0))


def ortho_kernel(rank, left_ref, enc_ref, dec_ref):
    rows = left_ref[...]
    index = lax.broadcasted_iota(jnp.int32, rows.shape, 0)
    is_enc = index < rank
    place = jnp.where(is_enc, index, index - rank)
    for i in range(rank):
        units = jnp.concatenate([rows[i : i + 1, :], rows[rank + i : rank + i + 1, :]], axis=0)
        units = units * lax.rsqrt(jnp.sum(units * units, axis=1, keepdims=True))
        unit = jnp.where(is_enc, units[:1], units[1:])
        along = jnp.sum(rows * unit, axis=1, keepdims=True)
        rows = jnp.where(place == i, unit, jnp.where(place > i, rows - along * unit, rows))
    for half, out_ref in ((rows[:rank], enc_ref), (rows[rank:], dec_ref)):
        one, two, three = split_floats(half)
        out_ref[...] = jnp.concatenate([one, one, two, two, one, three], axis=0).astype(bf16)


def orthonormal(left, rank):
    shape = jax.ShapeDtypeStruct((6 * rank, left.shape[1]), bf16)
    return pl.pallas_call(
        functools.partial(ortho_kernel, rank), out_shape=(shape, shape), name="orthonormal"
    )(left)


def right_kernel(numbers, rank, left_ref, full_ref, out_ref):
    product = dot(left_ref[...], full_ref[...].astype(bf16), numbers)
    total = product[:rank] + product[2 * rank : 3 * rank] + product[5 * rank :]
    out_ref[...] = total.astype(out_ref.dtype)


def right_part(left, full, by_rows, dtype, *deps):
    latents, width = full.shape if by_rows else full.shape[::-1]
    rank = left.shape[0] // 6
    block = min(1024, latents)
    return call(
        functools.partial(right_kernel, contract_cols if by_rows else contract_plain, rank),
        "right_part",
        (left, full),
        like((rank, latents), dtype),
        (latents // block,),
        [whole_of(left.shape), row_block(block, width) if by_rows else column_block(width, block)],
        column_block(rank, block),
        deps,
        (24 * rank * latents * width, 4 * latents * width),
    )


def stack_kernel(right_ref, bias_ref, out_ref):
    index = lax.broadcasted_iota(jnp.int32, right_ref.shape, 0)
    bias = jnp.where(index == 0, bias_ref[...], 0.0)
    out_ref[...] = jnp.concatenate([right_ref[...], bias], axis=0).astype(bf16)


def pieces_of_right(right):
    one, two, three = split_floats(right)
    return jnp.concatenate([one, two, one, two, three, one], axis=0).astype(bf16)


def enc_final_kernel(rep_count, left_ref, right_ref, full_ref, mom_ref, w_ref, w_out, mom_out, err_out):
    approx = dot(left_ref[...], pieces_of_right(right_ref[:8, :]), contract_rows)
    err_out[...] = full_ref[...] - approx * (1.0 / rep_count)
    mom = momentum_decay * mom_ref[...] + approx
    mom_out[...] = mom
    w_out[...] = w_ref[...] - rate_enc * mom


def dec_final_kernel(rep_count, left_ref, right_ref, full_ref, mom_ref, w_ref, w_out, mom_out, err_out):
    approx = dot(pieces_of_right(right_ref[:8, :]), left_ref[...], contract_rows)
    err_out[...] = full_ref[...] - approx * (1.0 / rep_count)
    mom = momentum_decay * mom_ref[...] + approx
    mom_out[...] = mom
    step = w_ref[...] - rate_dec * mom
    w_out[...] = step * lax.rsqrt(jnp.sum(step * step, axis=1, keepdims=True) + 1e-06)


def final_update(kernel, by_rows, rep_count, left, right, full, mom, weight, *deps):
    latents, width = right.shape[1], left.shape[1]
    block = min(1024, latents)
    big = row_block(block, width) if by_rows else column_block(width, block)
    return call(
        functools.partial(kernel, rep_count),
        "final_update",
        (left, right, full, mom, weight),
        (like(full.shape),) * 3,
        (latents // block,),
        [whole_of(left.shape), column_block(right.shape[0], block), big, big, big],
        (big, big, big),
        deps,
        (2 * 48 * latents * width, 24 * latents * width),
    )


def stack_weights_kernel(qkv_ref, out_ref, fc_ref, proj_ref, stacked_ref):
    share, width = out_ref.shape
    squares = [qkv_ref[:, k * width : (k + 1) * width] for k in range(3)] + [out_ref[...]]
    squares += [fc_ref[:, k * width : (k + 1) * width] for k in range(fc_ref.shape[1] // width)]
    for k, square in enumerate(squares):
        stacked_ref[k * share : (k + 1) * share, :] = square
    stacked_ref[len(squares) * share :, :] = proj_ref[...]


def stack_weights(w_qkv, w_out, w_fc, w_proj):
    share, width = w_out.shape
    rows = share * (4 + w_fc.shape[1] // width) + w_proj.shape[0]
    return call(stack_weights_kernel, "stack_weights", (w_qkv, w_out, w_fc, w_proj), like((rows, width), bf16))


def cut_kernel(four_ref, two_ref, top_ref, bottom_ref):
    rows = top_ref.shape[0]
    top_ref[...] = four_ref[:rows, :]
    bottom_ref[...] = two_ref[rows:, :]


def cut_weights(by_four, by_two, *deps):
    half = like((by_four.shape[0] // 2, by_four.shape[1]), bf16)
    return call(cut_kernel, "cut_weights", (by_four, by_two), (half, half), deps=deps)


def frozen_kernel(share, *refs):
    residual_ref, norm_ref, bias_ref, dec_bias_ref = refs[:4]
    count = refs[-2].shape[0]
    *pieces, stream_out, centered_out, orig_out, weights, sems = refs[4:]
    me = lax.axis_index("lat")
    total_rows, width = weights.shape[1:]
    hidden = (total_rows // share - 8) * share * count
    cuts = [0, 3 * share, total_rows // 2, total_rows]
    copies = [[] for _ in cuts[1:]]
    pieces = iter(pieces)
    for j in range(count):
        parts = [(next(pieces), 0)] * 3 if j & 6 != 6 else [(next(pieces), 0)] * 2 + [(next(pieces), total_rows // 2)]
        for k, (piece, start) in enumerate(parts):
            rows = cuts[k + 1] - cuts[k]
            copies[k].append(
                pltpu.make_async_copy(
                    piece.at[pl.ds(cuts[k] - start, rows), :],
                    weights.at[me ^ j, pl.ds(cuts[k], rows), :],
                    sems.at[k, j],
                )
            )
    for group in copies:
        for copy in group:
            copy.start()

    def square(k):
        return weights[:, k * share : (k + 1) * share, :].reshape(width, width)

    def norm(values, row):
        return layer_norm(values, norm_ref[row : row + 1, :], norm_ref[row + 1 : row + 2, :])

    def bias(k, count=1):
        return bias_ref[:, k * width : (k + count) * width]

    stream = residual_ref[...].astype(f32)
    normed = norm(stream, 0).astype(bf16)
    for copy in copies[0]:
        copy.wait()
    queries, keys, values = [
        (dot(normed, square(k), contract_plain) + bias(k)).astype(bf16) for k in range(3)
    ]
    seq_len = stream.shape[0]
    early = lax.broadcasted_iota(jnp.int32, (seq_len, lanes), 1) < width // HEADS
    causal = lax.broadcasted_iota(jnp.int32, (seq_len, seq_len), 0) >= lax.broadcasted_iota(
        jnp.int32, (seq_len, seq_len), 1
    )
    nothing = jnp.zeros((), bf16)
    attended = []
    for k in range(0, width, lanes):
        pair_q, pair_k, pair_v = (part[:, k : k + lanes] for part in (queries, keys, values))
        outs = []
        for is_early in (True, False):
            head_q = jnp.where(early == is_early, pair_q, nothing)
            scores = dot(head_q, pair_k, contract_cols) / math.sqrt(width // HEADS)
            scores = jnp.where(causal, scores, -1e30)
            grown = jnp.exp(scores - jnp.max(scores, axis=1, keepdims=True))
            share_of = (grown / jnp.sum(grown, axis=1, keepdims=True)).astype(bf16)
            outs.append(dot(share_of, pair_v, contract_plain))
        attended.append(jnp.where(early, outs[0], outs[1]).astype(bf16))
    attended = jnp.concatenate(attended, axis=1)
    for copy in copies[1]:
        copy.wait()
    stream = stream + dot(attended, square(3), contract_plain) + bias(3)
    normed = norm(stream, 2).astype(bf16)
    for copy in copies[2]:
        copy.wait()
    out = None
    for k in range(hidden // width):
        inner = dot(normed, square(4 + k), contract_plain) + bias(4 + k)
        activated = jax.nn.gelu(inner, approximate=True).astype(bf16)
        per = width // (hidden // weights.shape[0])
        block = weights[k * per : (k + 1) * per, 8 * share :, :].reshape(width, width)
        part = dot(activated, block, contract_plain)
        out = part if out is None else out + part
    stream = stream + out + bias(4 + hidden // width)
    stream_out[...] = stream
    centered_out[...] = (stream - dec_bias_ref[...]).astype(bf16)
    orig_out[...] = norm(stream, 4).astype(bf16)


def frozen_whole(residual, norm_params, biases, dec_bias, pieces, share, *deps):
    rows, width = residual.shape
    total, count = pieces[0].shape[0], 8
    return call(
        functools.partial(frozen_kernel, share),
        "frozen_block",
        (residual, norm_params, biases[None, :], dec_bias[None, :], *pieces),
        (like((rows, width)), like((rows, width), bf16), like((rows, width), bf16)),
        (),
        [in_vmem] * 4 + [untouched] * len(pieces),
        (in_vmem,) * 3,
        deps,
        (2 * rows * count * total * width, 2 * count * total * width),
        scratch=[pltpu.VMEM((count, total, width), bf16), pltpu.SemaphoreType.DMA((3, count))],
    )


def layer_norm(values, gain_row, shift_row):
    center = values - jnp.mean(values, axis=-1, keepdims=True)
    spread = jnp.mean(center * center, axis=-1, keepdims=True)
    return center * lax.rsqrt(spread + 1e-05) * gain_row + shift_row


def frozen_block(residual, norm_params, biases, qkv, w_out, fc, w_proj):
    seq_len = residual.shape[0]
    model_width = residual.shape[1]
    hidden_units = w_proj.shape[0]
    head_dim = model_width // HEADS
    stream = residual.astype(f32)
    normed = layer_norm(stream, norm_params[0], norm_params[1]).astype(bf16)

    def times(values, parts, bias):
        width = parts[0].shape[1]
        return [
            jnp.dot(values, part, preferred_element_type=f32) + bias[k * width : (k + 1) * width]
            for k, part in enumerate(parts)
        ]

    queries, keys, values = [
        part.astype(bf16).reshape(seq_len, HEADS, head_dim)
        for part in times(normed, qkv, biases[: 3 * model_width])
    ]
    scores = jnp.einsum("qhd,khd->hqk", queries, keys, preferred_element_type=f32) / math.sqrt(head_dim)
    causal = jnp.arange(seq_len)[:, None] >= jnp.arange(seq_len)[None, :]
    scores = jnp.where(causal, scores, -1e30)
    weights = jax.nn.softmax(scores, axis=-1).astype(bf16)
    attended = jnp.einsum("hqk,khd->qhd", weights, values, preferred_element_type=f32)
    attended = attended.astype(bf16).reshape(seq_len, model_width)
    stream = (
        stream
        + jnp.dot(attended, w_out, preferred_element_type=f32)
        + biases[3 * model_width : 4 * model_width]
    )
    normed = layer_norm(stream, norm_params[2], norm_params[3]).astype(bf16)
    inner_in = times(normed, fc, biases[4 * model_width : 4 * model_width + hidden_units])
    activated = jnp.concatenate(
        [jax.nn.gelu(part, approximate=True).astype(bf16) for part in inner_in], axis=1
    )
    return (
        stream
        + jnp.dot(activated, w_proj, preferred_element_type=f32)
        + biases[4 * model_width + hidden_units :]
    )


def per_device(
    residual,
    valid_mask,
    top_idx,
    aux_idx,
    dead_flags,
    norm_params,
    biases,
    w_qkv,
    w_out,
    w_fc,
    w_proj,
    head_table,
    w_enc,
    encoder_bias_vec,
    w_dec,
    decoder_bias_vec,
    mom_enc,
    mom_benc,
    mom_dec,
    mom_bdec,
    q_enc,
    q_dec,
    err_enc,
    err_dec,
):
    rep_count = lax.axis_size("rep")
    made_with.clear()
    lat_index = lax.axis_index("lat")
    model_width = residual.shape[1]
    hidden_units = w_fc.shape[1]
    lat_dev = w_enc.shape[1]
    top_count, aux_count = top_idx.shape[1], aux_idx.shape[1]
    rank = q_enc.shape[1]
    err_enc, err_dec = err_enc[0], err_dec[0]

    half = aux_count // 2
    valid_float = valid_mask.astype(f32)
    packed = pack_picks(aux_idx, top_idx.T, valid_mask[None, :])
    dead_pair = jnp.concatenate(
        [
            lax.dynamic_slice_in_dim(dead_flags, base * lat_dev, lat_dev)
            for base in (lat_index, lat_index ^ 1)
        ]
    ).astype(f32)[None, :]
    share = w_qkv.shape[0]
    by_piece = lax.axis_size("lat") == 8 and share % 16 == 0
    if by_piece:
        stacked = stack_weights(w_qkv, w_out, w_fc, w_proj)
        picks = Gather(packed)
        two_rows, four_rows = swap(stacked, "lat", 2), swap(stacked, "lat", 4)
        rows = packed.shape[0]
        masks, valid_0 = build_mask(packed, dead_pair, aux_count, top_count, 4 * rows, 3 * rows, deps=(stacked,))
        by_two, by_six, by_four, _ = picks.blocks
        masks, valid_1 = build_mask(
            by_two, dead_pair, aux_count, top_count, 4 * rows, 0, masks, deps=(by_six, by_four)
        )
        masks, valid_2 = build_mask(by_four, dead_pair, aux_count, top_count, 4 * rows, 2 * rows, masks)
        masks, valid_3 = build_mask(by_six, dead_pair, aux_count, top_count, 4 * rows, rows, masks)
        valid_total = valid_0 + valid_1 + valid_2 + valid_3
        top, bottom = cut_weights(four_rows, two_rows, masks[0])
        top, bottom = swap(top, "lat", 2), swap(bottom, "lat", 4)
        enc_weight = rounded(w_enc, False, masks[0])
        dec_weight = rounded(w_dec, True, enc_weight)
        q_enc_rows, q_enc_columns = factor_pieces(q_enc.T, dec_weight)
        q_dec_rows, q_dec_columns = factor_pieces(q_dec.T, q_enc_rows)
        top, bottom = pass_after(top, q_enc_rows), pass_after(bottom, q_enc_rows)
        pieces = []
        for piece in ((stacked,), (two_rows,), (four_rows,), (top, bottom)):
            pieces += [*piece, *(swap(part, "lat", 1) for part in piece)]
    else:
        joined = lax.all_gather(jnp.concatenate([w_qkv, w_out, w_fc], axis=1), "lat", axis=0, tiled=True)
        proj_all = lax.all_gather(w_proj, "lat", axis=0, tiled=True)
        squares = [joined[:, k : k + model_width] for k in range(0, joined.shape[1], model_width)]
        packed = gather_even(packed)
        masks, valid_total = build_mask(packed, dead_pair, aux_count, top_count, packed.shape[0], 0)
        enc_weight, dec_weight = rounded(w_enc, False), rounded(w_dec, True)
        q_enc_rows, q_enc_columns = factor_pieces(q_enc.T)
        q_dec_rows, q_dec_columns = factor_pieces(q_dec.T)
    mask_even, mask_partner = masks
    valid_total = sum_round(valid_total, "lat", [1])
    def final_norm(values):
        return layer_norm(values, norm_params[4], norm_params[5])

    if by_piece:
        stream, centered_own, orig_blocks = frozen_whole(
            residual,
            norm_params,
            biases,
            decoder_bias_vec,
            pieces,
            share,
            q_dec_rows,
            valid_total,
        )
        mask_partner = pass_after(mask_partner, centered_own)
    else:
        stream = frozen_block(residual, norm_params, biases, squares[:3], squares[3], squares[4:], proj_all)
        centered_own = (stream - decoder_bias_vec).astype(bf16)
        orig_blocks = final_norm(stream).astype(bf16)
    gather = Gather(centered_own)
    mask_odd = swap(mask_partner, "lat", 1)
    valid_total = sum_round(pass_after(valid_total, centered_own), "rep", bits_of("rep"))
    weight_own = (valid_float / valid_total[0, 0])[:, None]
    left_enc = err_left(q_enc_rows, err_enc, centered_own, valid_total)
    centered = gather.end(left_enc)

    bias_row = encoder_bias_vec[None, :]
    tops_odd, auxes_odd, top_odd = forward(
        centered[1], enc_weight, bias_row, mask_odd, dec_weight, q_dec_rows
    )
    rebuilt = Scatter(top_odd)
    tops_even, auxes_even, top_even = forward(centered[0], enc_weight, bias_row, mask_even, dec_weight, top_odd)
    sent = rebuilt.chip(top_even)
    aux_part = aux_forward(auxes_odd, auxes_even, dec_weight, sent)
    auxiliary_rebuilt = lax.psum_scatter(aux_part, "lat", scatter_dimension=0, tiled=False)
    orig_group = gather_behind(orig_blocks, aux_part)
    rebuilt_input = rebuilt.last(orig_group[0]) + decoder_bias_vec
    rec_float, norm_back = jax.vjp(final_norm, rebuilt_input)
    gather = Gather(rec_float.astype(bf16))
    orig_odd = head_part(orig_group[1], head_table, gather.own)
    rec_group = gather.end(orig_odd)
    orig_mean = Scatter(pass_after(orig_odd, rec_group[0]), lanes)
    orig_even = head_part(orig_group[0], head_table, rec_group[0])
    sent = orig_mean.chip(orig_even)
    rec_odd = head_part(rec_group[1], head_table, sent)
    orig_mean = orig_mean.last(rec_odd)
    rec_odd = pass_after(rec_odd, orig_mean)
    rec_mean = Scatter(rec_odd, lanes)
    aux_pull, aux_blocks, err_square = residual_pull(
        stream, rebuilt_input, auxiliary_rebuilt, weight_own, orig_mean
    )
    rec_even = head_part(rec_group[0], head_table, aux_blocks)
    sent = rec_mean.chip(rec_even)

    products_dec = factor_products(tops_odd, tops_even, q_dec_columns, sent)
    aux_group = gather_behind(aux_blocks, products_dec[0])
    pre_odd, pre_even = aux_back(aux_group[1], aux_group[0], dec_weight, mask_odd, mask_even)
    rec_mean = rec_mean.last(pre_odd)

    orig_lse, rec_lse = orig_mean[:, model_width], rec_mean[:, model_width]
    orig_mean, rec_mean = orig_mean[:, :model_width], rec_mean[:, :model_width]
    (grad_head,) = norm_back(weight_own * (rec_mean - orig_mean))
    grad_recon = (grad_head + aux_pull).astype(bf16)
    gather = Gather(grad_recon)
    dec_part, left_dec = part_dec(
        (auxes_odd, auxes_even), (aux_group[1], aux_group[0]), err_dec, q_dec_rows, grad_recon
    )
    recon_group = gather.end(dec_part)
    gap = orig_blocks.astype(f32) - rec_float.astype(bf16).astype(f32)
    kl_own = jnp.sum(gap * orig_mean, axis=1) - orig_lse + rec_lse
    loss_tokens = (valid_float * (kl_own + aux_weight * err_square[:, 0]))[None, :]

    pre_odd, pre_even, grad_benc, bias_pull, enc_odd, enc_even = back_pass(
        recon_group[1],
        recon_group[0],
        dec_weight,
        enc_weight,
        mask_odd,
        mask_even,
        pre_odd,
        pre_even,
        q_enc_columns,
    )
    small = call(
        functools.partial(left_sums_kernel, rank),
        "left_sums",
        (
            enc_odd,
            enc_even,
            centered[1],
            centered[0],
            *products_dec,
            recon_group[1],
            recon_group[0],
            left_enc,
            left_dec,
            grad_recon,
            bias_pull,
            loss_tokens,
        ),
        like((2 * rank + 8, model_width)),
    )
    codes, grads = (tops_odd, tops_even), (recon_group[1], recon_group[0])
    full_dec = add_dec(codes, grads, dec_part, 0, 2, small)
    small = sum_round(small, "lat", [1])
    full_dec = add_dec(codes, grads, full_dec, 1, 2, small)
    small = sum_round(small, "lat", bits_of("lat")[1:])
    full_enc = form_enc((centered[1], centered[0]), (pre_odd, pre_even), err_enc, small, full_dec)
    small = sum_round(small, "rep", bits_of("rep"))
    grad_bdec, loss_sum = small[2 * rank], small[2 * rank + 1, 0]

    ortho_enc, ortho_dec = orthonormal(small[: 2 * rank], rank)
    right_enc = right_part(ortho_enc, full_enc, False, bf16)
    right_dec = right_part(ortho_dec, full_dec, True, f32, right_enc)
    right_enc = sum_round(right_enc, "rep", bits_of("rep"), sent_as=bf16)
    right_dec = call(
        stack_kernel, "stack", (right_dec, grad_benc), like((2 * rank, lat_dev), bf16), deps=(right_enc,)
    )
    right_dec = sum_round(right_dec, "rep", bits_of("rep"), sent_as=bf16)
    grad_benc = right_dec[rank]

    w_enc_new, mom_enc_new, err_enc_new = final_update(
        enc_final_kernel, False, rep_count, ortho_enc, right_enc, full_enc, mom_enc, w_enc
    )
    w_dec_new, mom_dec_new, err_dec_new = final_update(
        dec_final_kernel, True, rep_count, ortho_dec, right_dec, full_dec, mom_dec, w_dec, w_enc_new
    )
    mom_benc_new = momentum_decay * mom_benc + grad_benc
    mom_bdec_new = momentum_decay * mom_bdec + grad_bdec
    b_enc_new = encoder_bias_vec - rate_benc * mom_benc_new
    b_dec_new = decoder_bias_vec - rate_bdec * mom_bdec_new
    return (
        loss_sum,
        valid_total[0, 0],
        w_enc_new,
        b_enc_new,
        w_dec_new,
        b_dec_new,
        mom_enc_new,
        mom_benc_new,
        mom_dec_new,
        mom_bdec_new,
        right_enc.T,
        right_dec[:rank].T,
        err_enc_new[None],
        err_dec_new[None],
    )


def solution(mesh):
    in_specs = (
        P(("rep", "lat"), None),
        P(("rep", "lat")),
        P(("rep", "lat"), None),
        P(("rep", "lat"), None),
        P(),
        P(),
        P(),
        P("lat", None),
        P("lat", None),
        P("lat", None),
        P("lat", None),
        P("lat", None),
        P(None, "lat"),
        P("lat"),
        P("lat", None),
        P(),
        P(None, "lat"),
        P("lat"),
        P("lat", None),
        P(),
        P("lat", None),
        P("lat", None),
        P("rep", None, "lat"),
        P("rep", "lat", None),
    )
    out_specs = (
        P(),
        P(),
        P(None, "lat"),
        P("lat"),
        P("lat", None),
        P(),
        P(None, "lat"),
        P("lat"),
        P("lat", None),
        P(),
        P("lat", None),
        P("lat", None),
        P("rep", None, "lat"),
        P("rep", "lat", None),
    )
    return jax.shard_map(
        per_device, mesh=mesh, in_specs=in_specs, out_specs=out_specs, check_vma=False
    )
```
